32 devices in a mesh: member: 2 (over y), curve: 4 (over z), sub: 4 (over x, core).
Axes of the slice: x: 2, y: 2, z: 4, core: 2. Of those that a mesh axis runs over, the one named last changes fastest.
Arguments:
- old_cells: float32 [768, 4, 128, 128], P(('member', 'curve', 'sub')), parts along dimension 0, as said below
- old_range: int32 [32, 2], P(('member', 'curve', 'sub')), parts along dimension 0, may hold values from 0 to 256, as said below
- neighbours: int32 [512, 4], P(('member', 'curve', 'sub')), parts along dimension 0, may hold values from -1 to 255, as said below
Outputs:
- new_state: float32 [512, 3, 128, 128], P(('member', 'curve', 'sub')), parts along dimension 0
The draws below stay inside these ranges and needn't reach their ends.
There are 2 independent parts, one for each index of `member`. The reference program is written for one: setup_inputs(seed, part) draws one part's arguments, and reference() takes and returns one part's arrays. A program takes and returns all parts, laid end to end along the dimension named above; each array names one. Nothing has to cross between parts.
Inputs may be any that keep to these rules, and one draw needn't show every extreme that they name: `old_range`: consecutive rows adjoin; row 0 starts at 0 and the last row ends at 256; each row's start lies within 4 of its device index times 16, and some start lies exactly 4 above and some exactly 4 below it. `neighbours`: A patch's owner after the regrid is its curve index // 16. Every listed neighbour is owned by the same device or by a device at most 2 positions away along the curve. Among the 64 entries of the rows of one device's patches, no other device is named more than 8 times, and on every device some other device is named exactly 8 times. `old_cells`: depth lies in 0.5 to 1.5, momenta within -0.6 to 0.6, bed within -0.5 to 0.5.
All inputs are finite; a program needn't handle non-finite values.
Results may differ from the reference program's by a relative error of at most 0.00002.
Values sent between devices are 32-bit elements; how exact they have to be, the bound alone decides.
No kernel may reach another device: no remote copies, remote signals or barrier semaphores. Data moves between devices by JAX's collectives and lax.ppermute only.
A program may use at most 128 MiB of HBM per device.

```python
import jax
import jax.numpy as jnp
from jax import lax

S = 128
PD = 16
MCAP = 4
OLD_CAP = 24
N_CURVE = 4
N_SUB = 4


def draw_old_cells(key, part):
    key = jax.random.fold_in(key, 37)
    shape = (N_CURVE * N_SUB * OLD_CAP, S, S)
    keys = jax.random.split(key, 4)
    height = 1.0 + 0.2 * jnp.clip(jax.random.normal(keys[0], shape, jnp.float32), -2.5, 2.5)
    flow_x = 0.2 * jnp.clip(jax.random.normal(keys[1], shape, jnp.float32), -3.0, 3.0)
    flow_y = 0.2 * jnp.clip(jax.random.normal(keys[2], shape, jnp.float32), -3.0, 3.0)
    bed = 0.2 * jnp.clip(jax.random.normal(keys[3], shape, jnp.float32), -2.5, 2.5)
    return jnp.stack([height, flow_x, flow_y, bed], axis=1)


def draw_old_range(key, part):
    key = jax.random.fold_in(key, 11)
    devices = N_CURVE * N_SUB
    first_key, second_key, third_key = jax.random.split(key, 3)
    spread = (MCAP + 3) // 4
    magnitude = MCAP - jax.random.randint(first_key, (devices - 1,), 0, spread)
    direction = jnp.where(jax.random.randint(third_key, (devices - 1,), 0, 2) == 0, -1, 1)
    inner = (direction * magnitude).astype(jnp.int32)
    chosen = jax.random.permutation(second_key, devices - 1)
    inner = jnp.where(chosen == 0, MCAP, jnp.where(chosen == 1, -MCAP, inner))
    shifts = jnp.concatenate([jnp.zeros((1,), jnp.int32), inner.astype(jnp.int32), jnp.zeros((1,), jnp.int32)])
    base = jnp.arange(devices, dtype=jnp.int32) * PD
    starts = base + shifts[:-1]
    finish = base + PD + shifts[1:]
    return jnp.stack([starts, finish], axis=1).astype(jnp.int32)


def draw_neighbours(key, part):
    key = jax.random.fold_in(key, 23)
    devices = N_CURVE * N_SUB
    gcap = PD // 2
    keys = jax.random.split(key, 4)
    device_ids = jnp.arange(devices, dtype=jnp.int32)
    lowest = max(gcap // 2, 1)
    counts = jax.random.randint(keys[0], (devices, 4), lowest, gcap + 1)
    forced = jnp.where(device_ids < devices - 1, 2, 1)
    counts = jnp.where(jnp.arange(4, dtype=jnp.int32)[None, :] == forced[:, None], gcap, counts)
    request = jnp.arange(4 * PD, dtype=jnp.int32)
    peer = jnp.minimum(request // gcap, 3)
    within = request % gcap
    remote_slot = (request[None, :] < 4 * gcap) & (within[None, :] < counts[:, peer])
    offsets = jnp.array([-2, -1, 1, 2], jnp.int32)
    owner = device_ids[:, None] + offsets[peer][None, :]
    valid = (owner >= 0) & (owner < devices)
    local = jax.random.randint(keys[1], (devices, 4 * PD), 0, PD)
    remote_value = jnp.where(valid, owner * PD + local, -1)
    wall = jax.random.randint(keys[2], (devices, 4 * PD), 0, 8) == 0
    own_value = jnp.where(wall, -1, device_ids[:, None] * PD + local)
    listed = jnp.where(remote_slot, remote_value, own_value)
    orders = jax.vmap(lambda each: jax.random.permutation(each, 4 * PD))(jax.random.split(keys[3], devices))
    listed = jnp.take_along_axis(listed, orders, axis=1)
    return listed.reshape(devices * PD, 4).astype(jnp.int32)


def setup_inputs(seed: int = 0, part: int = 0) -> dict:
    key_of = jax.random.split(jax.random.key(seed), 4)
    part_splits = jax.random.split(jax.random.fold_in(key_of[3], part), 4)
    old_cells = draw_old_cells(jax.random.fold_in(jax.random.fold_in(key_of[3], part), 71), part)
    old_range = draw_old_range(jax.random.fold_in(jax.random.fold_in(key_of[3], part), 71), part)
    neighbours = draw_neighbours(jax.random.fold_in(jax.random.fold_in(key_of[3], part), 71), part)
    return {"old_cells": old_cells, "old_range": old_range, "neighbours": neighbours}


RATE_STEP = 0.1

def side_edges(cells):
    return jnp.stack([cells[:, :, :, 0], cells[:, :, :, -1], cells[:, :, 0, :], cells[:, :, -1, :]], axis=1)

def wall_edges(cells):
    signs = jnp.array([[1.0, -1.0, 1.0, 1.0], [1.0, -1.0, 1.0, 1.0], [1.0, 1.0, -1.0, 1.0], [1.0, 1.0, -1.0, 1.0]], jnp.float32)
    return side_edges(cells) * signs[None, :, :, None]

def rusanov_flux(left, right, normal):
    across = 3 - normal
    height_l = left[:, 0]
    height_r = right[:, 0]
    speed_l = left[:, normal] / height_l
    speed_r = right[:, normal] / height_r
    flux_l = [left[:, normal], left[:, normal] * speed_l + 0.5 * height_l * height_l, left[:, across] * speed_l]
    flux_r = [right[:, normal], right[:, normal] * speed_r + 0.5 * height_r * height_r, right[:, across] * speed_r]
    wave_rate = jnp.maximum(jnp.abs(speed_l) + jnp.sqrt(height_l), jnp.abs(speed_r) + jnp.sqrt(height_r))
    jumps = [right[:, 0] + right[:, 3] - left[:, 0] - left[:, 3], right[:, normal] - left[:, normal], right[:, across] - left[:, across]]
    parts = []
    for which in range(3):
        parts.append(0.5 * (flux_l[which] + flux_r[which]) - 0.5 * wave_rate * jumps[which])
    if normal == 1:
        return jnp.stack([parts[0], parts[1], parts[2]], axis=1)
    return jnp.stack([parts[0], parts[2], parts[1]], axis=1)

def advance(cells, ghosts):
    west = ghosts[:, 0][:, :, :, None]
    east = ghosts[:, 1][:, :, :, None]
    south = ghosts[:, 2][:, :, None, :]
    north = ghosts[:, 3][:, :, None, :]
    along_x = jnp.concatenate([west, cells, east], axis=3)
    along_y = jnp.concatenate([south, cells, north], axis=2)
    flux_x = rusanov_flux(along_x[:, :, :, :-1], along_x[:, :, :, 1:], 1)
    flux_y = rusanov_flux(along_y[:, :, :-1, :], along_y[:, :, 1:, :], 2)
    height = cells[:, 0]
    slope_x = 0.5 * (along_x[:, 3, :, 2:] - along_x[:, 3, :, :-2])
    slope_y = 0.5 * (along_y[:, 3, 2:, :] - along_y[:, 3, :-2, :])
    source = jnp.stack([jnp.zeros_like(height), -height * slope_x, -height * slope_y], axis=1)
    change = flux_x[:, :, :, 1:] - flux_x[:, :, :, :-1] + (flux_y[:, :, 1:, :] - flux_y[:, :, :-1, :])
    return cells[:, :3] - RATE_STEP * change + RATE_STEP * source

def reference(old_cells, old_range, neighbours):
    devices = N_CURVE * N_SUB
    patches = devices * PD
    curve_index = jnp.arange(patches, dtype=jnp.int32)
    owner = lax.optimization_barrier(jnp.sum((old_range[:, 0][None, :] <= curve_index[:, None]).astype(jnp.int32), axis=1)) - 1
    old_slot = (owner * OLD_CAP + curve_index - owner * PD + MCAP).astype(jnp.int32)
    cells = old_cells[old_slot]
    all_edges = side_edges(cells).reshape(patches * 4, 4, S)
    walls = wall_edges(cells)
    opposite = jnp.array([1, 0, 3, 2], jnp.int32)
    target = jnp.maximum(neighbours, 0) * 4 + opposite[None, :]
    fetched = all_edges[target.reshape(-1)].reshape(patches, 4, 4, S)
    ghosts = jnp.where((neighbours >= 0)[:, :, None, None], fetched, walls)
    blocks = (cells.reshape(devices, PD, 4, S, S), ghosts.reshape(devices, PD, 4, 4, S))
    result = lax.map(lambda pair: advance(pair[0], pair[1]), blocks)
    return result.reshape(patches, 3, S, S)
```

```python
import functools

import jax
import jax.numpy as jnp
from jax import lax
from jax.experimental import pallas as pl
from jax.experimental.pallas import tpu as pltpu
from jax.sharding import PartitionSpec as P

RATE_STEP = 0.1
HALF = 0.5 * RATE_STEP
AXES = ("curve", "sub")
OFFSETS = (-2, -1, 1, 2)
CAP = 8


def terms(h, mx, my, bed):
    root = lax.rsqrt(h)
    celerity = h * root
    inverse = root * root
    u = mx * inverse
    v = my * inverse
    half_sq = 0.5 * h * h
    cross = my * u
    return dict(
        fx=mx * u + half_sq,
        cross=cross,
        fy=my * v + half_sq,
        rate_x=jnp.abs(u) + celerity,
        rate_y=jnp.abs(v) + celerity,
        eta=h + bed,
    )


def inner_update(h, mx, my, bed):
    t = terms(h, mx, my, bed)
    side = h.shape[0]

    def along(axis, normal, across, flux_n, flux_t, rate):
        place = lax.broadcasted_iota(jnp.int32, h.shape, axis)
        ahead = lambda a: pltpu.roll(a, side - 1, axis)
        behind = lambda a: pltpu.roll(a, 1, axis)
        last = place == side - 1
        top = jnp.maximum(rate, ahead(rate))
        normal_a = ahead(normal)
        q_h = (normal + normal_a) - top * (ahead(t["eta"]) - t["eta"])
        q_n = (flux_n + ahead(flux_n)) - top * (normal_a - normal)
        q_t = (flux_t + ahead(flux_t)) - top * (ahead(across) - across)
        out = []
        for q in (q_h, q_n, q_t):
            q = jnp.where(last, 0.0, q)
            out.append(q - behind(q))
        slope = jnp.where(last, 0.0, ahead(bed)) - jnp.where(place == 0, 0.0, behind(bed))
        return out[0], out[1] + h * slope, out[2]

    xh, xn, xt = along(1, mx, my, t["fx"], t["cross"], t["rate_x"])
    yh, yn, yt = along(0, my, mx, t["fy"], t["cross"], t["rate_y"])
    return h - HALF * (xh + yh), mx - HALF * (xn + yt), my - HALF * (xt + yn)


def patches_kernel(count, cells_ref, out_ref, edge_ref, columns):
    step = pl.program_id(0)
    fields = [cells_ref[0, f] for f in range(4)]
    new = inner_update(*fields)
    for f in range(3):
        out_ref[0, f] = new[f]
    side = fields[0].shape[0]
    lane = lax.broadcasted_iota(jnp.int32, (side, side), 1)
    gathered = columns[...]
    for f in range(4):
        at = 8 * step + 2 * f
        moved = pltpu.roll(fields[f], at + 1, 1)
        gathered = jnp.where((lane == at) | (lane == at + 1), moved, gathered)
        row = 16 * step + 8 + 2 * f
        edge_ref[pl.ds(row, 1), :] = cells_ref[0, f, side - 1 : side, :]
        edge_ref[pl.ds(row + 1, 1), :] = cells_ref[0, f, 0:1, :]
    columns[...] = gathered

    @pl.when(step == count - 1)
    def _():
        turned = jnp.transpose(columns[...])
        for p in range(count):
            edge_ref[16 * p : 16 * p + 8, :] = turned[8 * p : 8 * p + 8, :]


def inner_patches(cells, first, count):
    side = cells.shape[3]
    return pl.pallas_call(
        functools.partial(patches_kernel, count),
        grid=(count,),
        in_specs=[pl.BlockSpec((1, 4, side, side), lambda i: (first + i, 0, 0, 0))],
        out_specs=[
            pl.BlockSpec((1, 3, side, side), lambda i: (i, 0, 0, 0)),
            pl.BlockSpec((16 * count, side), lambda i: (0, 0)),
        ],
        out_shape=[
            jax.ShapeDtypeStruct((count, 3, side, side), jnp.float32),
            jax.ShapeDtypeStruct((16 * count, side), jnp.float32),
        ],
        scratch_shapes=[pltpu.VMEM((side, side), jnp.float32)],
        cost_estimate=pl.CostEstimate(
            flops=count * side * side * 100,
            bytes_accessed=count * side * side * 28,
            transcendentals=count * side * side,
        ),
    )(cells)


def answer_kernel(margin, take_ref, rows_ref, own_ref, left_ref, right_ref, edge_ref, *messages):
    count = own_ref.shape[0] // 16
    edge_ref[...] = own_ref[...]
    for m in range(margin):
        for source, p in ((left_ref, m), (right_ref, count - margin + m)):

            @pl.when(take_ref[p] != 0)
            def _(source=source, p=p, m=m):
                edge_ref[16 * p : 16 * p + 16, :] = source[16 * m : 16 * m + 16, :]

    for k in range(4):
        for j in range(CAP):
            row = rows_ref[k * CAP + j]
            messages[k][pl.ds(8 * (j // 2) + j % 2, 4, stride=2), :] = edge_ref[pl.ds(row, 4, stride=2), :]


def answers(take, rows, own, left, right, margin):
    side = own.shape[1]
    whole = pl.BlockSpec(memory_space=pltpu.VMEM)
    scalars = pl.BlockSpec(memory_space=pltpu.SMEM)
    return pl.pallas_call(
        functools.partial(answer_kernel, margin),
        in_specs=[scalars, scalars, whole, whole, whole],
        out_specs=[whole] * 5,
        out_shape=[jax.ShapeDtypeStruct(own.shape, jnp.float32)]
        + [jax.ShapeDtypeStruct((4 * CAP, side), jnp.float32)] * 4,
    )(take, rows, own, left, right)


def rim_kernel(rows_ref, wall_ref, edge_ref, m0, m1, m2, m3, columns_ref, lines_ref, source, ghost, turn):
    total = edge_ref.shape[0]
    count = total // 16
    source[0:total, :] = edge_ref[...]
    for k, message in enumerate((m0, m1, m2, m3)):
        source[total + 4 * CAP * k : total + 4 * CAP * (k + 1), :] = message[...]
    for p in range(count):
        for s in range(4):
            row = rows_ref[4 * p + s]
            target = 16 * p + 8 * (s // 2) + 1 - s % 2
            ghost[pl.ds(target, 4, stride=2), :] = source[pl.ds(row, 4, stride=2), :]
    turn[...] = jnp.zeros_like(turn)
    for s in range(4):
        parity = 1 - s % 2
        sign = 1.0 - 2.0 * parity
        axis = s // 2
        normal, across = (1, 2) if axis == 0 else (2, 1)

        def pick(ref, f):
            return ref[pl.ds(8 * axis + 2 * f + parity, count, stride=16), :]

        flip = wall_ref[count * s : count * (s + 1), :]
        hc, hg = pick(edge_ref, 0), pick(ghost, 0)
        nc, ng = pick(edge_ref, normal), pick(ghost, normal) * flip
        ac, ag = pick(edge_ref, across), pick(ghost, across)
        bc, bg = pick(edge_ref, 3), pick(ghost, 3)
        rc, rg = lax.rsqrt(hc), lax.rsqrt(hg)
        uc, ug = nc * rc * rc, ng * rg * rg
        top = jnp.maximum(jnp.abs(uc) + hc * rc, jnp.abs(ug) + hg * rg)
        fc, fg = nc * uc + 0.5 * hc * hc, ng * ug + 0.5 * hg * hg
        c_h = -HALF * (sign * (nc + ng) - top * ((hg + bg) - (hc + bc)))
        c_n = -HALF * (sign * (fc + fg + hc * bg) - top * (ng - nc))
        c_t = -HALF * (sign * (ac * uc + ag * ug) - top * (ag - ac))
        for f, value in ((0, c_h), (normal, c_n), (across, c_t)):
            where = pl.ds(2 * f + parity, count, stride=8)
            if axis == 0:
                turn[where, :] = value
            else:
                lines_ref[where, :] = value
    columns_ref[...] = jnp.transpose(turn[...])


def rims(rows, walls, edges, messages):
    total, side = edges.shape
    whole = pl.BlockSpec(memory_space=pltpu.VMEM)
    scalars = pl.BlockSpec(memory_space=pltpu.SMEM)
    return pl.pallas_call(
        rim_kernel,
        in_specs=[scalars] + [whole] * 6,
        out_specs=[whole] * 2,
        out_shape=[jax.ShapeDtypeStruct((side, side), jnp.float32)] * 2,
        scratch_shapes=[
            pltpu.VMEM((total + 16 * CAP, side), jnp.float32),
            pltpu.VMEM((total, side), jnp.float32),
            pltpu.VMEM((side, side), jnp.float32),
        ],
    )(rows, walls, edges, *messages)


def add_rim(p, value, f, columns_ref, lines_ref, lane):
    side = value.shape[0]
    moved = pltpu.roll(columns_ref[...], 2 * side - (8 * p + 2 * f + 1), 1)
    return value + jnp.where((lane == 0) | (lane == side - 1), moved, 0.0)


def finish_patch(p, values, columns_ref, lines_ref, out_ref):
    side = columns_ref.shape[0]
    lane = lax.broadcasted_iota(jnp.int32, (side, side), 1)
    for f in range(3):
        out_ref[0, f] = add_rim(p, values(f), f, columns_ref, lines_ref, lane)
        out_ref[0, f, side - 1 : side, :] += lines_ref[pl.ds(8 * p + 2 * f, 1), :]
        out_ref[0, f, 0:1, :] += lines_ref[pl.ds(8 * p + 2 * f + 1, 1), :]


def middle_kernel(margin, own_ref, columns_ref, lines_ref, out_ref):
    p = pl.program_id(0) + margin
    finish_patch(p, lambda f: own_ref[0, f], columns_ref, lines_ref, out_ref)


def middle(own, columns, lines, margin):
    count, _, side, _ = own.shape
    block = pl.BlockSpec((1, 3, side, side), lambda i: (i + margin, 0, 0, 0))
    whole = pl.BlockSpec(memory_space=pltpu.VMEM)
    return pl.pallas_call(
        functools.partial(middle_kernel, margin),
        grid=(count - 2 * margin,),
        in_specs=[block, whole, whole],
        out_specs=block,
        out_shape=jax.ShapeDtypeStruct(own.shape, jnp.float32),
    )(own, columns, lines)


def ends_kernel(margin, count, take_ref, own_ref, left_ref, right_ref, columns_ref, lines_ref, _, out_ref):
    i = pl.program_id(0)
    p = jnp.where(i < margin, i, count - 2 * margin + i)
    taken = take_ref[p] != 0

    def values(f):
        moved = jnp.where(i < margin, left_ref[0, f], right_ref[0, f])
        return jnp.where(taken, moved, own_ref[0, f])

    finish_patch(p, values, columns_ref, lines_ref, out_ref)


def ends(take, own, left, right, columns, lines, filled, margin):
    count, _, side, _ = own.shape
    at = lambda i: jnp.where(i < margin, i, count - 2 * margin + i)
    block = pl.BlockSpec((1, 3, side, side), lambda i: (at(i), 0, 0, 0))
    whole = pl.BlockSpec(memory_space=pltpu.VMEM)
    return pl.pallas_call(
        functools.partial(ends_kernel, margin, count),
        grid=(2 * margin,),
        in_specs=[
            pl.BlockSpec(memory_space=pltpu.SMEM),
            block,
            pl.BlockSpec((1, 3, side, side), lambda i: (jnp.minimum(i, margin - 1), 0, 0, 0)),
            pl.BlockSpec((1, 3, side, side), lambda i: (jnp.maximum(i - margin, 0), 0, 0, 0)),
            whole,
            whole,
            pl.BlockSpec(memory_space=pl.ANY),
        ],
        out_specs=block,
        out_shape=jax.ShapeDtypeStruct(own.shape, jnp.float32),
        input_output_aliases={6: 0},
    )(take, own, left, right, columns, lines, filled)


def shifted(value, steps):
    count = lax.axis_size(AXES)
    first, last = max(0, -steps), min(count, count - steps)
    return lax.ppermute(value, AXES, [(i, i + steps) for i in range(first, last)])


def ranks(named):
    size = named.shape[-1]
    earlier = jnp.arange(size)[:, None] < jnp.arange(size)[None, :]
    return jnp.sum(jnp.where(named[..., :, None] & earlier, 1, 0), axis=-2)


def local(old_cells, old_range, neighbours):
    per_device = neighbours.shape[0]
    slots = old_cells.shape[0]
    side = old_cells.shape[3]
    margin = (slots - per_device) // 2
    devices = lax.axis_size(AXES)
    me = lax.axis_index(AXES)

    tables = lax.all_gather(neighbours, AXES, tiled=True)

    down, down_edges = inner_patches(old_cells, 0, margin)
    from_right = shifted(down, -1)
    up, up_edges = inner_patches(old_cells, slots - margin, margin)
    from_left = shifted(up, 1)
    edges_right = shifted(down_edges, -1)
    edges_left = shifted(up_edges, 1)
    own, own_edges = inner_patches(old_cells, margin, per_device)

    curve_index = me * per_device + jnp.arange(per_device, dtype=jnp.int32)
    take = ((curve_index < old_range[0, 0]) | (curve_index >= old_range[0, 1])).astype(jnp.int32)

    entry = jnp.arange(4 * per_device, dtype=jnp.int32)
    entry_side = entry % 4
    offsets = jnp.array(OFFSETS, jnp.int32)
    asking = me - offsets
    present = (asking >= 0) & (asking < devices)
    listed_by = tables.reshape(devices, 4 * per_device)[jnp.clip(asking, 0, devices - 1)]
    asked = present[:, None] & (listed_by >= 0) & (listed_by // per_device == me)
    order = ranks(asked)
    edge_row = 16 * (listed_by % per_device) + 8 * (entry_side // 2) + entry_side % 2
    chosen = asked[:, None, :] & (order[:, None, :] == jnp.arange(CAP)[None, :, None])
    send_rows = jnp.sum(jnp.where(chosen, edge_row[:, None, :], 0), axis=2).reshape(-1)

    edges, *outgoing = answers(take, send_rows, own_edges, edges_left, edges_right, margin)
    messages = [shifted(outgoing[k], -OFFSETS[k]) for k in range(4)]

    listed = neighbours.reshape(-1)
    alive = listed >= 0
    distance = jnp.where(alive, listed // per_device - me, 0)
    named = distance[None, :] == offsets[:, None]
    place = ranks(named)
    total = 16 * per_device
    base = total + 4 * CAP * jnp.arange(4, dtype=jnp.int32)[:, None]
    remote = jnp.sum(jnp.where(named, base + 8 * (place // 2) + place % 2, 0), axis=0)
    home = 16 * (listed % per_device) + 8 * (entry_side // 2) + entry_side % 2
    wall = 16 * (entry // 4) + 8 * (entry_side // 2) + 1 - entry_side % 2
    ghost_rows = jnp.where(alive, jnp.where(distance == 0, home, remote), wall)
    flips = jnp.where(neighbours >= 0, 1.0, -1.0).astype(jnp.float32).T.reshape(-1, 1)
    walls = jnp.broadcast_to(flips, (4 * per_device, side))

    columns, lines = rims(ghost_rows, walls, edges, messages)
    filled = middle(own, columns, lines, margin)
    return ends(take, own, from_left, from_right, columns, lines, filled, margin)


def solution(mesh):
    placed = (
        P(("member", "curve", "sub"), None, None, None),
        P(("member", "curve", "sub"), None),
        P(("member", "curve", "sub"), None),
    )
    return jax.shard_map(
        local,
        mesh=mesh,
        in_specs=placed,
        out_specs=P(("member", "curve", "sub"), None, None, None),
        check_vma=False,
    )
```

```python
import functools

import jax
import jax.numpy as jnp
from jax import lax
from jax.experimental import pallas as pl
from jax.experimental.pallas import tpu as pltpu
from jax.sharding import PartitionSpec as P

RATE_STEP = 0.1
HALF = 0.5 * RATE_STEP
AXES = ("curve", "sub")
CAP = 8
ROWS = 8
VMEM = pl.BlockSpec(memory_space=pltpu.VMEM)
SMEM = pl.BlockSpec(memory_space=pltpu.SMEM)
HBM = pl.BlockSpec(memory_space=pltpu.HBM)


def position():
    me = lax.axis_index(AXES)
    return me, lax.rem(me, 2)


def iota(axis, side):
    return lax.broadcasted_iota(jnp.int32, (ROWS, side), axis)


def inner_update(load, store, columns, at, side):
    lane, line = iota(1, side), iota(0, side)
    pair = lane // 2
    west, east = lane == 0, lane == side - 1
    first, last = line == 0, line == ROWS - 1
    strips = side // ROWS
    ahead = lambda a: pltpu.roll(a, side - 1, 1)
    behind = lambda a: pltpu.roll(a, 1, 1)
    below = None
    pending = None

    def finish(k, held, ups):
        h, part_h, part_x, part_y, lows, bed_low, up_own = held
        north = [jnp.where(last, u, o) for u, o in zip(ups, up_own)]
        part_y = part_y + h * (north[3] - bed_low)
        store(0, k, h - HALF * (part_h + (north[0] - lows[0])))
        mx, my = load(1, k), load(2, k)
        store(1, k, mx - HALF * (part_x + (north[1] - lows[1])))
        store(2, k, my - HALF * (part_y + (north[2] - lows[2])))

    for k in range(strips):
        h, mx, my, bed = (load(f, k) for f in range(4))
        held = columns[ROWS * k : ROWS * (k + 1), :]
        for f, value in enumerate((h, mx, my, bed)):
            held = jnp.where(pair == at // 2 + f, pltpu.roll(value, at + 2 * f + 1, 1), held)
        columns[ROWS * k : ROWS * (k + 1), :] = held
        root = lax.rsqrt(h)
        celerity = h * root
        inverse = root * root
        u = mx * inverse
        v = my * inverse
        half_sq = 0.5 * h * h
        cross = my * u
        fx = mx * u + half_sq
        fy = my * v + half_sq
        rate_x = jnp.abs(u) + celerity
        rate_y = jnp.abs(v) + celerity
        eta = h + bed
        top = jnp.maximum(rate_x, ahead(rate_x))
        mx_e, my_e, bed_e = ahead(mx), ahead(my), ahead(bed)
        q = [
            (mx + mx_e) - top * (ahead(eta) - eta),
            (fx + ahead(fx)) - top * (mx_e - mx),
            (cross + ahead(cross)) - top * (my_e - my),
        ]
        q = [jnp.where(east, 0.0, each) for each in q]
        slope = jnp.where(east, 0.0, bed_e) - jnp.where(west, 0.0, behind(bed))
        part_h = q[0] - behind(q[0])
        part_x = q[1] - behind(q[1]) + h * slope
        part_y = q[2] - behind(q[2])
        values = (rate_y, eta, mx, my, cross, fy, bed)
        turned = [pltpu.roll(each, 1, 0) for each in values]
        if below is None:
            south = turned[:6] + [jnp.where(first, 0.0, turned[6])]
        else:
            south = [jnp.where(first, b, t) for b, t in zip(below, turned)]
        below = turned
        top = jnp.maximum(rate_y, south[0])
        q = [
            (my + south[3]) - top * (eta - south[1]),
            (cross + south[4]) - top * (mx - south[2]),
            (fy + south[5]) - top * (my - south[3]),
        ]
        if k == 0:
            q = [jnp.where(first, 0.0, each) for each in q]
        ups = [pltpu.roll(each, ROWS - 1, 0) for each in q + [bed]]
        if pending is not None:
            finish(k - 1, pending, ups)
        pending = (h, part_h, part_x, part_y, q, south[6], ups)
    finish(strips - 1, pending, [0.0] * 4)


def take_edges(count, cells, slot_of, columns, edges, base):
    side = columns.shape[0]
    turned = jnp.transpose(columns[...])
    for p in range(count):
        edges[base + 16 * p : base + 16 * p + 8, :] = turned[8 * p : 8 * p + 8, :]
        for f in range(4):
            row = base + 16 * p + 8 + 2 * f
            edges[row : row + 1, :] = cells[slot_of(p), f, side - 1 : side, :]
            edges[row + 1 : row + 2, :] = cells[slot_of(p), f, 0:1, :]


def update_one(cells, i, columns, lane_at, side, put):
    inner_update(
        lambda f, k: cells[i, f, ROWS * k : ROWS * (k + 1), :],
        lambda f, k, value: put(f, ROWS * k, value),
        columns,
        lane_at,
        side,
    )


def fetch(cells_hbm, first, cells, sems, count):
    def copy(i):
        return pltpu.make_async_copy(cells_hbm.at[first + i], cells.at[i], sems.at[i])

    for i in range(count):
        copy(i).start()
    return copy


def outer_kernel(margin, cells_hbm, out, edges, cells, columns, sems):
    side = columns.shape[0]
    _, odd = position()
    copy = fetch(cells_hbm, odd * (cells_hbm.shape[0] - margin), cells, sems, margin)

    @pl.loop(0, margin)
    def _(i):
        copy(i).wait()

        def put(f, row, value):
            out[i, f, row : row + ROWS, :] = value

        update_one(cells, i, columns, 8 * i, side, put)

    take_edges(margin, cells, lambda p: p, columns, edges, 0)


def cost(patches, side):
    return pl.CostEstimate(
        flops=patches * side * side * 800,
        bytes_accessed=patches * side * side * 28,
        transcendentals=patches * side * side,
    )


def outer_patches(old_cells, margin):
    side = old_cells.shape[3]
    return pl.pallas_call(
        functools.partial(outer_kernel, margin),
        in_specs=[HBM],
        out_specs=[VMEM, VMEM],
        out_shape=[
            jax.ShapeDtypeStruct((margin, 3, side, side), jnp.float32),
            jax.ShapeDtypeStruct((16 * margin, side), jnp.float32),
        ],
        scratch_shapes=[
            pltpu.VMEM((margin, 4, side, side), jnp.float32),
            pltpu.VMEM((side, side), jnp.float32),
            pltpu.SemaphoreType.DMA((margin,)),
        ],
        cost_estimate=cost(margin, side),
        name="outer",
    )(old_cells)


def layout(margin, per_device, side):
    inner = 3 * side * margin
    home = inner + 16 * margin
    limit = home + 16 * per_device
    brought = limit + 8
    return inner, home, limit, brought, brought + 16 * margin + 8


def home_kernel(margin, range_ref, cells_hbm, shared, own, cells, columns, sems):
    side = columns.shape[0]
    count = own.shape[0]
    inner, home, limit, _, _ = layout(margin, count, side)
    _, odd = position()
    copy = fetch(cells_hbm, (1 - odd) * margin, cells, sems, margin + count)
    inner_at = (1 - odd) * count
    home_at = odd * margin

    @pl.loop(0, margin)
    def _(i):
        copy(inner_at + i).wait()

        def put(f, row, value):
            at = pl.multiple_of(i * (3 * side) + (f * side + row), ROWS)
            shared[pl.ds(at, ROWS), :] = value

        update_one(cells, inner_at + i, columns, 8 * i, side, put)

    take_edges(margin, cells, lambda p: inner_at + p, columns, shared, inner)

    @pl.loop(0, count)
    def _(i):
        copy(home_at + i).wait()

        def put(f, row, value):
            own[i, f, row : row + ROWS, :] = value

        update_one(cells, home_at + i, columns, 8 * i, side, put)

    take_edges(count, cells, lambda p: home_at + p, columns, shared, home)
    outer_limit = jnp.where(odd == 1, range_ref[0, 1], range_ref[0, 0])
    shared[limit : limit + 8, :] = jnp.full((8, side), outer_limit, jnp.int32).astype(jnp.float32)


def home_patches(old_range, old_cells, margin, per_device):
    side = old_cells.shape[3]
    total = layout(margin, per_device, side)[-1]
    return pl.pallas_call(
        functools.partial(home_kernel, margin),
        in_specs=[SMEM, HBM],
        out_specs=[VMEM, VMEM],
        out_shape=[
            jax.ShapeDtypeStruct((total, side), jnp.float32),
            jax.ShapeDtypeStruct((per_device, 3, side, side), jnp.float32),
        ],
        scratch_shapes=[
            pltpu.VMEM((margin + per_device, 4, side, side), jnp.float32),
            pltpu.VMEM((side, side), jnp.float32),
            pltpu.SemaphoreType.DMA((margin + per_device,)),
        ],
        cost_estimate=cost(margin + per_device, side),
        compiler_params=pltpu.CompilerParams(vmem_limit_bytes=24 << 20),
        name="home",
    )(old_range, old_cells)


def answer_kernel(margin, count, range_ref, rows_ref, mine, theirs, edges, message):
    side = edges.shape[1]
    inner, home, limit, brought, _ = layout(margin, count, side)
    me, odd = position()
    start, stop = range_ref[0, 0], range_ref[0, 1]
    even = odd == 0
    at_me = pl.multiple_of(16 * count * odd, 16)
    at_them = pl.multiple_of(16 * count * (1 - odd), 16)
    edges[pl.ds(at_me, 16 * count), :] = mine[home : home + 16 * count, :]
    edges[pl.ds(at_them, 16 * count), :] = theirs[home : home + 16 * count, :]
    their_limit = theirs[limit : limit + 8, :]
    low, high = 0, count - margin
    for m in range(margin):
        l = jnp.where(even, high, low) + m
        g = me * count + l
        taken = jnp.where(even, g >= stop, g < start)
        to = pl.multiple_of(at_me + 16 * l, 16)
        from_pair = theirs[inner + 16 * m : inner + 16 * (m + 1), :]
        edges[pl.ds(to, 16), :] = jnp.where(taken, from_pair, edges[pl.ds(to, 16), :])
        l = jnp.where(even, low, high) + m
        g = (me + 1 - 2 * odd) * count + l
        taken = jnp.where(even, g < stop, g >= start)
        to = pl.multiple_of(at_them + 16 * l, 16)
        from_pair = mine[inner + 16 * m : inner + 16 * (m + 1), :]
        edges[pl.ds(to, 16), :] = jnp.where(taken, from_pair, edges[pl.ds(to, 16), :])
        l = jnp.where(even, low, high) + m
        g = me * count + l
        taken = jnp.where(even, g < start, g >= stop)
        to = pl.multiple_of(at_me + 16 * l, 16)
        crossed = mine[brought + 16 * m : brought + 16 * (m + 1), :]
        edges[pl.ds(to, 16), :] = jnp.where(taken, crossed, edges[pl.ds(to, 16), :])
        l = jnp.where(even, high, low) + m
        g = ((me + 1 - 2 * odd) * count + l).astype(jnp.float32)
        to = pl.multiple_of(at_them + 16 * l, 16)
        taken = jnp.where(even, g - their_limit, their_limit - g - 1.0) >= 0.0
        for half in range(2):
            crossed = theirs[brought + 16 * m + 8 * half : brought + 16 * m + 8 * half + 8, :]
            at = pl.multiple_of(to + 8 * half, 8)
            edges[pl.ds(at, 8), :] = jnp.where(taken, crossed, edges[pl.ds(at, 8), :])
    for n in range(3 * CAP):
        message[pl.ds(8 * (n // 2) + n % 2, 4, stride=2), :] = edges[pl.ds(rows_ref[n], 4, stride=2), :]


def answers(old_range, rows, mine, theirs, margin, per_device):
    side = mine.shape[1]
    return pl.pallas_call(
        functools.partial(answer_kernel, margin, per_device),
        in_specs=[SMEM, SMEM, VMEM, VMEM],
        out_specs=[VMEM, VMEM],
        out_shape=[
            jax.ShapeDtypeStruct((32 * per_device, side), jnp.float32),
            jax.ShapeDtypeStruct((12 * CAP, side), jnp.float32),
        ],
        name="answers",
    )(old_range, rows, mine, theirs)


def add_rim(p, load, store, columns, lines):
    side = columns.shape[0]
    lane, line = iota(1, side), iota(0, side)
    rim = (lane == 0) | (lane == side - 1)
    south = [lines[pl.ds(8 * p + 2 * f + 1, 1), :] for f in range(3)]
    north = [lines[pl.ds(8 * p + 2 * f, 1), :] for f in range(3)]
    strips = side // ROWS
    for k in range(strips):
        held = columns[ROWS * k : ROWS * (k + 1), :]
        for f in range(3):
            value = load(f, k) + jnp.where(rim, pltpu.roll(held, side - 1 - 8 * p - 2 * f, 1), 0.0)
            if k == 0:
                value = value + jnp.where(line == 0, south[f], 0.0)
            if k == strips - 1:
                value = value + jnp.where(line == ROWS - 1, north[f], 0.0)
            store(f, k, value)


def rim_terms(rows_ref, edges, crossed, passed, columns, lines, source, ghost, turn, count, odd):
    total = edges.shape[0]
    step = crossed.shape[0]
    source[0:total, :] = edges[...]
    source[total : total + step, :] = crossed[...]
    source[total + step : total + 2 * step, :] = passed[...]
    field = lax.broadcasted_iota(jnp.int32, (4, edges.shape[1]), 0)
    for p in range(count):
        for s in range(4):
            row = rows_ref[4 * p + s]
            wall = row < 0
            value = source[pl.ds(jnp.where(wall, -1 - row, row), 4, stride=2), :]
            value = jnp.where((field == 1 + s // 2) & wall, -value, value)
            ghost[pl.ds(16 * p + 8 * (s // 2) + 1 - s % 2, 4, stride=2), :] = value
    turn[...] = jnp.zeros_like(turn)
    lines[...] = jnp.zeros_like(lines)
    for s in range(4):
        parity = 1 - s % 2
        sign = 1.0 - 2.0 * parity
        axis = s // 2
        normal, across = (1, 2) if axis == 0 else (2, 1)

        def both(f):
            row = 8 * axis + 2 * f + parity
            own = source[pl.ds(16 * count * odd + row, count, stride=16), :]
            return own, ghost[pl.ds(row, count, stride=16), :]

        hc, hg = both(0)
        nc, ng = both(normal)
        ac, ag = both(across)
        bc, bg = both(3)
        rc, rg = lax.rsqrt(hc), lax.rsqrt(hg)
        uc, ug = nc * rc * rc, ng * rg * rg
        top = jnp.maximum(jnp.abs(uc) + hc * rc, jnp.abs(ug) + hg * rg)
        fc, fg = nc * uc + 0.5 * hc * hc, ng * ug + 0.5 * hg * hg
        c_h = -HALF * (sign * (nc + ng) - top * ((hg + bg) - (hc + bc)))
        c_n = -HALF * (sign * (fc + fg + hc * bg) - top * (ng - nc))
        c_t = -HALF * (sign * (ac * uc + ag * ug) - top * (ag - ac))
        for f, value in ((0, c_h), (normal, c_n), (across, c_t)):
            target = turn if axis == 0 else lines
            target[pl.ds(2 * f + parity, count, stride=8), :] = value
    columns[...] = jnp.transpose(turn[...])


def most_kernel(
    margin, range_ref, rows_ref, edges, crossed, passed, own, theirs, out, columns, lines, result, source, ghost, turn, sems
):
    count, side = own.shape[0], columns.shape[0]
    me, odd = position()
    even = odd == 0
    rim_terms(rows_ref, edges, crossed, passed, columns, lines, source, ghost, turn, count, odd)
    start, stop = range_ref[0, 0], range_ref[0, 1]
    first = (1 - odd) * margin
    many = count - margin

    def copy(i):
        return pltpu.make_async_copy(result.at[i], out.at[first + i], sems.at[i])

    @pl.loop(0, many)
    def _(i):
        p = first + i
        g = me * count + p
        taken = jnp.where(even, g >= stop, g < start)
        m = jnp.clip(jnp.where(even, p - (count - margin), p), 0, margin - 1)

        def load(f, k):
            at = pl.multiple_of(m * (3 * side) + (f * side + ROWS * k), ROWS)
            return jnp.where(taken, theirs[pl.ds(at, ROWS), :], own[p, f, ROWS * k : ROWS * (k + 1), :])

        def store(f, k, value):
            result[i, f, ROWS * k : ROWS * (k + 1), :] = value

        add_rim(p, load, store, columns, lines)
        copy(i).start()

    for i in range(many):
        copy(i).wait()


def most(old_range, rows, edges, crossed, passed, own, theirs, margin):
    count, _, side, _ = own.shape
    many = count - margin
    return pl.pallas_call(
        functools.partial(most_kernel, margin),
        in_specs=[SMEM, SMEM] + [VMEM] * 5,
        out_specs=[HBM, VMEM, VMEM],
        out_shape=[
            jax.ShapeDtypeStruct(own.shape, jnp.float32),
            jax.ShapeDtypeStruct((side, side), jnp.float32),
            jax.ShapeDtypeStruct((side, side), jnp.float32),
        ],
        scratch_shapes=[
            pltpu.VMEM((many, 3, side, side), jnp.float32),
            pltpu.VMEM((edges.shape[0] + 2 * crossed.shape[0], side), jnp.float32),
            pltpu.VMEM((16 * count, side), jnp.float32),
            pltpu.VMEM((side, side), jnp.float32),
            pltpu.SemaphoreType.DMA((many,)),
        ],
        compiler_params=pltpu.CompilerParams(vmem_limit_bytes=24 << 20),
        name="most",
    )(old_range, rows, edges, crossed, passed, own, theirs)


def rest_kernel(margin, range_ref, own, arrived, columns, lines, _, out, result, sems):
    count, side = own.shape[0], columns.shape[0]
    me, odd = position()
    even = odd == 0
    start, stop = range_ref[0, 0], range_ref[0, 1]
    first = odd * (count - margin)

    def copy(i):
        return pltpu.make_async_copy(result.at[i], out.at[first + i], sems.at[i])

    @pl.loop(0, margin)
    def _(i):
        p = first + i
        g = me * count + p
        taken = jnp.where(even, g < start, g >= stop)

        def load(f, k):
            at = slice(ROWS * k, ROWS * (k + 1))
            return jnp.where(taken, arrived[i, f, at, :], own[p, f, at, :])

        def store(f, k, value):
            result[i, f, ROWS * k : ROWS * (k + 1), :] = value

        add_rim(p, load, store, columns, lines)
        copy(i).start()

    for i in range(margin):
        copy(i).wait()


def rest(old_range, own, arrived, columns, lines, filled, margin):
    count, _, side, _ = own.shape
    return pl.pallas_call(
        functools.partial(rest_kernel, margin),
        in_specs=[SMEM] + [VMEM] * 4 + [HBM],
        out_specs=HBM,
        out_shape=jax.ShapeDtypeStruct(own.shape, jnp.float32),
        scratch_shapes=[
            pltpu.VMEM((margin, 3, side, side), jnp.float32),
            pltpu.SemaphoreType.DMA((margin,)),
        ],
        input_output_aliases={5: 0},
        name="rest",
    )(old_range, own, arrived, columns, lines, filled)


def swapped(value, first):
    pairs = [(i, i + 1) for i in range(first, lax.axis_size(AXES) - 1, 2)]
    return lax.ppermute(value, AXES, pairs + [(j, i) for i, j in pairs])


def ranks(named):
    size = named.shape[-1]
    earlier = jnp.arange(size)[:, None] < jnp.arange(size)[None, :]
    return jnp.sum(jnp.where(named[..., :, None] & earlier, 1, 0), axis=-2)


def local(old_cells, old_range, neighbours):
    per_device = neighbours.shape[0]
    side = old_cells.shape[3]
    margin = (old_cells.shape[0] - per_device) // 2
    entries = 4 * per_device
    me, odd = position()
    brought = layout(margin, per_device, side)[3]

    their_table = swapped(neighbours, 0)
    leaving, leaving_edges = outer_patches(old_cells, margin)
    arrived = swapped(leaving, 1)

    tables = jnp.where(
        odd == 0,
        jnp.concatenate([neighbours.reshape(1, -1), their_table.reshape(1, -1)], axis=1),
        jnp.concatenate([their_table.reshape(1, -1), neighbours.reshape(1, -1)], axis=1),
    ).astype(jnp.float32)
    tables = jnp.pad(tables, ((0, 7), (0, side - 2 * entries)))
    came = swapped(jnp.concatenate([leaving_edges, tables], axis=0), 1)

    shared, own = home_patches(old_range, old_cells, margin, per_device)
    shared = lax.dynamic_update_slice(shared, came, (brought, 0))
    theirs = swapped(shared, 0)

    entry = jnp.arange(entries, dtype=jnp.int32)
    entry_side = entry % 4
    at_side = 8 * (entry_side // 2) + entry_side % 2
    asked_by = came[16 * margin, : 2 * entries].astype(jnp.int32).reshape(2, entries)
    middle = jnp.where(odd == 0, asked_by[1], asked_by[0])
    listed = jnp.stack([asked_by[0], middle, asked_by[1]])
    owners = me + jnp.where(odd == 0, jnp.array([0, 0, 1], jnp.int32), jnp.array([-1, 0, 0], jnp.int32))
    asked = (listed >= 0) & (listed // per_device == owners[:, None])
    rows = 16 * (listed - 2 * per_device * (me // 2)) + at_side
    chosen = asked[:, None, :] & (ranks(asked)[:, None, :] == jnp.arange(CAP)[None, :, None])
    send_rows = jnp.sum(jnp.where(chosen, rows[:, None, :], 0), axis=2).reshape(-1)

    edges, message = answers(old_range, send_rows, shared, theirs, margin, per_device)
    crossed = swapped(message, 1)
    passed = swapped(crossed, 0)

    listed = neighbours.reshape(-1)
    owner = listed // per_device
    mine, total, step = 32 * per_device, 16 * per_device, 12 * CAP
    lists = jnp.where(
        odd == 0,
        jnp.array([[-2, mine], [-1, mine + 4 * CAP], [2, mine + step]], jnp.int32),
        jnp.array([[-2, mine + step + 8 * CAP], [1, mine + 4 * CAP], [2, mine + 8 * CAP]], jnp.int32),
    )
    named = (listed >= 0) & (owner - me == lists[:, :1])
    place = ranks(named)
    across = jnp.sum(jnp.where(named, lists[:, 1:] + 8 * (place // 2) + place % 2, 0), axis=0)
    within = 16 * (listed - 2 * per_device * (me // 2)) + at_side
    wall = total * odd + 16 * (entry // 4) + 8 * (entry_side // 2) + 1 - entry_side % 2
    ghost_rows = jnp.where(listed < 0, -1 - wall, jnp.where(owner // 2 == me // 2, within, across))

    filled, columns, lines = most(old_range, ghost_rows, edges, crossed, passed, own, theirs, margin)
    return rest(old_range, own, arrived, columns, lines, filled, margin)


def solution(mesh):
    placed = (
        P(("member", "curve", "sub"), None, None, None),
        P(("member", "curve", "sub"), None),
        P(("member", "curve", "sub"), None),
    )
    return jax.shard_map(
        local,
        mesh=mesh,
        in_specs=placed,
        out_specs=P(("member", "curve", "sub"), None, None, None),
        check_vma=False,
    )
```

```python
import functools

import jax
import jax.numpy as jnp
from jax import lax
from jax.experimental import pallas as pl
from jax.experimental.pallas import tpu as pltpu
from jax.sharding import PartitionSpec as P

RATE_STEP = 0.1
HALF = 0.5 * RATE_STEP
AXES = ("curve", "sub")
CAP = 8
ROWS = 8
VMEM = pl.BlockSpec(memory_space=pltpu.VMEM)
SMEM = pl.BlockSpec(memory_space=pltpu.SMEM)
HBM = pl.BlockSpec(memory_space=pltpu.HBM)


def position():
    me = lax.axis_index(AXES)
    return me, lax.rem(me, 2)


def iota(axis, side):
    return lax.broadcasted_iota(jnp.int32, (ROWS, side), axis)


def spread(j, side):
    return pl.ds(j, ROWS, stride=side // ROWS)


def inner_update(load, store, columns, at, side):
    lane, line = iota(1, side), iota(0, side)
    pair = lane // 2
    west, east = lane == 0, lane == side - 1
    first, last = line == 0, line == ROWS - 1
    steps = side // ROWS
    ahead = lambda a: pltpu.roll(a, side - 1, 1)
    behind = lambda a: pltpu.roll(a, 1, 1)
    marks = [pair == at // 2 + f for f in range(4)]

    def cell(h, mx, my, bed):
        root = lax.rsqrt(h)
        celerity = h * root
        inverse = root * root
        u = mx * inverse
        v = my * inverse
        half_sq = 0.5 * h * h
        cross = my * u
        rate_y = jnp.abs(v) + celerity
        rate_x = jnp.abs(u) + celerity
        return (rate_y, h + bed, mx, my, cross, my * v + half_sq, bed), rate_x, mx * u + half_sq

    def face_y(low, high):
        top = jnp.maximum(low[0], high[0])
        return [
            (high[3] + low[3]) - top * (high[1] - low[1]),
            (high[4] + low[4]) - top * (high[2] - low[2]),
            (high[5] + low[5]) - top * (high[3] - low[3]),
        ]

    def fields(j):
        return [load(f, j) for f in range(4)]

    def finish(held, north, bed_north):
        h, mx, my, part_h, part_x, part_y, south, bed_south = held
        return (
            h - HALF * (part_h + (north[0] - south[0])),
            mx - HALF * (part_x + (north[1] - south[1])),
            my - HALF * (part_y + (north[2] - south[2]) + h * (bed_north - bed_south)),
        )

    top_fields = fields(steps - 1)
    loaded = [fields(0), fields(1)]
    low = [pltpu.roll(each, 1, 0) for each in cell(*top_fields)[0]]
    pending, ready = None, []

    moved_of = {}
    for j in range(steps):
        if j + 2 < steps:
            loaded.append(top_fields if j + 2 == steps - 1 else fields(j + 2))
        h, mx, my, bed = loaded[j]
        while ready and ready[0][0] <= j - 3:
            at_j, values = ready.pop(0)
            for f in range(3):
                store(f, at_j, values[f])
            columns.store(at_j, moved_of.pop(at_j))
        held = columns.load(j)
        for f, value in enumerate((h, mx, my, bed)):
            held = jnp.where(marks[f], pltpu.roll(value, at + 2 * f + 1, 1), held)
        moved_of[j] = held
        high, rate_x, fx = cell(h, mx, my, bed)
        cross, eta = high[4], high[1]
        top = jnp.maximum(rate_x, ahead(rate_x))
        mx_e, my_e, bed_e = ahead(mx), ahead(my), ahead(bed)
        q = [
            (mx + mx_e) - top * (ahead(eta) - eta),
            (fx + ahead(fx)) - top * (mx_e - mx),
            (cross + ahead(cross)) - top * (my_e - my),
        ]
        q = [jnp.where(east, 0.0, each) for each in q]
        slope = jnp.where(east, 0.0, bed_e) - jnp.where(west, 0.0, behind(bed))
        part_h = q[0] - behind(q[0])
        part_x = q[1] - behind(q[1]) + h * slope
        part_y = q[2] - behind(q[2])
        south = face_y(low, high)
        bed_south = low[6]
        if j == 0:
            south = [jnp.where(first, 0.0, each) for each in south]
            bed_south = jnp.where(first, 0.0, bed_south)
            seam = [jnp.where(last, 0.0, pltpu.roll(each, ROWS - 1, 0)) for each in south + [bed]]
        if pending is not None:
            ready.append((j - 1, finish(pending, south, bed)))
        pending = (h, mx, my, part_h, part_x, part_y, south, bed_south)
        low = high
    ready.append((steps - 1, finish(pending, seam[:3], seam[3])))
    for at_j, values in ready:
        for f in range(3):
            store(f, at_j, values[f])
        columns.store(at_j, moved_of.pop(at_j))


class Columns:
    def __init__(self, ref):
        self.ref, self.side = ref, ref.shape[0]

    def load(self, j):
        return self.ref[spread(j, self.side), :]

    def store(self, j, value):
        self.ref[spread(j, self.side), :] = value


def take_edges(count, cells, slot_of, columns, edges, base):
    side = columns.shape[0]
    turned = jnp.transpose(columns[...])
    for p in range(count):
        edges[base + 16 * p : base + 16 * p + 8, :] = turned[8 * p : 8 * p + 8, :]
        for f in range(4):
            row = base + 16 * p + 8 + 2 * f
            edges[row : row + 1, :] = cells[slot_of(p), f, side - 1 : side, :]
            edges[row + 1 : row + 2, :] = cells[slot_of(p), f, 0:1, :]


def update_one(cells, i, columns, lane_at, side, put):
    inner_update(
        lambda f, j: cells[i, f, spread(j, side), :],
        lambda f, j, value: put(f, ROWS * j, value),
        Columns(columns),
        lane_at,
        side,
    )


def fetch(cells_hbm, first, cells, sems, count):
    def copy(i):
        return pltpu.make_async_copy(cells_hbm.at[first + i], cells.at[i], sems.at[i])

    for i in range(count):
        copy(i).start()
    return copy


def outer_kernel(margin, cells_hbm, out, edges, cells, columns, sems):
    side = columns.shape[0]
    _, odd = position()
    copy = fetch(cells_hbm, odd * (cells_hbm.shape[0] - margin), cells, sems, margin)

    @pl.loop(0, margin)
    def _(i):
        copy(i).wait()

        def put(f, row, value):
            out[i, f, row : row + ROWS, :] = value

        update_one(cells, i, columns, 8 * i, side, put)

    take_edges(margin, cells, lambda p: p, columns, edges, 0)


def cost(patches, side):
    return pl.CostEstimate(
        flops=patches * side * side * 800,
        bytes_accessed=patches * side * side * 28,
        transcendentals=patches * side * side,
    )


def room(mebibytes):
    return pltpu.CompilerParams(vmem_limit_bytes=mebibytes << 20)


def outer_patches(old_cells, margin):
    side = old_cells.shape[3]
    return pl.pallas_call(
        functools.partial(outer_kernel, margin),
        in_specs=[HBM],
        out_specs=[VMEM, VMEM],
        out_shape=[
            jax.ShapeDtypeStruct((margin, 3, side, side), jnp.float32),
            jax.ShapeDtypeStruct((16 * margin, side), jnp.float32),
        ],
        scratch_shapes=[
            pltpu.VMEM((margin, 4, side, side), jnp.float32),
            pltpu.VMEM((side, side), jnp.float32),
            pltpu.SemaphoreType.DMA((margin,)),
        ],
        cost_estimate=cost(margin, side),
        compiler_params=room(48),
        name="outer",
    )(old_cells)


def layout(margin, per_device, side):
    inner = 3 * side * margin
    home = inner + 16 * margin
    limit = home + 16 * per_device
    brought = limit + 8
    return inner, home, limit, brought, brought + 16 * margin + 8


def home_kernel(margin, range_ref, cells_hbm, shared, own, cells, columns, sems):
    side = columns.shape[0]
    count = own.shape[0]
    inner, home, limit, _, _ = layout(margin, count, side)
    _, odd = position()
    copy = fetch(cells_hbm, (1 - odd) * margin, cells, sems, margin + count)
    inner_at = (1 - odd) * count
    home_at = odd * margin

    @pl.loop(0, margin)
    def _(i):
        copy(inner_at + i).wait()

        def put(f, row, value):
            at = pl.multiple_of(i * (3 * side) + (f * side + row), ROWS)
            shared[pl.ds(at, ROWS), :] = value

        update_one(cells, inner_at + i, columns, 8 * i, side, put)

    take_edges(margin, cells, lambda p: inner_at + p, columns, shared, inner)

    @pl.loop(0, count)
    def _(i):
        copy(home_at + i).wait()

        def put(f, row, value):
            own[i, f, row : row + ROWS, :] = value

        update_one(cells, home_at + i, columns, 8 * i, side, put)

    take_edges(count, cells, lambda p: home_at + p, columns, shared, home)
    outer_limit = jnp.where(odd == 1, range_ref[0, 1], range_ref[0, 0])
    shared[limit : limit + 8, :] = jnp.full((8, side), outer_limit, jnp.int32).astype(jnp.float32)


def home_patches(old_range, old_cells, margin, per_device):
    side = old_cells.shape[3]
    total = layout(margin, per_device, side)[-1]
    return pl.pallas_call(
        functools.partial(home_kernel, margin),
        in_specs=[SMEM, HBM],
        out_specs=[VMEM, VMEM],
        out_shape=[
            jax.ShapeDtypeStruct((total, side), jnp.float32),
            jax.ShapeDtypeStruct((per_device, 3, side, side), jnp.float32),
        ],
        scratch_shapes=[
            pltpu.VMEM((margin + per_device, 4, side, side), jnp.float32),
            pltpu.VMEM((side, side), jnp.float32),
            pltpu.SemaphoreType.DMA((margin + per_device,)),
        ],
        cost_estimate=cost(margin + per_device, side),
        compiler_params=room(48),
        name="home",
    )(old_range, old_cells)


def answer_kernel(margin, count, range_ref, rows_ref, mine, theirs, edges, message):
    side = edges.shape[1]
    inner, home, limit, brought, _ = layout(margin, count, side)
    me, odd = position()
    start, stop = range_ref[0, 0], range_ref[0, 1]
    even = odd == 0
    at_me = pl.multiple_of(16 * count * odd, 16)
    at_them = pl.multiple_of(16 * count * (1 - odd), 16)
    edges[pl.ds(at_me, 16 * count), :] = mine[home : home + 16 * count, :]
    edges[pl.ds(at_them, 16 * count), :] = theirs[home : home + 16 * count, :]
    their_limit = theirs[limit : limit + 8, :]
    low, high = 0, count - margin
    for m in range(margin):
        l = jnp.where(even, high, low) + m
        g = me * count + l
        taken = jnp.where(even, g >= stop, g < start)
        to = pl.multiple_of(at_me + 16 * l, 16)
        from_pair = theirs[inner + 16 * m : inner + 16 * (m + 1), :]
        edges[pl.ds(to, 16), :] = jnp.where(taken, from_pair, edges[pl.ds(to, 16), :])
        l = jnp.where(even, low, high) + m
        g = (me + 1 - 2 * odd) * count + l
        taken = jnp.where(even, g < stop, g >= start)
        to = pl.multiple_of(at_them + 16 * l, 16)
        from_pair = mine[inner + 16 * m : inner + 16 * (m + 1), :]
        edges[pl.ds(to, 16), :] = jnp.where(taken, from_pair, edges[pl.ds(to, 16), :])
        l = jnp.where(even, low, high) + m
        g = me * count + l
        taken = jnp.where(even, g < start, g >= stop)
        to = pl.multiple_of(at_me + 16 * l, 16)
        crossed = mine[brought + 16 * m : brought + 16 * (m + 1), :]
        edges[pl.ds(to, 16), :] = jnp.where(taken, crossed, edges[pl.ds(to, 16), :])
        l = jnp.where(even, high, low) + m
        g = ((me + 1 - 2 * odd) * count + l).astype(jnp.float32)
        to = pl.multiple_of(at_them + 16 * l, 16)
        taken = jnp.where(even, g - their_limit, their_limit - g - 1.0) >= 0.0
        for half in range(2):
            crossed = theirs[brought + 16 * m + 8 * half : brought + 16 * m + 8 * half + 8, :]
            at = pl.multiple_of(to + 8 * half, 8)
            edges[pl.ds(at, 8), :] = jnp.where(taken, crossed, edges[pl.ds(at, 8), :])
    for k in range(3):
        asked = range(k * CAP, (k + 1) * CAP)
        values = [edges[pl.ds(rows_ref[n], 4, stride=2), :] for n in asked]
        for n, value in zip(asked, values):
            message[pl.ds(8 * (n // 2) + n % 2, 4, stride=2), :] = value


def answers(old_range, rows, mine, theirs, margin, per_device):
    side = mine.shape[1]
    return pl.pallas_call(
        functools.partial(answer_kernel, margin, per_device),
        in_specs=[SMEM, SMEM, VMEM, VMEM],
        out_specs=[VMEM, VMEM],
        out_shape=[
            jax.ShapeDtypeStruct((32 * per_device, side), jnp.float32),
            jax.ShapeDtypeStruct((12 * CAP, side), jnp.float32),
        ],
        compiler_params=room(4),
        name="answers",
    )(old_range, rows, mine, theirs)


def add_rim(p, load, store, columns, lines):
    side = columns.shape[0]
    lane, line = iota(1, side), iota(0, side)
    rim = (lane == 0) | (lane == side - 1)
    south = [lines[pl.ds(8 * p + 2 * f + 1, 1), :] for f in range(3)]
    north = [lines[pl.ds(8 * p + 2 * f, 1), :] for f in range(3)]
    steps = side // ROWS
    group = 4
    for start in range(0, steps, group):
        done = []
        for j in range(start, start + group):
            held = columns[spread(j, side), :]
            for f in range(3):
                value = load(f, j) + jnp.where(rim, pltpu.roll(held, side - 1 - 8 * p - 2 * f, 1), 0.0)
                if j == 0:
                    value = value + jnp.where(line == 0, south[f], 0.0)
                if j == steps - 1:
                    value = value + jnp.where(line == ROWS - 1, north[f], 0.0)
                done.append((f, j, value))
        for f, j, value in done:
            store(f, j, value)


def rim_terms(rows_ref, edges, crossed, passed, columns, lines, source, ghost, turn, count, odd):
    total = edges.shape[0]
    step = crossed.shape[0]
    source[0:total, :] = edges[...]
    source[total : total + step, :] = crossed[...]
    source[total + step : total + 2 * step, :] = passed[...]
    field = lax.broadcasted_iota(jnp.int32, (4, edges.shape[1]), 0)
    group = 4
    for start in range(0, count, group):
        fetched = []
        for p in range(start, start + group):
            for s in range(4):
                row = rows_ref[4 * p + s]
                wall = row < 0
                value = source[pl.ds(jnp.where(wall, -1 - row, row), 4, stride=2), :]
                value = jnp.where((field == 1 + s // 2) & wall, -value, value)
                fetched.append((16 * p + 8 * (s // 2) + 1 - s % 2, value))
        for target, value in fetched:
            ghost[pl.ds(target, 4, stride=2), :] = value
    turn[...] = jnp.zeros_like(turn)
    lines[...] = jnp.zeros_like(lines)
    for s in range(4):
        parity = 1 - s % 2
        sign = 1.0 - 2.0 * parity
        axis = s // 2
        normal, across = (1, 2) if axis == 0 else (2, 1)

        def both(f):
            row = 8 * axis + 2 * f + parity
            own = source[pl.ds(16 * count * odd + row, count, stride=16), :]
            return own, ghost[pl.ds(row, count, stride=16), :]

        hc, hg = both(0)
        nc, ng = both(normal)
        ac, ag = both(across)
        bc, bg = both(3)
        rc, rg = lax.rsqrt(hc), lax.rsqrt(hg)
        uc, ug = nc * rc * rc, ng * rg * rg
        top = jnp.maximum(jnp.abs(uc) + hc * rc, jnp.abs(ug) + hg * rg)
        fc, fg = nc * uc + 0.5 * hc * hc, ng * ug + 0.5 * hg * hg
        c_h = -HALF * (sign * (nc + ng) - top * ((hg + bg) - (hc + bc)))
        c_n = -HALF * (sign * (fc + fg + hc * bg) - top * (ng - nc))
        c_t = -HALF * (sign * (ac * uc + ag * ug) - top * (ag - ac))
        for f, value in ((0, c_h), (normal, c_n), (across, c_t)):
            target = turn if axis == 0 else lines
            target[pl.ds(2 * f + parity, count, stride=8), :] = value
    columns[...] = jnp.transpose(turn[...])


def most_kernel(
    margin, range_ref, rows_ref, edges, crossed, passed, own, theirs, out, columns, lines, result, source, ghost, turn, sems
):
    count, side = own.shape[0], columns.shape[0]
    me, odd = position()
    even = odd == 0
    rim_terms(rows_ref, edges, crossed, passed, columns, lines, source, ghost, turn, count, odd)
    start, stop = range_ref[0, 0], range_ref[0, 1]
    first = (1 - odd) * margin
    many = count - margin

    def copy(i):
        return pltpu.make_async_copy(result.at[i], out.at[first + i], sems.at[i])

    @pl.loop(0, many)
    def _(i):
        p = first + i
        g = me * count + p
        taken = jnp.where(even, g >= stop, g < start)
        m = jnp.clip(jnp.where(even, p - (count - margin), p), 0, margin - 1)

        def load(f, k):
            at = pl.multiple_of(m * (3 * side) + (f * side + ROWS * k), ROWS)
            return jnp.where(taken, theirs[pl.ds(at, ROWS), :], own[p, f, ROWS * k : ROWS * (k + 1), :])

        def store(f, k, value):
            result[i, f, spread(k, side), :] = value

        add_rim(p, load, store, columns, lines)
        copy(i).start()

    for i in range(many):
        copy(i).wait()


def most(old_range, rows, edges, crossed, passed, own, theirs, margin):
    count, _, side, _ = own.shape
    many = count - margin
    return pl.pallas_call(
        functools.partial(most_kernel, margin),
        in_specs=[SMEM, SMEM] + [VMEM] * 5,
        out_specs=[HBM, VMEM, VMEM],
        out_shape=[
            jax.ShapeDtypeStruct(own.shape, jnp.float32),
            jax.ShapeDtypeStruct((side, side), jnp.float32),
            jax.ShapeDtypeStruct((side, side), jnp.float32),
        ],
        scratch_shapes=[
            pltpu.VMEM((many, 3, side, side), jnp.float32),
            pltpu.VMEM((edges.shape[0] + 2 * crossed.shape[0], side), jnp.float32),
            pltpu.VMEM((16 * count, side), jnp.float32),
            pltpu.VMEM((side, side), jnp.float32),
            pltpu.SemaphoreType.DMA((many,)),
        ],
        compiler_params=room(6),
        name="most",
    )(old_range, rows, edges, crossed, passed, own, theirs)


def rest_kernel(margin, range_ref, own, arrived, columns, lines, _, out, result, sems):
    count, side = own.shape[0], columns.shape[0]
    me, odd = position()
    even = odd == 0
    start, stop = range_ref[0, 0], range_ref[0, 1]
    first = odd * (count - margin)

    def copy(i):
        return pltpu.make_async_copy(result.at[i], out.at[first + i], sems.at[i])

    @pl.loop(0, margin)
    def _(i):
        p = first + i
        g = me * count + p
        taken = jnp.where(even, g < start, g >= stop)

        def load(f, k):
            at = slice(ROWS * k, ROWS * (k + 1))
            return jnp.where(taken, arrived[i, f, at, :], own[p, f, at, :])

        def store(f, k, value):
            result[i, f, spread(k, side), :] = value

        add_rim(p, load, store, columns, lines)
        copy(i).start()

    for i in range(margin):
        copy(i).wait()


def rest(old_range, own, arrived, columns, lines, filled, margin):
    count, _, side, _ = own.shape
    return pl.pallas_call(
        functools.partial(rest_kernel, margin),
        in_specs=[SMEM] + [VMEM] * 4 + [HBM],
        out_specs=HBM,
        out_shape=jax.ShapeDtypeStruct(own.shape, jnp.float32),
        scratch_shapes=[
            pltpu.VMEM((margin, 3, side, side), jnp.float32),
            pltpu.SemaphoreType.DMA((margin,)),
        ],
        input_output_aliases={5: 0},
        compiler_params=room(4),
        name="rest",
    )(old_range, own, arrived, columns, lines, filled)


def swapped(value, first):
    pairs = [(i, i + 1) for i in range(first, lax.axis_size(AXES) - 1, 2)]
    return lax.ppermute(value, AXES, pairs + [(j, i) for i, j in pairs])


def ranks(named):
    size = named.shape[-1]
    earlier = jnp.arange(size)[:, None] < jnp.arange(size)[None, :]
    return jnp.sum(jnp.where(named[..., :, None] & earlier, 1, 0), axis=-2)


def local(old_cells, old_range, neighbours):
    per_device = neighbours.shape[0]
    side = old_cells.shape[3]
    margin = (old_cells.shape[0] - per_device) // 2
    entries = 4 * per_device
    me, odd = position()
    brought = layout(margin, per_device, side)[3]

    their_table = swapped(neighbours, 0)
    leaving, leaving_edges = outer_patches(old_cells, margin)
    arrived = swapped(leaving, 1)

    tables = jnp.where(
        odd == 0,
        jnp.concatenate([neighbours.reshape(1, -1), their_table.reshape(1, -1)], axis=1),
        jnp.concatenate([their_table.reshape(1, -1), neighbours.reshape(1, -1)], axis=1),
    ).astype(jnp.float32)
    tables = jnp.pad(tables, ((0, 7), (0, side - 2 * entries)))
    came = swapped(jnp.concatenate([leaving_edges, tables], axis=0), 1)

    shared, own = home_patches(old_range, old_cells, margin, per_device)
    shared = lax.dynamic_update_slice(shared, came, (brought, 0))
    theirs = swapped(shared, 0)

    entry = jnp.arange(entries, dtype=jnp.int32)
    entry_side = entry % 4
    at_side = 8 * (entry_side // 2) + entry_side % 2
    asked_by = came[16 * margin, : 2 * entries].astype(jnp.int32).reshape(2, entries)
    middle = jnp.where(odd == 0, asked_by[1], asked_by[0])
    listed = jnp.stack([asked_by[0], middle, asked_by[1]])
    owners = me + jnp.where(odd == 0, jnp.array([0, 0, 1], jnp.int32), jnp.array([-1, 0, 0], jnp.int32))
    asked = (listed >= 0) & (listed // per_device == owners[:, None])
    rows = 16 * (listed - 2 * per_device * (me // 2)) + at_side
    chosen = asked[:, None, :] & (ranks(asked)[:, None, :] == jnp.arange(CAP)[None, :, None])
    send_rows = jnp.sum(jnp.where(chosen, rows[:, None, :], 0), axis=2).reshape(-1)

    edges, message = answers(old_range, send_rows, shared, theirs, margin, per_device)
    crossed = swapped(message, 1)
    passed = swapped(crossed, 0)

    listed = neighbours.reshape(-1)
    owner = listed // per_device
    mine, total, step = 32 * per_device, 16 * per_device, 12 * CAP
    lists = jnp.where(
        odd == 0,
        jnp.array([[-2, mine], [-1, mine + 4 * CAP], [2, mine + step]], jnp.int32),
        jnp.array([[-2, mine + step + 8 * CAP], [1, mine + 4 * CAP], [2, mine + 8 * CAP]], jnp.int32),
    )
    named = (listed >= 0) & (owner - me == lists[:, :1])
    place = ranks(named)
    across = jnp.sum(jnp.where(named, lists[:, 1:] + 8 * (place // 2) + place % 2, 0), axis=0)
    within = 16 * (listed - 2 * per_device * (me // 2)) + at_side
    wall = total * odd + 16 * (entry // 4) + 8 * (entry_side // 2) + 1 - entry_side % 2
    ghost_rows = jnp.where(listed < 0, -1 - wall, jnp.where(owner // 2 == me // 2, within, across))

    filled, columns, lines = most(old_range, ghost_rows, edges, crossed, passed, own, theirs, margin)
    return rest(old_range, own, arrived, columns, lines, filled, margin)


def solution(mesh):
    placed = (
        P(("member", "curve", "sub"), None, None, None),
        P(("member", "curve", "sub"), None),
        P(("member", "curve", "sub"), None),
    )
    return jax.shard_map(
        local,
        mesh=mesh,
        in_specs=placed,
        out_specs=P(("member", "curve", "sub"), None, None, None),
        check_vma=False,
    )
```

```python
import functools

import jax
import jax.numpy as jnp
from jax import lax
from jax.experimental import pallas as pl
from jax.experimental.pallas import tpu as pltpu
from jax.sharding import PartitionSpec as P

RATE_STEP = 0.1
HALF = 0.5 * RATE_STEP
AXES = ("curve", "sub")
CAP = 8
ROWS = 8
VMEM = pl.BlockSpec(memory_space=pltpu.VMEM)
SMEM = pl.BlockSpec(memory_space=pltpu.SMEM)
HBM = pl.BlockSpec(memory_space=pltpu.HBM)


def position():
    me = lax.axis_index(AXES)
    return me, lax.rem(me, 2)


def iota(axis, side):
    return lax.broadcasted_iota(jnp.int32, (ROWS, side), axis)


def spread(j, side):
    return pl.ds(j, ROWS, stride=side // ROWS)


def pieces(x):
    high = x.astype(jnp.bfloat16)
    low = (x - high.astype(jnp.float32)).astype(jnp.bfloat16)
    return jnp.concatenate([high, low], axis=1)


def product(parts, weights):
    return jnp.dot(parts, weights, preferred_element_type=jnp.float32)


AHEAD, EAST, SUMS, SLOPE = slice(0, 2), slice(2, 4), slice(4, 5), slice(5, 6)


def fill_weights(weights):
    side = weights.shape[0] // 2
    row = lax.broadcasted_iota(jnp.int32, (side, side), 0)
    lane = lax.broadcasted_iota(jnp.int32, (side, side), 1)
    one = lambda where: jnp.where(where, 1.0, 0.0)
    after, here, before = one(row == lane + 1), one(row == lane), one(row == lane - 1)
    inner_e, inner_w = lane != side - 1, lane != 0
    east = jnp.where(inner_e, after + here, 0.0)
    west = jnp.where(inner_w, here + before, 0.0)
    blocks = (
        after,
        before,
        jnp.where(inner_e, after - here, 0.0),
        jnp.where(inner_w, here - before, 0.0),
        east - west,
        after - before,
    )
    for n, block in enumerate(blocks):
        for half in range(2):
            weights[half * side : (half + 1) * side, n * side : (n + 1) * side] = block.astype(jnp.bfloat16)


def inner_update(load, store, columns, at, side, weights):
    lane, line = iota(1, side), iota(0, side)
    pair = lane // 2
    first, last = line == 0, line == ROWS - 1
    steps = side // ROWS
    marks = [pair == at // 2 + f for f in range(4)]

    def cell(h, mx, my, bed):
        root = lax.rsqrt(h)
        celerity = h * root
        inverse = root * root
        u = mx * inverse
        v = my * inverse
        half_sq = 0.5 * h * h
        cross = my * u
        rate_y = jnp.abs(v) + celerity
        rate_x = jnp.abs(u) + celerity
        return (rate_y, h + bed, mx, my, cross, my * v + half_sq, bed), rate_x, mx * u + half_sq, h

    def face_y(low, high):
        top = jnp.maximum(low[0], high[0])
        return [
            (high[3] + low[3]) - top * (high[1] - low[1]),
            (high[4] + low[4]) - top * (high[2] - low[2]),
            (high[5] + low[5]) - top * (high[3] - low[3]),
        ]

    def taken(block):
        return weights[:, block.start * side : block.stop * side]

    cells = [cell(*[load(f, j) for f in range(4)]) for j in range(steps)]
    stack = lambda pick: jnp.concatenate([pick(c) for c in cells], axis=0)
    rates = product(pieces(stack(lambda c: c[1])), taken(AHEAD))
    eta, mx, my, cross, bed = (pieces(stack(lambda c, n=n: c[0][n])) for n in (1, 2, 3, 4, 6))
    fx = pieces(stack(lambda c: c[2]))
    jumps = [product(each, taken(EAST)) for each in (eta, mx, my)]
    sums = [product(each, taken(SUMS)) for each in (mx, fx, cross)]
    slopes = product(bed, taken(SLOPE))

    for j in range(steps):
        held = columns.load(j)
        _, _, mx, my, _, _, bed = cells[j][0]
        for f, value in enumerate((cells[j][3], mx, my, bed)):
            held = jnp.where(marks[f], pltpu.roll(value, at + 2 * f + 1, 1), held)
        columns.store(j, held)

    low = [pltpu.roll(each, 1, 0) for each in cells[steps - 1][0]]
    faces = []
    for j in range(steps):
        faces.append(face_y(low, cells[j][0]))
        low = cells[j][0]
    faces[0] = [jnp.where(first, 0.0, each) for each in faces[0]]
    beds = [c[0][6] for c in cells]
    under = jnp.where(first, 0.0, pltpu.roll(beds[-1], 1, 0))
    over = jnp.where(last, 0.0, pltpu.roll(beds[0], ROWS - 1, 0))
    faces.append([jnp.where(last, 0.0, pltpu.roll(each, ROWS - 1, 0)) for each in faces[0]])
    for j in range(steps):
        (_, _, mx, my, _, _, _), rate, _, h = cells[j]
        rows = slice(ROWS * j, ROWS * (j + 1))
        top_e = jnp.maximum(rate, rates[rows, :side])
        top_w = jnp.maximum(rate, rates[rows, side:])
        x = [s[rows] - (top_e * d[rows, :side] - top_w * d[rows, side:]) for s, d in zip(sums, jumps)]
        south, north = faces[j], faces[j + 1]
        slope_y = (beds[j + 1] if j + 1 < steps else over) - (beds[j - 1] if j else under)
        store(0, j, h - HALF * (x[0] + (north[0] - south[0])))
        store(1, j, mx - HALF * (x[1] + h * slopes[rows] + (north[1] - south[1])))
        store(2, j, my - HALF * (x[2] + h * slope_y + (north[2] - south[2])))


class Columns:
    def __init__(self, ref):
        self.ref, self.side = ref, ref.shape[0]

    def load(self, j):
        return self.ref[spread(j, self.side), :]

    def store(self, j, value):
        self.ref[spread(j, self.side), :] = value


def take_edges(count, cells, slot_of, columns, edges, base):
    side = columns.shape[0]
    turned = jnp.transpose(columns[...])
    for p in range(count):
        edges[base + 16 * p : base + 16 * p + 8, :] = turned[8 * p : 8 * p + 8, :]
        for f in range(4):
            row = base + 16 * p + 8 + 2 * f
            edges[row : row + 1, :] = cells[slot_of(p), f, side - 1 : side, :]
            edges[row + 1 : row + 2, :] = cells[slot_of(p), f, 0:1, :]


def update_one(cells, i, columns, lane_at, side, weights, put):
    inner_update(
        lambda f, j: cells[i, f, spread(j, side), :],
        lambda f, j, value: put(f, ROWS * j, value),
        Columns(columns),
        lane_at,
        side,
        weights,
    )


def fetch(cells_hbm, first, cells, sems, parts):
    def copy(i):
        return pltpu.make_async_copy(cells_hbm.at[first + i], cells.at[i], sems.at[i])

    for start, count in parts:
        for i in range(count):
            copy(start + i).start()
    return copy


def outer_kernel(margin, cells_hbm, out, edges, cells, columns, weights, sems):
    side = columns.shape[0]
    _, odd = position()
    copy = fetch(cells_hbm, odd * (cells_hbm.shape[0] - margin), cells, sems, [(0, margin)])
    fill_weights(weights)

    @pl.loop(0, margin)
    def _(i):
        copy(i).wait()

        def put(f, row, value):
            out[i, f, row : row + ROWS, :] = value

        update_one(cells, i, columns, 8 * i, side, weights, put)

    take_edges(margin, cells, lambda p: p, columns, edges, 0)


def cost(patches, side):
    return pl.CostEstimate(
        flops=patches * side * side * 800,
        bytes_accessed=patches * side * side * 28,
        transcendentals=patches * side * side,
    )


def room(mebibytes):
    return pltpu.CompilerParams(vmem_limit_bytes=mebibytes << 20)


def outer_patches(old_cells, margin):
    side = old_cells.shape[3]
    return pl.pallas_call(
        functools.partial(outer_kernel, margin),
        in_specs=[HBM],
        out_specs=[VMEM, VMEM],
        out_shape=[
            jax.ShapeDtypeStruct((margin, 3, side, side), jnp.float32),
            jax.ShapeDtypeStruct((16 * margin, side), jnp.float32),
        ],
        scratch_shapes=[
            pltpu.VMEM((margin, 4, side, side), jnp.float32),
            pltpu.VMEM((side, side), jnp.float32),
            pltpu.VMEM((2 * side, 6 * side), jnp.bfloat16),
            pltpu.SemaphoreType.DMA((margin,)),
        ],
        cost_estimate=cost(margin, side),
        compiler_params=room(48),
        name="outer",
    )(old_cells)


def layout(margin, per_device, side):
    inner = 3 * side * margin
    home = inner + 16 * margin
    limit = home + 16 * per_device
    brought = limit + 8
    return inner, home, limit, brought, brought + 16 * margin + 8


def home_kernel(margin, range_ref, cells_hbm, shared, own, cells, columns, weights, sems):
    side = columns.shape[0]
    count = own.shape[0]
    inner, home, limit, _, _ = layout(margin, count, side)
    _, odd = position()
    inner_at = (1 - odd) * count
    home_at = odd * margin
    parts = [(inner_at, margin), (home_at, count)]
    copy = fetch(cells_hbm, (1 - odd) * margin, cells, sems, parts)
    fill_weights(weights)

    @pl.loop(0, margin)
    def _(i):
        copy(inner_at + i).wait()

        def put(f, row, value):
            at = pl.multiple_of(i * (3 * side) + (f * side + row), ROWS)
            shared[pl.ds(at, ROWS), :] = value

        update_one(cells, inner_at + i, columns, 8 * i, side, weights, put)

    take_edges(margin, cells, lambda p: inner_at + p, columns, shared, inner)

    @pl.loop(0, count)
    def _(i):
        copy(home_at + i).wait()

        def put(f, row, value):
            own[i, f, row : row + ROWS, :] = value

        update_one(cells, home_at + i, columns, 8 * i, side, weights, put)

    take_edges(count, cells, lambda p: home_at + p, columns, shared, home)
    outer_limit = jnp.where(odd == 1, range_ref[0, 1], range_ref[0, 0])
    shared[limit : limit + 8, :] = jnp.full((8, side), outer_limit, jnp.int32).astype(jnp.float32)


def home_patches(old_range, old_cells, margin, per_device):
    side = old_cells.shape[3]
    total = layout(margin, per_device, side)[-1]
    return pl.pallas_call(
        functools.partial(home_kernel, margin),
        in_specs=[SMEM, HBM],
        out_specs=[VMEM, VMEM],
        out_shape=[
            jax.ShapeDtypeStruct((total, side), jnp.float32),
            jax.ShapeDtypeStruct((per_device, 3, side, side), jnp.float32),
        ],
        scratch_shapes=[
            pltpu.VMEM((margin + per_device, 4, side, side), jnp.float32),
            pltpu.VMEM((side, side), jnp.float32),
            pltpu.VMEM((2 * side, 6 * side), jnp.bfloat16),
            pltpu.SemaphoreType.DMA((margin + per_device,)),
        ],
        cost_estimate=cost(margin + per_device, side),
        compiler_params=room(48),
        name="home",
    )(old_range, old_cells)


def answer_kernel(margin, count, range_ref, rows_ref, mine, theirs, edges, message):
    side = edges.shape[1]
    inner, home, limit, brought, _ = layout(margin, count, side)
    me, odd = position()
    start, stop = range_ref[0, 0], range_ref[0, 1]
    even = odd == 0
    at_me = pl.multiple_of(16 * count * odd, 16)
    at_them = pl.multiple_of(16 * count * (1 - odd), 16)
    edges[pl.ds(at_me, 16 * count), :] = mine[home : home + 16 * count, :]
    edges[pl.ds(at_them, 16 * count), :] = theirs[home : home + 16 * count, :]
    their_limit = theirs[limit : limit + 8, :]
    low, high = 0, count - margin
    for m in range(margin):
        l = jnp.where(even, high, low) + m
        g = me * count + l
        taken = jnp.where(even, g >= stop, g < start)
        to = pl.multiple_of(at_me + 16 * l, 16)
        from_pair = theirs[inner + 16 * m : inner + 16 * (m + 1), :]
        edges[pl.ds(to, 16), :] = jnp.where(taken, from_pair, edges[pl.ds(to, 16), :])
        l = jnp.where(even, low, high) + m
        g = (me + 1 - 2 * odd) * count + l
        taken = jnp.where(even, g < stop, g >= start)
        to = pl.multiple_of(at_them + 16 * l, 16)
        from_pair = mine[inner + 16 * m : inner + 16 * (m + 1), :]
        edges[pl.ds(to, 16), :] = jnp.where(taken, from_pair, edges[pl.ds(to, 16), :])
        l = jnp.where(even, low, high) + m
        g = me * count + l
        taken = jnp.where(even, g < start, g >= stop)
        to = pl.multiple_of(at_me + 16 * l, 16)
        crossed = mine[brought + 16 * m : brought + 16 * (m + 1), :]
        edges[pl.ds(to, 16), :] = jnp.where(taken, crossed, edges[pl.ds(to, 16), :])
        l = jnp.where(even, high, low) + m
        g = ((me + 1 - 2 * odd) * count + l).astype(jnp.float32)
        to = pl.multiple_of(at_them + 16 * l, 16)
        taken = jnp.where(even, g - their_limit, their_limit - g - 1.0) >= 0.0
        for half in range(2):
            crossed = theirs[brought + 16 * m + 8 * half : brought + 16 * m + 8 * half + 8, :]
            at = pl.multiple_of(to + 8 * half, 8)
            edges[pl.ds(at, 8), :] = jnp.where(taken, crossed, edges[pl.ds(at, 8), :])
    for k in range(3):
        asked = range(k * CAP, (k + 1) * CAP)
        values = [edges[pl.ds(rows_ref[n], 4, stride=2), :] for n in asked]
        for n, value in zip(asked, values):
            message[pl.ds(8 * (n // 2) + n % 2, 4, stride=2), :] = value


def answers(old_range, rows, mine, theirs, margin, per_device):
    side = mine.shape[1]
    return pl.pallas_call(
        functools.partial(answer_kernel, margin, per_device),
        in_specs=[SMEM, SMEM, VMEM, VMEM],
        out_specs=[VMEM, VMEM],
        out_shape=[
            jax.ShapeDtypeStruct((32 * per_device, side), jnp.float32),
            jax.ShapeDtypeStruct((12 * CAP, side), jnp.float32),
        ],
        compiler_params=room(4),
        name="answers",
    )(old_range, rows, mine, theirs)


def add_rim(p, load, store, columns, lines):
    side = lines.shape[1]
    line = iota(0, side)
    row = lax.broadcasted_iota(jnp.int32, (side, side), 0)
    lane = lax.broadcasted_iota(jnp.int32, (side, side), 1)
    source = row - jnp.where(lane == 0, 1, jnp.where(lane == side - 1, 0, 1024))
    places = [jnp.where(source == 8 * p + 2 * f, 1.0, 0.0).astype(jnp.bfloat16) for f in range(3)]
    place = jnp.concatenate(places, axis=1)
    terms = product(columns[...], jnp.concatenate([place, place], axis=0))
    south = [lines[pl.ds(8 * p + 2 * f + 1, 1), :] for f in range(3)]
    north = [lines[pl.ds(8 * p + 2 * f, 1), :] for f in range(3)]
    steps = side // ROWS
    group = 4
    for start in range(0, steps, group):
        done = []
        for j in range(start, start + group):
            for f in range(3):
                value = load(f, j) + terms[ROWS * j : ROWS * (j + 1), f * side : (f + 1) * side]
                if j == 0:
                    value = value + jnp.where(line == 0, south[f], 0.0)
                if j == steps - 1:
                    value = value + jnp.where(line == ROWS - 1, north[f], 0.0)
                done.append((f, j, value))
        for f, j, value in done:
            store(f, j, value)


def rim_terms(rows_ref, edges, crossed, passed, columns, lines, source, ghost, turn, count, odd):
    total = edges.shape[0]
    step = crossed.shape[0]
    source[0:total, :] = edges[...]
    source[total : total + step, :] = crossed[...]
    source[total + step : total + 2 * step, :] = passed[...]
    field = lax.broadcasted_iota(jnp.int32, (4, edges.shape[1]), 0)
    group = 4
    for start in range(0, count, group):
        fetched = []
        for p in range(start, start + group):
            for s in range(4):
                row = rows_ref[4 * p + s]
                wall = row < 0
                value = source[pl.ds(jnp.where(wall, -1 - row, row), 4, stride=2), :]
                value = jnp.where((field == 1 + s // 2) & wall, -value, value)
                fetched.append((16 * p + 8 * (s // 2) + 1 - s % 2, value))
        for target, value in fetched:
            ghost[pl.ds(target, 4, stride=2), :] = value
    turn[...] = jnp.zeros_like(turn)
    lines[...] = jnp.zeros_like(lines)
    for s in range(4):
        parity = 1 - s % 2
        sign = 1.0 - 2.0 * parity
        axis = s // 2
        normal, across = (1, 2) if axis == 0 else (2, 1)

        def both(f):
            row = 8 * axis + 2 * f + parity
            own = source[pl.ds(16 * count * odd + row, count, stride=16), :]
            return own, ghost[pl.ds(row, count, stride=16), :]

        hc, hg = both(0)
        nc, ng = both(normal)
        ac, ag = both(across)
        bc, bg = both(3)
        rc, rg = lax.rsqrt(hc), lax.rsqrt(hg)
        uc, ug = nc * rc * rc, ng * rg * rg
        top = jnp.maximum(jnp.abs(uc) + hc * rc, jnp.abs(ug) + hg * rg)
        fc, fg = nc * uc + 0.5 * hc * hc, ng * ug + 0.5 * hg * hg
        c_h = -HALF * (sign * (nc + ng) - top * ((hg + bg) - (hc + bc)))
        c_n = -HALF * (sign * (fc + fg + hc * bg) - top * (ng - nc))
        c_t = -HALF * (sign * (ac * uc + ag * ug) - top * (ag - ac))
        for f, value in ((0, c_h), (normal, c_n), (across, c_t)):
            target = turn if axis == 0 else lines
            target[pl.ds(2 * f + parity, count, stride=8), :] = value
    turn[...] = jnp.transpose(turn[...])
    side = turn.shape[0]
    columns[...] = pieces(jnp.concatenate([turn[spread(j, side), :] for j in range(side // ROWS)], axis=0))


def most_kernel(
    margin, range_ref, rows_ref, edges, crossed, passed, own, theirs, out, columns, lines, result, source, ghost, turn, sems
):
    count, side = own.shape[0], columns.shape[0]
    me, odd = position()
    even = odd == 0
    rim_terms(rows_ref, edges, crossed, passed, columns, lines, source, ghost, turn, count, odd)
    start, stop = range_ref[0, 0], range_ref[0, 1]
    first = (1 - odd) * margin
    many = count - margin

    def copy(i):
        return pltpu.make_async_copy(result.at[i], out.at[first + i], sems.at[i])

    @pl.loop(0, many)
    def _(i):
        p = first + i
        g = me * count + p
        taken = jnp.where(even, g >= stop, g < start)
        m = jnp.clip(jnp.where(even, p - (count - margin), p), 0, margin - 1)

        def load(f, k):
            at = pl.multiple_of(m * (3 * side) + (f * side + ROWS * k), ROWS)
            return jnp.where(taken, theirs[pl.ds(at, ROWS), :], own[p, f, ROWS * k : ROWS * (k + 1), :])

        def store(f, k, value):
            result[i, f, spread(k, side), :] = value

        add_rim(p, load, store, columns, lines)
        copy(i).start()

    for i in range(many):
        copy(i).wait()


def most(old_range, rows, edges, crossed, passed, own, theirs, margin):
    count, _, side, _ = own.shape
    many = count - margin
    return pl.pallas_call(
        functools.partial(most_kernel, margin),
        in_specs=[SMEM, SMEM] + [VMEM] * 5,
        out_specs=[HBM, VMEM, VMEM],
        out_shape=[
            jax.ShapeDtypeStruct(own.shape, jnp.float32),
            jax.ShapeDtypeStruct((side, 2 * side), jnp.bfloat16),
            jax.ShapeDtypeStruct((side, side), jnp.float32),
        ],
        scratch_shapes=[
            pltpu.VMEM((many, 3, side, side), jnp.float32),
            pltpu.VMEM((edges.shape[0] + 2 * crossed.shape[0], side), jnp.float32),
            pltpu.VMEM((16 * count, side), jnp.float32),
            pltpu.VMEM((side, side), jnp.float32),
            pltpu.SemaphoreType.DMA((many,)),
        ],
        compiler_params=room(6),
        name="most",
    )(old_range, rows, edges, crossed, passed, own, theirs)


def rest_kernel(margin, range_ref, own, arrived, columns, lines, _, out, result, sems):
    count, side = own.shape[0], columns.shape[0]
    me, odd = position()
    even = odd == 0
    start, stop = range_ref[0, 0], range_ref[0, 1]
    first = odd * (count - margin)

    def copy(i):
        return pltpu.make_async_copy(result.at[i], out.at[first + i], sems.at[i])

    @pl.loop(0, margin)
    def _(i):
        p = first + i
        g = me * count + p
        taken = jnp.where(even, g < start, g >= stop)

        def load(f, k):
            at = slice(ROWS * k, ROWS * (k + 1))
            return jnp.where(taken, arrived[i, f, at, :], own[p, f, at, :])

        def store(f, k, value):
            result[i, f, spread(k, side), :] = value

        add_rim(p, load, store, columns, lines)
        copy(i).start()

    for i in range(margin):
        copy(i).wait()


def rest(old_range, own, arrived, columns, lines, filled, margin):
    count, _, side, _ = own.shape
    return pl.pallas_call(
        functools.partial(rest_kernel, margin),
        in_specs=[SMEM] + [VMEM] * 4 + [HBM],
        out_specs=HBM,
        out_shape=jax.ShapeDtypeStruct(own.shape, jnp.float32),
        scratch_shapes=[
            pltpu.VMEM((margin, 3, side, side), jnp.float32),
            pltpu.SemaphoreType.DMA((margin,)),
        ],
        input_output_aliases={5: 0},
        compiler_params=room(4),
        name="rest",
    )(old_range, own, arrived, columns, lines, filled)


def swapped(value, first):
    pairs = [(i, i + 1) for i in range(first, lax.axis_size(AXES) - 1, 2)]
    return lax.ppermute(value, AXES, pairs + [(j, i) for i, j in pairs])


def ranks(named):
    size = named.shape[-1]
    earlier = jnp.arange(size)[:, None] < jnp.arange(size)[None, :]
    return jnp.sum(jnp.where(named[..., :, None] & earlier, 1, 0), axis=-2)


def local(old_cells, old_range, neighbours):
    per_device = neighbours.shape[0]
    side = old_cells.shape[3]
    margin = (old_cells.shape[0] - per_device) // 2
    entries = 4 * per_device
    me, odd = position()
    brought = layout(margin, per_device, side)[3]

    their_table = swapped(neighbours, 0)
    leaving, leaving_edges = outer_patches(old_cells, margin)
    arrived = swapped(leaving, 1)

    tables = jnp.where(
        odd == 0,
        jnp.concatenate([neighbours.reshape(1, -1), their_table.reshape(1, -1)], axis=1),
        jnp.concatenate([their_table.reshape(1, -1), neighbours.reshape(1, -1)], axis=1),
    ).astype(jnp.float32)
    tables = jnp.pad(tables, ((0, 7), (0, side - 2 * entries)))
    came = swapped(jnp.concatenate([leaving_edges, tables], axis=0), 1)

    shared, own = home_patches(old_range, old_cells, margin, per_device)
    shared = lax.dynamic_update_slice(shared, came, (brought, 0))
    theirs = swapped(shared, 0)

    entry = jnp.arange(entries, dtype=jnp.int32)
    entry_side = entry % 4
    at_side = 8 * (entry_side // 2) + entry_side % 2
    asked_by = came[16 * margin, : 2 * entries].astype(jnp.int32).reshape(2, entries)
    middle = jnp.where(odd == 0, asked_by[1], asked_by[0])
    listed = jnp.stack([asked_by[0], middle, asked_by[1]])
    owners = me + jnp.where(odd == 0, jnp.array([0, 0, 1], jnp.int32), jnp.array([-1, 0, 0], jnp.int32))
    asked = (listed >= 0) & (listed // per_device == owners[:, None])
    rows = 16 * (listed - 2 * per_device * (me // 2)) + at_side
    chosen = asked[:, None, :] & (ranks(asked)[:, None, :] == jnp.arange(CAP)[None, :, None])
    send_rows = jnp.sum(jnp.where(chosen, rows[:, None, :], 0), axis=2).reshape(-1)

    edges, message = answers(old_range, send_rows, shared, theirs, margin, per_device)
    crossed = swapped(message, 1)
    passed = swapped(crossed, 0)

    listed = neighbours.reshape(-1)
    owner = listed // per_device
    mine, total, step = 32 * per_device, 16 * per_device, 12 * CAP
    lists = jnp.where(
        odd == 0,
        jnp.array([[-2, mine], [-1, mine + 4 * CAP], [2, mine + step]], jnp.int32),
        jnp.array([[-2, mine + step + 8 * CAP], [1, mine + 4 * CAP], [2, mine + 8 * CAP]], jnp.int32),
    )
    named = (listed >= 0) & (owner - me == lists[:, :1])
    place = ranks(named)
    across = jnp.sum(jnp.where(named, lists[:, 1:] + 8 * (place // 2) + place % 2, 0), axis=0)
    within = 16 * (listed - 2 * per_device * (me // 2)) + at_side
    wall = total * odd + 16 * (entry // 4) + 8 * (entry_side // 2) + 1 - entry_side % 2
    ghost_rows = jnp.where(listed < 0, -1 - wall, jnp.where(owner // 2 == me // 2, within, across))

    filled, columns, lines = most(old_range, ghost_rows, edges, crossed, passed, own, theirs, margin)
    return rest(old_range, own, arrived, columns, lines, filled, margin)


def solution(mesh):
    placed = (
        P(("member", "curve", "sub"), None, None, None),
        P(("member", "curve", "sub"), None),
        P(("member", "curve", "sub"), None),
    )
    return jax.shard_map(
        local,
        mesh=mesh,
        in_specs=placed,
        out_specs=P(("member", "curve", "sub"), None, None, None),
        check_vma=False,
    )
```

```python
import functools

import jax
import jax.numpy as jnp
from jax import lax
from jax.experimental import pallas as pl
from jax.experimental.pallas import tpu as pltpu
from jax.sharding import PartitionSpec as P

RATE_STEP = 0.1
HALF = 0.5 * RATE_STEP
AXES = ("curve", "sub")
CAP = 8
ROWS = 8
PAIR = 2
VMEM = pl.BlockSpec(memory_space=pltpu.VMEM)
SMEM = pl.BlockSpec(memory_space=pltpu.SMEM)
HBM = pl.BlockSpec(memory_space=pltpu.HBM)


def position():
    me = lax.axis_index(AXES)
    return me, lax.rem(me, 2)


def iota(axis, side):
    return lax.broadcasted_iota(jnp.int32, (ROWS, side), axis)


def spread(j, side):
    return pl.ds(j, ROWS, stride=side // ROWS)


def pieces(x):
    high = x.astype(jnp.bfloat16)
    low = (x - high.astype(jnp.float32)).astype(jnp.bfloat16)
    return jnp.concatenate([high, low], axis=1)


def product(parts, weights):
    return jnp.dot(parts, weights, preferred_element_type=jnp.float32)


AHEAD, EAST, SUMS, SLOPE = slice(0, 2), slice(2, 4), slice(4, 5), slice(5, 6)


def fill_weights(weights):
    side = weights.shape[0] // 2
    row = lax.broadcasted_iota(jnp.int32, (side, side), 0)
    lane = lax.broadcasted_iota(jnp.int32, (side, side), 1)
    one = lambda where: jnp.where(where, 1.0, 0.0)
    after, here, before = one(row == lane + 1), one(row == lane), one(row == lane - 1)
    inner_e, inner_w = lane != side - 1, lane != 0
    east = jnp.where(inner_e, after + here, 0.0)
    west = jnp.where(inner_w, here + before, 0.0)
    blocks = (
        after,
        before,
        jnp.where(inner_e, after - here, 0.0),
        jnp.where(inner_w, here - before, 0.0),
        east - west,
        after - before,
    )
    for n, block in enumerate(blocks):
        for half in range(2):
            weights[half * side : (half + 1) * side, n * side : (n + 1) * side] = block.astype(jnp.bfloat16)


def inner_update(load, store, side, weights):
    line = iota(0, side)
    first, last = line == 0, line == ROWS - 1
    steps = side // ROWS

    def cell(h, mx, my, bed):
        root = lax.rsqrt(h)
        celerity = h * root
        inverse = root * root
        u = mx * inverse
        v = my * inverse
        half_sq = 0.5 * h * h
        cross = my * u
        rate_y = jnp.abs(v) + celerity
        rate_x = jnp.abs(u) + celerity
        return (rate_y, h + bed, mx, my, cross, my * v + half_sq, bed), rate_x, mx * u + half_sq, h

    def face_y(low, high):
        top = jnp.maximum(low[0], high[0])
        return [
            (high[3] + low[3]) - top * (high[1] - low[1]),
            (high[4] + low[4]) - top * (high[2] - low[2]),
            (high[5] + low[5]) - top * (high[3] - low[3]),
        ]

    def taken(block):
        return weights[:, block.start * side : block.stop * side]

    cells = [cell(*[load(f, j) for f in range(4)]) for j in range(steps)]
    stack = lambda pick: jnp.concatenate([pick(c) for c in cells], axis=0)
    rates = product(pieces(stack(lambda c: c[1])), taken(AHEAD))
    eta, mx, my, cross, bed = (pieces(stack(lambda c, n=n: c[0][n])) for n in (1, 2, 3, 4, 6))
    fx = pieces(stack(lambda c: c[2]))
    jumps = [product(each, taken(EAST)) for each in (eta, mx, my)]
    sums = [product(each, taken(SUMS)) for each in (mx, fx, cross)]
    slopes = product(bed, taken(SLOPE))
    low = [pltpu.roll(each, 1, 0) for each in cells[steps - 1][0]]
    faces = []
    for j in range(steps):
        faces.append(face_y(low, cells[j][0]))
        low = cells[j][0]
    faces[0] = [jnp.where(first, 0.0, each) for each in faces[0]]
    beds = [c[0][6] for c in cells]
    under = jnp.where(first, 0.0, pltpu.roll(beds[-1], 1, 0))
    over = jnp.where(last, 0.0, pltpu.roll(beds[0], ROWS - 1, 0))
    faces.append([jnp.where(last, 0.0, pltpu.roll(each, ROWS - 1, 0)) for each in faces[0]])
    for j in range(steps):
        (_, _, mx, my, _, _, _), rate, _, h = cells[j]
        rows = slice(ROWS * j, ROWS * (j + 1))
        top_e = jnp.maximum(rate, rates[rows, :side])
        top_w = jnp.maximum(rate, rates[rows, side:])
        x = [s[rows] - (top_e * d[rows, :side] - top_w * d[rows, side:]) for s, d in zip(sums, jumps)]
        south, north = faces[j], faces[j + 1]
        slope_y = (beds[j + 1] if j + 1 < steps else over) - (beds[j - 1] if j else under)
        store(0, j, h - HALF * (x[0] + (north[0] - south[0])))
        store(1, j, mx - HALF * (x[1] + h * slopes[rows] + (north[1] - south[1])))
        store(2, j, my - HALF * (x[2] + h * slope_y + (north[2] - south[2])))


def gather_columns(loads, columns, first_at, side):
    pair = iota(1, side) // 2
    for j in range(side // ROWS):
        held = columns[spread(j, side), :]
        for n, load in enumerate(loads):
            at = first_at + 8 * n
            for f in range(4):
                held = jnp.where(pair == at // 2 + f, pltpu.roll(load(f, j), at + 2 * f + 1, 1), held)
        columns[spread(j, side), :] = held


def take_edges(count, cells, slot_of, columns, edges, base):
    side = columns.shape[0]
    turned = jnp.transpose(columns[...])
    for p in range(count):
        edges[base + 16 * p : base + 16 * p + 8, :] = turned[8 * p : 8 * p + 8, :]
        for f in range(4):
            row = base + 16 * p + 8 + 2 * f
            edges[row : row + 1, :] = cells[slot_of(p), f, side - 1 : side, :]
            edges[row + 1 : row + 2, :] = cells[slot_of(p), f, 0:1, :]


def loader(cells, i):
    side = cells.shape[3]
    return lambda f, j: cells[i, f, spread(j, side), :]


def update(cells, first, many, weights, put):
    for n in range(many):
        store = lambda f, j, value, n=n: put(n, f, ROWS * j, value)
        inner_update(loader(cells, first + n), store, cells.shape[3], weights)


def fetch(cells_hbm, first, cells, sems, parts):
    def copy(i):
        return pltpu.make_async_copy(cells_hbm.at[first + i], cells.at[i], sems.at[i])

    for start, count in parts:
        for i in range(count):
            copy(start + i).start()
    return copy


def outer_slot(cells_hbm, margin):
    _, odd = position()
    return odd * (cells_hbm.shape[0] - margin)


def outer_edges_kernel(margin, cells_hbm, edges, cells, columns, sems):
    copy = fetch(cells_hbm, outer_slot(cells_hbm, margin), cells, sems, [(0, margin)])
    for i in range(margin):
        copy(i).wait()
    gather_columns([loader(cells, i) for i in range(margin)], columns, 0, columns.shape[0])
    take_edges(margin, cells, lambda p: p, columns, edges, 0)


def outer_kernel(margin, cells_hbm, _, out, cells, weights, sems):
    copy = fetch(cells_hbm, outer_slot(cells_hbm, margin), cells, sems, [(0, margin)])
    fill_weights(weights)

    @pl.loop(0, margin // PAIR)
    def _(step):
        i = step * PAIR
        for n in range(PAIR):
            copy(i + n).wait()

        def put(n, f, row, value):
            out[i + n, f, row : row + ROWS, :] = value

        update(cells, i, PAIR, weights, put)


def cost(patches, side):
    return pl.CostEstimate(
        flops=patches * side * side * 800,
        bytes_accessed=patches * side * side * 28,
        transcendentals=patches * side * side,
    )


def room(mebibytes):
    return pltpu.CompilerParams(vmem_limit_bytes=mebibytes << 20)


def outer_edges(old_cells, margin):
    side = old_cells.shape[3]
    return pl.pallas_call(
        functools.partial(outer_edges_kernel, margin),
        in_specs=[HBM],
        out_specs=VMEM,
        out_shape=jax.ShapeDtypeStruct((16 * margin, side), jnp.float32),
        scratch_shapes=[
            pltpu.VMEM((margin, 4, side, side), jnp.float32),
            pltpu.VMEM((side, side), jnp.float32),
            pltpu.SemaphoreType.DMA((margin,)),
        ],
        compiler_params=room(48),
        name="outer_edges",
    )(old_cells)


def outer_patches(old_cells, before, margin):
    side = old_cells.shape[3]
    return pl.pallas_call(
        functools.partial(outer_kernel, margin),
        in_specs=[HBM, HBM],
        out_specs=VMEM,
        out_shape=jax.ShapeDtypeStruct((margin, 3, side, side), jnp.float32),
        scratch_shapes=[
            pltpu.VMEM((margin, 4, side, side), jnp.float32),
            pltpu.VMEM((2 * side, 6 * side), jnp.bfloat16),
            pltpu.SemaphoreType.DMA((margin,)),
        ],
        cost_estimate=cost(margin, side),
        compiler_params=room(48),
        name="outer",
    )(old_cells, before)


def layout(margin, per_device):
    home = 16 * margin
    limit = home + 16 * per_device
    brought = limit + 8
    return home, limit, brought, brought + 16 * margin


def home_kernel(margin, range_ref, cells_hbm, came, shared, inner, own, cells, columns, weights, sems):
    side = columns.shape[0]
    count = own.shape[0]
    home, limit, brought, total = layout(margin, count)
    _, odd = position()
    inner_at = (1 - odd) * count
    home_at = odd * margin
    parts = [(inner_at, margin), (home_at, count)]
    copy = fetch(cells_hbm, (1 - odd) * margin, cells, sems, parts)
    fill_weights(weights)

    for at, many, out, row in ((inner_at, margin, inner, 0), (home_at, count, own, home)):

        @pl.loop(0, many // PAIR)
        def _(step, at=at, out=out):
            i = step * PAIR
            for n in range(PAIR):
                copy(at + i + n).wait()

            def put(n, f, row, value):
                out[i + n, f, row : row + ROWS, :] = value

            gather_columns([loader(cells, at + i + n) for n in range(PAIR)], columns, 8 * i, side)
            update(cells, at + i, PAIR, weights, put)

        take_edges(many, cells, lambda p, at=at: at + p, columns, shared, row)

    outer_limit = jnp.where(odd == 1, range_ref[0, 1], range_ref[0, 0])
    shared[limit : limit + 8, :] = jnp.full((8, side), outer_limit, jnp.int32).astype(jnp.float32)
    shared[brought:total, :] = came[0 : total - brought, :]


def home_patches(old_range, old_cells, came, margin, per_device):
    side = old_cells.shape[3]
    total = layout(margin, per_device)[-1]
    return pl.pallas_call(
        functools.partial(home_kernel, margin),
        in_specs=[SMEM, HBM, VMEM],
        out_specs=[VMEM] * 3,
        out_shape=[
            jax.ShapeDtypeStruct((total, side), jnp.float32),
            jax.ShapeDtypeStruct((margin, 3, side, side), jnp.float32),
            jax.ShapeDtypeStruct((per_device, 3, side, side), jnp.float32),
        ],
        scratch_shapes=[
            pltpu.VMEM((margin + per_device, 4, side, side), jnp.float32),
            pltpu.VMEM((side, side), jnp.float32),
            pltpu.VMEM((2 * side, 6 * side), jnp.bfloat16),
            pltpu.SemaphoreType.DMA((margin + per_device,)),
        ],
        cost_estimate=cost(margin + per_device, side),
        compiler_params=room(48),
        name="home",
    )(old_range, old_cells, came)


def answer_kernel(margin, count, range_ref, rows_ref, mine, theirs, edges, message):
    side = edges.shape[1]
    home, limit, brought, _ = layout(margin, count)
    inner = 0
    me, odd = position()
    start, stop = range_ref[0, 0], range_ref[0, 1]
    even = odd == 0
    at_me = pl.multiple_of(16 * count * odd, 16)
    at_them = pl.multiple_of(16 * count * (1 - odd), 16)
    edges[pl.ds(at_me, 16 * count), :] = mine[home : home + 16 * count, :]
    edges[pl.ds(at_them, 16 * count), :] = theirs[home : home + 16 * count, :]
    their_limit = theirs[limit : limit + 8, :]
    low, high = 0, count - margin
    for m in range(margin):
        l = jnp.where(even, high, low) + m
        g = me * count + l
        taken = jnp.where(even, g >= stop, g < start)
        to = pl.multiple_of(at_me + 16 * l, 16)
        from_pair = theirs[inner + 16 * m : inner + 16 * (m + 1), :]
        edges[pl.ds(to, 16), :] = jnp.where(taken, from_pair, edges[pl.ds(to, 16), :])
        l = jnp.where(even, low, high) + m
        g = (me + 1 - 2 * odd) * count + l
        taken = jnp.where(even, g < stop, g >= start)
        to = pl.multiple_of(at_them + 16 * l, 16)
        from_pair = mine[inner + 16 * m : inner + 16 * (m + 1), :]
        edges[pl.ds(to, 16), :] = jnp.where(taken, from_pair, edges[pl.ds(to, 16), :])
        l = jnp.where(even, low, high) + m
        g = me * count + l
        taken = jnp.where(even, g < start, g >= stop)
        to = pl.multiple_of(at_me + 16 * l, 16)
        crossed = mine[brought + 16 * m : brought + 16 * (m + 1), :]
        edges[pl.ds(to, 16), :] = jnp.where(taken, crossed, edges[pl.ds(to, 16), :])
        l = jnp.where(even, high, low) + m
        g = ((me + 1 - 2 * odd) * count + l).astype(jnp.float32)
        to = pl.multiple_of(at_them + 16 * l, 16)
        taken = jnp.where(even, g - their_limit, their_limit - g - 1.0) >= 0.0
        for half in range(2):
            crossed = theirs[brought + 16 * m + 8 * half : brought + 16 * m + 8 * half + 8, :]
            at = pl.multiple_of(to + 8 * half, 8)
            edges[pl.ds(at, 8), :] = jnp.where(taken, crossed, edges[pl.ds(at, 8), :])
    for k in range(3):
        asked = range(k * CAP, (k + 1) * CAP)
        values = [edges[pl.ds(rows_ref[n], 4, stride=2), :] for n in asked]
        for n, value in zip(asked, values):
            message[pl.ds(8 * (n // 2) + n % 2, 4, stride=2), :] = value


def answers(old_range, rows, mine, theirs, margin, per_device):
    side = mine.shape[1]
    return pl.pallas_call(
        functools.partial(answer_kernel, margin, per_device),
        in_specs=[SMEM, SMEM, VMEM, VMEM],
        out_specs=[VMEM, VMEM],
        out_shape=[
            jax.ShapeDtypeStruct((32 * per_device, side), jnp.float32),
            jax.ShapeDtypeStruct((12 * CAP, side), jnp.float32),
        ],
        compiler_params=room(4),
        name="answers",
    )(old_range, rows, mine, theirs)


def rim_terms(rows_ref, edges, crossed, passed, columns, lines, source, ghost, turn, count, odd):
    total = edges.shape[0]
    step = crossed.shape[0]
    source[0:total, :] = edges[...]
    source[total : total + step, :] = crossed[...]
    source[total + step : total + 2 * step, :] = passed[...]
    field = lax.broadcasted_iota(jnp.int32, (4, edges.shape[1]), 0)
    group = 4
    for start in range(0, count, group):
        fetched = []
        for p in range(start, start + group):
            for s in range(4):
                row = rows_ref[4 * p + s]
                wall = row < 0
                value = source[pl.ds(jnp.where(wall, -1 - row, row), 4, stride=2), :]
                value = jnp.where((field == 1 + s // 2) & wall, -value, value)
                fetched.append((16 * p + 8 * (s // 2) + 1 - s % 2, value))
        for target, value in fetched:
            ghost[pl.ds(target, 4, stride=2), :] = value
    turn[...] = jnp.zeros_like(turn)
    lines[...] = jnp.zeros_like(lines)
    for s in range(4):
        parity = 1 - s % 2
        sign = 1.0 - 2.0 * parity
        axis = s // 2
        normal, across = (1, 2) if axis == 0 else (2, 1)

        def both(f):
            row = 8 * axis + 2 * f + parity
            own = source[pl.ds(16 * count * odd + row, count, stride=16), :]
            return own, ghost[pl.ds(row, count, stride=16), :]

        hc, hg = both(0)
        nc, ng = both(normal)
        ac, ag = both(across)
        bc, bg = both(3)
        rc, rg = lax.rsqrt(hc), lax.rsqrt(hg)
        uc, ug = nc * rc * rc, ng * rg * rg
        top = jnp.maximum(jnp.abs(uc) + hc * rc, jnp.abs(ug) + hg * rg)
        fc, fg = nc * uc + 0.5 * hc * hc, ng * ug + 0.5 * hg * hg
        c_h = -HALF * (sign * (nc + ng) - top * ((hg + bg) - (hc + bc)))
        c_n = -HALF * (sign * (fc + fg + hc * bg) - top * (ng - nc))
        c_t = -HALF * (sign * (ac * uc + ag * ug) - top * (ag - ac))
        for f, value in ((0, c_h), (normal, c_n), (across, c_t)):
            target = turn if axis == 0 else lines
            target[pl.ds(2 * f + parity, count, stride=8), :] = value
    turn[...] = jnp.transpose(turn[...])
    side = turn.shape[0]
    columns[...] = pieces(jnp.concatenate([turn[spread(j, side), :] for j in range(side // ROWS)], axis=0))


def fill_places(places):
    side = places.shape[0] // 2
    row = lax.broadcasted_iota(jnp.int32, (side, side), 0) % 8
    lane = lax.broadcasted_iota(jnp.int32, (side, side), 1)
    source = row - jnp.where(lane == 0, 1, jnp.where(lane == side - 1, 0, 1024))
    for f in range(3):
        block = jnp.where(source == 2 * f, 1.0, 0.0).astype(jnp.bfloat16)
        for half in range(2):
            places[half * side : (half + 1) * side, f * side : (f + 1) * side] = block


def final_kernel(
    margin, range_ref, rows_ref, edges, crossed, passed, own, theirs, arrived, out,
    result, source, ghost, turn, columns, lines, places, sems,
):
    count, side = own.shape[0], lines.shape[1]
    me, odd = position()
    even = odd == 0
    fill_places(places)
    rim_terms(rows_ref, edges, crossed, passed, columns, lines, source, ghost, turn, count, odd)
    start, stop = range_ref[0, 0], range_ref[0, 1]
    line = iota(0, side)
    lane = lax.broadcasted_iota(jnp.int32, (side, 2 * side), 1) % side
    steps = side // ROWS

    def copy(p):
        return pltpu.make_async_copy(result.at[p], out.at[p], sems.at[p])

    for group in range(0, count, margin):
        patches = range(group, group + margin)
        held = columns[...]
        masked = [held * jnp.where(lane // 8 == p, 1.0, 0.0).astype(jnp.bfloat16) for p in patches]
        terms = product(jnp.concatenate(masked, axis=0), places[...])
        for m, p in enumerate(patches):
            if group == 0:
                taken = me * count + p < start
            elif group == count - margin:
                taken = me * count + p >= stop
            else:
                taken = None
            near = even if group else odd == 1
            for f in range(3):
                for j in range(steps):
                    rows = slice(ROWS * j, ROWS * (j + 1))
                    value = own[p, f, rows, :]
                    if taken is not None:
                        moved = jnp.where(near, theirs[m, f, rows, :], arrived[m, f, rows, :])
                        value = jnp.where(taken, moved, value)
                    at = side * m + ROWS * j
                    value = value + terms[at : at + ROWS, f * side : (f + 1) * side]
                    if j == 0:
                        south = lines[8 * p + 2 * f + 1 : 8 * p + 2 * f + 2, :]
                        value = value + jnp.where(line == 0, south, 0.0)
                    if j == steps - 1:
                        north = lines[8 * p + 2 * f : 8 * p + 2 * f + 1, :]
                        value = value + jnp.where(line == ROWS - 1, north, 0.0)
                    result[p, f, spread(j, side), :] = value
            copy(p).start()
    for p in range(count):
        copy(p).wait()


def finished(old_range, rows, edges, crossed, passed, own, theirs, arrived, margin):
    count, _, side, _ = own.shape
    return pl.pallas_call(
        functools.partial(final_kernel, margin),
        in_specs=[SMEM, SMEM] + [VMEM] * 6,
        out_specs=HBM,
        out_shape=jax.ShapeDtypeStruct(own.shape, jnp.float32),
        scratch_shapes=[
            pltpu.VMEM(own.shape, jnp.float32),
            pltpu.VMEM((edges.shape[0] + 2 * crossed.shape[0], side), jnp.float32),
            pltpu.VMEM((16 * count, side), jnp.float32),
            pltpu.VMEM((side, side), jnp.float32),
            pltpu.VMEM((side, 2 * side), jnp.bfloat16),
            pltpu.VMEM((side, side), jnp.float32),
            pltpu.VMEM((2 * side, 3 * side), jnp.bfloat16),
            pltpu.SemaphoreType.DMA((count,)),
        ],
        compiler_params=room(12),
        name="final",
    )(old_range, rows, edges, crossed, passed, own, theirs, arrived)


def swapped(value, first):
    pairs = [(i, i + 1) for i in range(first, lax.axis_size(AXES) - 1, 2)]
    return lax.ppermute(value, AXES, pairs + [(j, i) for i, j in pairs])


def ranks(named):
    size = named.shape[-1]
    earlier = jnp.arange(size)[:, None] < jnp.arange(size)[None, :]
    return jnp.sum(jnp.where(named[..., :, None] & earlier, 1, 0), axis=-2)


def local(old_cells, old_range, neighbours):
    per_device = neighbours.shape[0]
    side = old_cells.shape[3]
    margin = (old_cells.shape[0] - per_device) // 2
    entries = 4 * per_device
    me, odd = position()

    their_table = swapped(neighbours, 0)
    leaving_edges = outer_edges(old_cells, margin)

    tables = jnp.where(
        odd == 0,
        jnp.concatenate([neighbours.reshape(1, -1), their_table.reshape(1, -1)], axis=1),
        jnp.concatenate([their_table.reshape(1, -1), neighbours.reshape(1, -1)], axis=1),
    ).astype(jnp.float32)
    tables = jnp.pad(tables, ((0, 7), (0, side - 2 * entries)))
    bundle = jnp.concatenate([leaving_edges, tables], axis=0)
    came = swapped(bundle, 1)

    arrived = swapped(outer_patches(old_cells, bundle, margin), 1)

    shared, inner, own = home_patches(old_range, old_cells, came, margin, per_device)
    their_edges = swapped(shared, 0)
    theirs = swapped(inner, 0)

    entry = jnp.arange(entries, dtype=jnp.int32)
    entry_side = entry % 4
    at_side = 8 * (entry_side // 2) + entry_side % 2
    asked_by = came[16 * margin, : 2 * entries].astype(jnp.int32).reshape(2, entries)
    middle = jnp.where(odd == 0, asked_by[1], asked_by[0])
    listed = jnp.stack([asked_by[0], middle, asked_by[1]])
    owners = me + jnp.where(odd == 0, jnp.array([0, 0, 1], jnp.int32), jnp.array([-1, 0, 0], jnp.int32))
    asked = (listed >= 0) & (listed // per_device == owners[:, None])
    rows = 16 * (listed - 2 * per_device * (me // 2)) + at_side
    chosen = asked[:, None, :] & (ranks(asked)[:, None, :] == jnp.arange(CAP)[None, :, None])
    send_rows = jnp.sum(jnp.where(chosen, rows[:, None, :], 0), axis=2).reshape(-1)

    edges, message = answers(old_range, send_rows, shared, their_edges, margin, per_device)
    crossed = swapped(message, 1)
    passed = swapped(crossed, 0)

    listed = neighbours.reshape(-1)
    owner = listed // per_device
    mine, total, step = 32 * per_device, 16 * per_device, 12 * CAP
    lists = jnp.where(
        odd == 0,
        jnp.array([[-2, mine], [-1, mine + 4 * CAP], [2, mine + step]], jnp.int32),
        jnp.array([[-2, mine + step + 8 * CAP], [1, mine + 4 * CAP], [2, mine + 8 * CAP]], jnp.int32),
    )
    named = (listed >= 0) & (owner - me == lists[:, :1])
    place = ranks(named)
    across = jnp.sum(jnp.where(named, lists[:, 1:] + 8 * (place // 2) + place % 2, 0), axis=0)
    within = 16 * (listed - 2 * per_device * (me // 2)) + at_side
    wall = total * odd + 16 * (entry // 4) + 8 * (entry_side // 2) + 1 - entry_side % 2
    ghost_rows = jnp.where(listed < 0, -1 - wall, jnp.where(owner // 2 == me // 2, within, across))

    return finished(old_range, ghost_rows, edges, crossed, passed, own, theirs, arrived, margin)


def solution(mesh):
    placed = (
        P(("member", "curve", "sub"), None, None, None),
        P(("member", "curve", "sub"), None),
        P(("member", "curve", "sub"), None),
    )
    return jax.shard_map(
        local,
        mesh=mesh,
        in_specs=placed,
        out_specs=P(("member", "curve", "sub"), None, None, None),
        check_vma=False,
    )
```

```python
import functools

import jax
import jax.numpy as jnp
from jax import lax
from jax.experimental import pallas as pl
from jax.experimental.pallas import tpu as pltpu
from jax.sharding import PartitionSpec as P

RATE_STEP = 0.1
HALF = 0.5 * RATE_STEP
AXES = ("curve", "sub")
CAP = 8
ROWS = 8
PAIR = 2
VMEM = pl.BlockSpec(memory_space=pltpu.VMEM)
SMEM = pl.BlockSpec(memory_space=pltpu.SMEM)
HBM = pl.BlockSpec(memory_space=pltpu.HBM)


def position():
    me = lax.axis_index(AXES)
    return me, lax.rem(me, 2)


def iota(axis, side):
    return lax.broadcasted_iota(jnp.int32, (ROWS, side), axis)


def spread(j, side):
    return pl.ds(j, ROWS, stride=side // ROWS)


def pieces(x):
    high = x.astype(jnp.bfloat16)
    low = (x - high.astype(jnp.float32)).astype(jnp.bfloat16)
    return jnp.concatenate([high, low], axis=1)


def product(parts, weights):
    return jnp.dot(parts, weights, preferred_element_type=jnp.float32)


AHEAD, EAST, SUMS, SLOPE = slice(0, 2), slice(2, 4), slice(4, 5), slice(5, 6)


def fill_weights(weights):
    side = weights.shape[0] // 2
    row = lax.broadcasted_iota(jnp.int32, (side, side), 0)
    lane = lax.broadcasted_iota(jnp.int32, (side, side), 1)
    one = lambda where: jnp.where(where, 1.0, 0.0)
    after, here, before = one(row == lane + 1), one(row == lane), one(row == lane - 1)
    inner_e, inner_w = lane != side - 1, lane != 0
    east = jnp.where(inner_e, after + here, 0.0)
    west = jnp.where(inner_w, here + before, 0.0)
    blocks = (
        after,
        before,
        jnp.where(inner_e, after - here, 0.0),
        jnp.where(inner_w, here - before, 0.0),
        east - west,
        after - before,
    )
    for n, block in enumerate(blocks):
        for half in range(2):
            weights[half * side : (half + 1) * side, n * side : (n + 1) * side] = block.astype(jnp.bfloat16)


def inner_update(loads, store, side, weights):
    line = iota(0, side)
    first, last = line == 0, line == ROWS - 1
    steps = side // ROWS
    many = len(loads)

    def cell(h, mx, my, bed):
        root = lax.rsqrt(h)
        celerity = h * root
        inverse = root * root
        u = mx * inverse
        v = my * inverse
        half_sq = 0.5 * h * h
        cross = my * u
        rate_y = jnp.abs(v) + celerity
        rate_x = jnp.abs(u) + celerity
        return (rate_y, h + bed, mx, my, cross, my * v + half_sq, bed), rate_x, mx * u + half_sq, h

    def face_y(low, high):
        top = jnp.maximum(low[0], high[0])
        return [
            (high[3] + low[3]) - top * (high[1] - low[1]),
            (high[4] + low[4]) - top * (high[2] - low[2]),
            (high[5] + low[5]) - top * (high[3] - low[3]),
        ]

    def taken(block):
        return weights[:, block.start * side : block.stop * side]

    cells = [cell(*[load(f, j) for f in range(4)]) for load in loads for j in range(steps)]
    stack = lambda pick: pieces(jnp.concatenate([pick(c) for c in cells], axis=0))
    eta, mx, my, cross, bed = (stack(lambda c, n=n: c[0][n]) for n in (1, 2, 3, 4, 6))
    fx = stack(lambda c: c[2])
    rates = product(stack(lambda c: c[1]), taken(AHEAD))
    jumps = product(jnp.concatenate([eta, mx, my], axis=0), taken(EAST))
    sums = product(jnp.concatenate([mx, fx, cross], axis=0), taken(SUMS))
    slopes = product(bed, taken(SLOPE))
    for n in range(many):
        mine = cells[n * steps : (n + 1) * steps]
        low = [pltpu.roll(each, 1, 0) for each in mine[steps - 1][0]]
        faces = []
        for j in range(steps):
            faces.append(face_y(low, mine[j][0]))
            low = mine[j][0]
        faces[0] = [jnp.where(first, 0.0, each) for each in faces[0]]
        beds = [c[0][6] for c in mine]
        under = jnp.where(first, 0.0, pltpu.roll(beds[-1], 1, 0))
        over = jnp.where(last, 0.0, pltpu.roll(beds[0], ROWS - 1, 0))
        faces.append([jnp.where(last, 0.0, pltpu.roll(each, ROWS - 1, 0)) for each in faces[0]])
        for j in range(steps):
            (_, _, mx, my, _, _, _), rate, _, h = mine[j]
            at = [(q * many + n) * side + ROWS * j for q in range(3)]
            rows = [slice(r, r + ROWS) for r in at]
            top_e = jnp.maximum(rate, rates[rows[0], :side])
            top_w = jnp.maximum(rate, rates[rows[0], side:])
            x = [sums[r] - (top_e * jumps[r, :side] - top_w * jumps[r, side:]) for r in rows]
            south, north = faces[j], faces[j + 1]
            slope_y = (beds[j + 1] if j + 1 < steps else over) - (beds[j - 1] if j else under)
            store(n, 0, j, h - HALF * (x[0] + (north[0] - south[0])))
            store(n, 1, j, mx - HALF * (x[1] + h * slopes[rows[0]] + (north[1] - south[1])))
            store(n, 2, j, my - HALF * (x[2] + h * slope_y + (north[2] - south[2])))


def gather_columns(loads, columns, first_at, side):
    pair = iota(1, side) // 2
    for j in range(side // ROWS):
        held = columns[spread(j, side), :]
        for n, load in enumerate(loads):
            at = first_at + 8 * n
            for f in range(4):
                held = jnp.where(pair == at // 2 + f, pltpu.roll(load(f, j), at + 2 * f + 1, 1), held)
        columns[spread(j, side), :] = held


def take_edges(count, cells, slot_of, columns, edges, base):
    side = columns.shape[0]
    turned = jnp.transpose(columns[...])
    for p in range(count):
        edges[base + 16 * p : base + 16 * p + 8, :] = turned[8 * p : 8 * p + 8, :]
        for f in range(4):
            row = base + 16 * p + 8 + 2 * f
            edges[row : row + 1, :] = cells[slot_of(p), f, side - 1 : side, :]
            edges[row + 1 : row + 2, :] = cells[slot_of(p), f, 0:1, :]


def loader(cells, i):
    side = cells.shape[3]
    return lambda f, j: cells[i, f, spread(j, side), :]


def update(cells, first, many, weights, put):
    loads = [loader(cells, first + n) for n in range(many)]
    inner_update(loads, lambda n, f, j, value: put(n, f, ROWS * j, value), cells.shape[3], weights)


def fetch(cells_hbm, first, cells, sems, parts):
    def copy(i):
        return pltpu.make_async_copy(cells_hbm.at[first + i], cells.at[i], sems.at[i])

    for start, count in parts:
        for i in range(count):
            copy(start + i).start()
    return copy


def outer_slot(cells_hbm, margin):
    _, odd = position()
    return odd * (cells_hbm.shape[0] - margin)


def outer_kernel(margin, cells_hbm, out, edges, cells, columns, weights, sems):
    side = columns.shape[0]
    copy = fetch(cells_hbm, outer_slot(cells_hbm, margin), cells, sems, [(0, margin)])
    fill_weights(weights)

    @pl.loop(0, margin // PAIR)
    def _(step):
        i = step * PAIR
        for n in range(PAIR):
            copy(i + n).wait()

        def put(n, f, row, value):
            out[i + n, f, row : row + ROWS, :] = value

        gather_columns([loader(cells, i + n) for n in range(PAIR)], columns, 8 * i, side)
        update(cells, i, PAIR, weights, put)

    take_edges(margin, cells, lambda p: p, columns, edges, 0)


def cost(patches, side):
    return pl.CostEstimate(
        flops=patches * side * side * 800,
        bytes_accessed=patches * side * side * 28,
        transcendentals=patches * side * side,
    )


def room(mebibytes):
    return pltpu.CompilerParams(vmem_limit_bytes=mebibytes << 20)


def outer_patches(old_cells, margin):
    side = old_cells.shape[3]
    return pl.pallas_call(
        functools.partial(outer_kernel, margin),
        in_specs=[HBM],
        out_specs=[VMEM, VMEM],
        out_shape=[
            jax.ShapeDtypeStruct((margin, 3, side, side), jnp.float32),
            jax.ShapeDtypeStruct((16 * margin, side), jnp.float32),
        ],
        scratch_shapes=[
            pltpu.VMEM((margin, 4, side, side), jnp.float32),
            pltpu.VMEM((side, side), jnp.float32),
            pltpu.VMEM((2 * side, 6 * side), jnp.bfloat16),
            pltpu.SemaphoreType.DMA((margin,)),
        ],
        cost_estimate=cost(margin, side),
        compiler_params=room(48),
        name="outer",
    )(old_cells)


def after(value, other):
    any_place = pl.BlockSpec(memory_space=pl.ANY)
    return pl.pallas_call(
        lambda value_ref, other_ref, out_ref: None,
        in_specs=[any_place, any_place],
        out_specs=any_place,
        out_shape=jax.ShapeDtypeStruct(value.shape, value.dtype),
        input_output_aliases={0: 0},
        compiler_params=room(4),
        name="after",
    )(value, other)


def layout(margin, per_device):
    home = 16 * margin
    limit = home + 16 * per_device
    brought = limit + 8
    return home, limit, brought, brought + 16 * margin


def home_kernel(margin, range_ref, cells_hbm, came, shared, inner, own, cells, columns, weights, sems):
    side = columns.shape[0]
    count = own.shape[0]
    home, limit, brought, total = layout(margin, count)
    _, odd = position()
    inner_at = (1 - odd) * count
    home_at = odd * margin
    parts = [(inner_at, margin), (home_at, count)]
    copy = fetch(cells_hbm, (1 - odd) * margin, cells, sems, parts)
    fill_weights(weights)

    for at, many, out, row in ((inner_at, margin, inner, 0), (home_at, count, own, home)):

        @pl.loop(0, many // PAIR)
        def _(step, at=at, out=out):
            i = step * PAIR
            for n in range(PAIR):
                copy(at + i + n).wait()

            def put(n, f, row, value):
                out[i + n, f, row : row + ROWS, :] = value

            gather_columns([loader(cells, at + i + n) for n in range(PAIR)], columns, 8 * i, side)
            update(cells, at + i, PAIR, weights, put)

        take_edges(many, cells, lambda p, at=at: at + p, columns, shared, row)

    outer_limit = jnp.where(odd == 1, range_ref[0, 1], range_ref[0, 0])
    shared[limit : limit + 8, :] = jnp.full((8, side), outer_limit, jnp.int32).astype(jnp.float32)
    shared[brought:total, :] = came[0 : total - brought, :]


def home_patches(old_range, old_cells, came, margin, per_device):
    side = old_cells.shape[3]
    total = layout(margin, per_device)[-1]
    return pl.pallas_call(
        functools.partial(home_kernel, margin),
        in_specs=[SMEM, HBM, VMEM],
        out_specs=[VMEM] * 3,
        out_shape=[
            jax.ShapeDtypeStruct((total, side), jnp.float32),
            jax.ShapeDtypeStruct((margin, 3, side, side), jnp.float32),
            jax.ShapeDtypeStruct((per_device, 3, side, side), jnp.float32),
        ],
        scratch_shapes=[
            pltpu.VMEM((margin + per_device, 4, side, side), jnp.float32),
            pltpu.VMEM((side, side), jnp.float32),
            pltpu.VMEM((2 * side, 6 * side), jnp.bfloat16),
            pltpu.SemaphoreType.DMA((margin + per_device,)),
        ],
        cost_estimate=cost(margin + per_device, side),
        compiler_params=room(48),
        name="home",
    )(old_range, old_cells, came)


def answer_kernel(margin, count, range_ref, rows_ref, mine, theirs, edges, message):
    side = edges.shape[1]
    home, limit, brought, _ = layout(margin, count)
    inner = 0
    me, odd = position()
    start, stop = range_ref[0, 0], range_ref[0, 1]
    even = odd == 0
    at_me = pl.multiple_of(16 * count * odd, 16)
    at_them = pl.multiple_of(16 * count * (1 - odd), 16)
    edges[pl.ds(at_me, 16 * count), :] = mine[home : home + 16 * count, :]
    edges[pl.ds(at_them, 16 * count), :] = theirs[home : home + 16 * count, :]
    their_limit = theirs[limit : limit + 8, :]
    low, high = 0, count - margin
    for m in range(margin):
        l = jnp.where(even, high, low) + m
        g = me * count + l
        taken = jnp.where(even, g >= stop, g < start)
        to = pl.multiple_of(at_me + 16 * l, 16)
        from_pair = theirs[inner + 16 * m : inner + 16 * (m + 1), :]
        edges[pl.ds(to, 16), :] = jnp.where(taken, from_pair, edges[pl.ds(to, 16), :])
        l = jnp.where(even, low, high) + m
        g = (me + 1 - 2 * odd) * count + l
        taken = jnp.where(even, g < stop, g >= start)
        to = pl.multiple_of(at_them + 16 * l, 16)
        from_pair = mine[inner + 16 * m : inner + 16 * (m + 1), :]
        edges[pl.ds(to, 16), :] = jnp.where(taken, from_pair, edges[pl.ds(to, 16), :])
        l = jnp.where(even, low, high) + m
        g = me * count + l
        taken = jnp.where(even, g < start, g >= stop)
        to = pl.multiple_of(at_me + 16 * l, 16)
        crossed = mine[brought + 16 * m : brought + 16 * (m + 1), :]
        edges[pl.ds(to, 16), :] = jnp.where(taken, crossed, edges[pl.ds(to, 16), :])
        l = jnp.where(even, high, low) + m
        g = ((me + 1 - 2 * odd) * count + l).astype(jnp.float32)
        to = pl.multiple_of(at_them + 16 * l, 16)
        taken = jnp.where(even, g - their_limit, their_limit - g - 1.0) >= 0.0
        for half in range(2):
            crossed = theirs[brought + 16 * m + 8 * half : brought + 16 * m + 8 * half + 8, :]
            at = pl.multiple_of(to + 8 * half, 8)
            edges[pl.ds(at, 8), :] = jnp.where(taken, crossed, edges[pl.ds(at, 8), :])
    for k in range(3):
        asked = range(k * CAP, (k + 1) * CAP)
        values = [edges[pl.ds(rows_ref[n], 4, stride=2), :] for n in asked]
        for n, value in zip(asked, values):
            message[pl.ds(8 * (n // 2) + n % 2, 4, stride=2), :] = value


def answers(old_range, rows, mine, theirs, margin, per_device):
    side = mine.shape[1]
    return pl.pallas_call(
        functools.partial(answer_kernel, margin, per_device),
        in_specs=[SMEM, SMEM, VMEM, VMEM],
        out_specs=[VMEM, VMEM],
        out_shape=[
            jax.ShapeDtypeStruct((32 * per_device, side), jnp.float32),
            jax.ShapeDtypeStruct((12 * CAP, side), jnp.float32),
        ],
        compiler_params=room(4),
        name="answers",
    )(old_range, rows, mine, theirs)


def rim_terms(rows_ref, edges, crossed, passed, columns, lines, source, ghost, turn, count, odd):
    total = edges.shape[0]
    step = crossed.shape[0]
    source[0:total, :] = edges[...]
    source[total : total + step, :] = crossed[...]
    source[total + step : total + 2 * step, :] = passed[...]
    field = lax.broadcasted_iota(jnp.int32, (4, edges.shape[1]), 0)
    group = 4
    for start in range(0, count, group):
        fetched = []
        for p in range(start, start + group):
            for s in range(4):
                row = rows_ref[4 * p + s]
                wall = row < 0
                value = source[pl.ds(jnp.where(wall, -1 - row, row), 4, stride=2), :]
                value = jnp.where((field == 1 + s // 2) & wall, -value, value)
                fetched.append((16 * p + 8 * (s // 2) + 1 - s % 2, value))
        for target, value in fetched:
            ghost[pl.ds(target, 4, stride=2), :] = value
    turn[...] = jnp.zeros_like(turn)
    lines[...] = jnp.zeros_like(lines)
    for s in range(4):
        parity = 1 - s % 2
        sign = 1.0 - 2.0 * parity
        axis = s // 2
        normal, across = (1, 2) if axis == 0 else (2, 1)

        def both(f):
            row = 8 * axis + 2 * f + parity
            own = source[pl.ds(16 * count * odd + row, count, stride=16), :]
            return own, ghost[pl.ds(row, count, stride=16), :]

        hc, hg = both(0)
        nc, ng = both(normal)
        ac, ag = both(across)
        bc, bg = both(3)
        rc, rg = lax.rsqrt(hc), lax.rsqrt(hg)
        uc, ug = nc * rc * rc, ng * rg * rg
        top = jnp.maximum(jnp.abs(uc) + hc * rc, jnp.abs(ug) + hg * rg)
        fc, fg = nc * uc + 0.5 * hc * hc, ng * ug + 0.5 * hg * hg
        c_h = -HALF * (sign * (nc + ng) - top * ((hg + bg) - (hc + bc)))
        c_n = -HALF * (sign * (fc + fg + hc * bg) - top * (ng - nc))
        c_t = -HALF * (sign * (ac * uc + ag * ug) - top * (ag - ac))
        for f, value in ((0, c_h), (normal, c_n), (across, c_t)):
            target = turn if axis == 0 else lines
            target[pl.ds(2 * f + parity, count, stride=8), :] = value
    turn[...] = jnp.transpose(turn[...])
    side = turn.shape[0]
    columns[...] = pieces(jnp.concatenate([turn[spread(j, side), :] for j in range(side // ROWS)], axis=0))


def fill_places(places):
    side = places.shape[0] // 2
    row = lax.broadcasted_iota(jnp.int32, (side, side), 0) % 8
    lane = lax.broadcasted_iota(jnp.int32, (side, side), 1)
    source = row - jnp.where(lane == 0, 1, jnp.where(lane == side - 1, 0, 1024))
    for f in range(3):
        block = jnp.where(source == 2 * f, 1.0, 0.0).astype(jnp.bfloat16)
        for half in range(2):
            places[half * side : (half + 1) * side, f * side : (f + 1) * side] = block


def final_kernel(
    margin, range_ref, rows_ref, edges, crossed, passed, own, theirs, arrived, out,
    result, source, ghost, turn, columns, lines, places, sems,
):
    count, side = own.shape[0], lines.shape[1]
    me, odd = position()
    even = odd == 0
    fill_places(places)
    rim_terms(rows_ref, edges, crossed, passed, columns, lines, source, ghost, turn, count, odd)
    start, stop = range_ref[0, 0], range_ref[0, 1]
    line = iota(0, side)
    lane = lax.broadcasted_iota(jnp.int32, (side, 2 * side), 1) % side
    steps = side // ROWS

    def copy(p):
        return pltpu.make_async_copy(result.at[p], out.at[p], sems.at[p])

    for group in range(0, count, margin):
        patches = range(group, group + margin)
        held = columns[...]
        masked = [held * jnp.where(lane // 8 == p, 1.0, 0.0).astype(jnp.bfloat16) for p in patches]
        terms = product(jnp.concatenate(masked, axis=0), places[...])
        for m, p in enumerate(patches):
            if group == 0:
                taken = me * count + p < start
            elif group == count - margin:
                taken = me * count + p >= stop
            else:
                taken = None
            near = even if group else odd == 1
            for f in range(3):
                for j in range(steps):
                    rows = slice(ROWS * j, ROWS * (j + 1))
                    value = own[p, f, rows, :]
                    if taken is not None:
                        moved = jnp.where(near, theirs[m, f, rows, :], arrived[m, f, rows, :])
                        value = jnp.where(taken, moved, value)
                    at = side * m + ROWS * j
                    value = value + terms[at : at + ROWS, f * side : (f + 1) * side]
                    if j == 0:
                        south = lines[8 * p + 2 * f + 1 : 8 * p + 2 * f + 2, :]
                        value = value + jnp.where(line == 0, south, 0.0)
                    if j == steps - 1:
                        north = lines[8 * p + 2 * f : 8 * p + 2 * f + 1, :]
                        value = value + jnp.where(line == ROWS - 1, north, 0.0)
                    result[p, f, spread(j, side), :] = value
            copy(p).start()
    for p in range(count):
        copy(p).wait()


def finished(old_range, rows, edges, crossed, passed, own, theirs, arrived, margin):
    count, _, side, _ = own.shape
    return pl.pallas_call(
        functools.partial(final_kernel, margin),
        in_specs=[SMEM, SMEM] + [VMEM] * 6,
        out_specs=HBM,
        out_shape=jax.ShapeDtypeStruct(own.shape, jnp.float32),
        scratch_shapes=[
            pltpu.VMEM(own.shape, jnp.float32),
            pltpu.VMEM((edges.shape[0] + 2 * crossed.shape[0], side), jnp.float32),
            pltpu.VMEM((16 * count, side), jnp.float32),
            pltpu.VMEM((side, side), jnp.float32),
            pltpu.VMEM((side, 2 * side), jnp.bfloat16),
            pltpu.VMEM((side, side), jnp.float32),
            pltpu.VMEM((2 * side, 3 * side), jnp.bfloat16),
            pltpu.SemaphoreType.DMA((count,)),
        ],
        compiler_params=room(12),
        name="final",
    )(old_range, rows, edges, crossed, passed, own, theirs, arrived)


def swapped(value, first):
    pairs = [(i, i + 1) for i in range(first, lax.axis_size(AXES) - 1, 2)]
    return lax.ppermute(value, AXES, pairs + [(j, i) for i, j in pairs])


def ranks(named):
    size = named.shape[-1]
    earlier = jnp.arange(size)[:, None] < jnp.arange(size)[None, :]
    return jnp.sum(jnp.where(named[..., :, None] & earlier, 1, 0), axis=-2)


def local(old_cells, old_range, neighbours):
    per_device = neighbours.shape[0]
    side = old_cells.shape[3]
    margin = (old_cells.shape[0] - per_device) // 2
    entries = 4 * per_device
    me, odd = position()

    their_table = swapped(neighbours, 0)
    leaving, leaving_edges = outer_patches(old_cells, margin)

    tables = jnp.where(
        odd == 0,
        jnp.concatenate([neighbours.reshape(1, -1), their_table.reshape(1, -1)], axis=1),
        jnp.concatenate([their_table.reshape(1, -1), neighbours.reshape(1, -1)], axis=1),
    ).astype(jnp.float32)
    tables = jnp.pad(tables, ((0, 7), (0, side - 2 * entries)))
    bundle = jnp.concatenate([leaving_edges, tables], axis=0)
    came = swapped(bundle, 1)

    arrived = swapped(after(leaving, bundle), 1)

    shared, inner, own = home_patches(old_range, old_cells, came, margin, per_device)
    their_edges = swapped(shared, 0)
    theirs = swapped(inner, 0)

    entry = jnp.arange(entries, dtype=jnp.int32)
    entry_side = entry % 4
    at_side = 8 * (entry_side // 2) + entry_side % 2
    asked_by = came[16 * margin, : 2 * entries].astype(jnp.int32).reshape(2, entries)
    middle = jnp.where(odd == 0, asked_by[1], asked_by[0])
    listed = jnp.stack([asked_by[0], middle, asked_by[1]])
    owners = me + jnp.where(odd == 0, jnp.array([0, 0, 1], jnp.int32), jnp.array([-1, 0, 0], jnp.int32))
    asked = (listed >= 0) & (listed // per_device == owners[:, None])
    rows = 16 * (listed - 2 * per_device * (me // 2)) + at_side
    chosen = asked[:, None, :] & (ranks(asked)[:, None, :] == jnp.arange(CAP)[None, :, None])
    send_rows = jnp.sum(jnp.where(chosen, rows[:, None, :], 0), axis=2).reshape(-1)

    edges, message = answers(old_range, send_rows, shared, their_edges, margin, per_device)
    crossed = swapped(message, 1)
    passed = swapped(crossed, 0)

    listed = neighbours.reshape(-1)
    owner = listed // per_device
    mine, total, step = 32 * per_device, 16 * per_device, 12 * CAP
    lists = jnp.where(
        odd == 0,
        jnp.array([[-2, mine], [-1, mine + 4 * CAP], [2, mine + step]], jnp.int32),
        jnp.array([[-2, mine + step + 8 * CAP], [1, mine + 4 * CAP], [2, mine + 8 * CAP]], jnp.int32),
    )
    named = (listed >= 0) & (owner - me == lists[:, :1])
    place = ranks(named)
    across = jnp.sum(jnp.where(named, lists[:, 1:] + 8 * (place // 2) + place % 2, 0), axis=0)
    within = 16 * (listed - 2 * per_device * (me // 2)) + at_side
    wall = total * odd + 16 * (entry // 4) + 8 * (entry_side // 2) + 1 - entry_side % 2
    ghost_rows = jnp.where(listed < 0, -1 - wall, jnp.where(owner // 2 == me // 2, within, across))

    return finished(old_range, ghost_rows, edges, crossed, passed, own, theirs, arrived, margin)


def solution(mesh):
    placed = (
        P(("member", "curve", "sub"), None, None, None),
        P(("member", "curve", "sub"), None),
        P(("member", "curve", "sub"), None),
    )
    return jax.shard_map(
        local,
        mesh=mesh,
        in_specs=placed,
        out_specs=P(("member", "curve", "sub"), None, None, None),
        check_vma=False,
    )
```

```python
import functools

import jax
import jax.numpy as jnp
from jax import lax
from jax.experimental import pallas as pl
from jax.experimental.pallas import tpu as pltpu
from jax.sharding import PartitionSpec as P

RATE_STEP = 0.1
HALF = 0.5 * RATE_STEP
AXES = ("curve", "sub")
CAP = 8
ROWS = 8
PAIR = 2
VMEM = pl.BlockSpec(memory_space=pltpu.VMEM)
SMEM = pl.BlockSpec(memory_space=pltpu.SMEM)
HBM = pl.BlockSpec(memory_space=pltpu.HBM)


def position():
    me = lax.axis_index(AXES)
    return me, lax.rem(me, 2)


def iota(axis, side):
    return lax.broadcasted_iota(jnp.int32, (ROWS, side), axis)


def spread(j, side):
    return pl.ds(j, ROWS, stride=side // ROWS)


def pieces(x):
    high = x.astype(jnp.bfloat16)
    low = (x - high.astype(jnp.float32)).astype(jnp.bfloat16)
    return jnp.concatenate([high, low], axis=1)


def product(parts, weights):
    return jnp.dot(parts, weights, preferred_element_type=jnp.float32)


AHEAD, EAST, SUMS, SLOPE = slice(0, 2), slice(2, 4), slice(4, 5), slice(5, 6)


def fill_weights(weights):
    side = weights.shape[0] // 2
    row = lax.broadcasted_iota(jnp.int32, (side, side), 0)
    lane = lax.broadcasted_iota(jnp.int32, (side, side), 1)
    one = lambda where: jnp.where(where, 1.0, 0.0)
    after, here, before = one(row == lane + 1), one(row == lane), one(row == lane - 1)
    inner_e, inner_w = lane != side - 1, lane != 0
    east = jnp.where(inner_e, after + here, 0.0)
    west = jnp.where(inner_w, here + before, 0.0)
    blocks = (
        after,
        before,
        jnp.where(inner_e, after - here, 0.0),
        jnp.where(inner_w, here - before, 0.0),
        east - west,
        after - before,
    )
    for n, block in enumerate(blocks):
        for half in range(2):
            weights[half * side : (half + 1) * side, n * side : (n + 1) * side] = block.astype(jnp.bfloat16)


def inner_update(loads, store, side, weights):
    line = iota(0, side)
    first, last = line == 0, line == ROWS - 1
    steps = side // ROWS
    many = len(loads)

    def cell(h, mx, my, bed):
        root = lax.rsqrt(h)
        celerity = h * root
        inverse = root * root
        u = mx * inverse
        v = my * inverse
        half_sq = 0.5 * h * h
        cross = my * u
        rate_y = jnp.abs(v) + celerity
        rate_x = jnp.abs(u) + celerity
        return (rate_y, h + bed, mx, my, cross, my * v + half_sq, bed), rate_x, mx * u + half_sq, h

    def face_y(low, high):
        top = jnp.maximum(low[0], high[0])
        return [
            (high[3] + low[3]) - top * (high[1] - low[1]),
            (high[4] + low[4]) - top * (high[2] - low[2]),
            (high[5] + low[5]) - top * (high[3] - low[3]),
        ]

    def taken(block):
        return weights[:, block.start * side : block.stop * side]

    cells = [cell(*[load(f, j) for f in range(4)]) for load in loads for j in range(steps)]
    stack = lambda pick: pieces(jnp.concatenate([pick(c) for c in cells], axis=0))
    eta, mx, my, cross, bed = (stack(lambda c, n=n: c[0][n]) for n in (1, 2, 3, 4, 6))
    fx = stack(lambda c: c[2])
    rates = product(stack(lambda c: c[1]), taken(AHEAD))
    jumps = product(jnp.concatenate([eta, mx, my], axis=0), taken(EAST))
    sums = product(jnp.concatenate([mx, fx, cross], axis=0), taken(SUMS))
    slopes = product(bed, taken(SLOPE))
    for n in range(many):
        mine = cells[n * steps : (n + 1) * steps]
        low = [pltpu.roll(each, 1, 0) for each in mine[steps - 1][0]]
        faces = []
        for j in range(steps):
            faces.append(face_y(low, mine[j][0]))
            low = mine[j][0]
        faces[0] = [jnp.where(first, 0.0, each) for each in faces[0]]
        beds = [c[0][6] for c in mine]
        under = jnp.where(first, 0.0, pltpu.roll(beds[-1], 1, 0))
        over = jnp.where(last, 0.0, pltpu.roll(beds[0], ROWS - 1, 0))
        faces.append([jnp.where(last, 0.0, pltpu.roll(each, ROWS - 1, 0)) for each in faces[0]])
        for j in range(steps):
            (_, _, mx, my, _, _, _), rate, _, h = mine[j]
            at = [(q * many + n) * side + ROWS * j for q in range(3)]
            rows = [slice(r, r + ROWS) for r in at]
            top_e = jnp.maximum(rate, rates[rows[0], :side])
            top_w = jnp.maximum(rate, rates[rows[0], side:])
            x = [sums[r] - (top_e * jumps[r, :side] - top_w * jumps[r, side:]) for r in rows]
            south, north = faces[j], faces[j + 1]
            slope_y = (beds[j + 1] if j + 1 < steps else over) - (beds[j - 1] if j else under)
            store(n, 0, j, h - HALF * (x[0] + (north[0] - south[0])))
            store(n, 1, j, mx - HALF * (x[1] + h * slopes[rows[0]] + (north[1] - south[1])))
            store(n, 2, j, my - HALF * (x[2] + h * slope_y + (north[2] - south[2])))


def gather_columns(loads, columns, first_at, side):
    pair = iota(1, side) // 2
    for j in range(side // ROWS):
        held = columns[spread(j, side), :]
        for n, load in enumerate(loads):
            at = first_at + 8 * n
            for f in range(4):
                held = jnp.where(pair == at // 2 + f, pltpu.roll(load(f, j), at + 2 * f + 1, 1), held)
        columns[spread(j, side), :] = held


def take_edges(count, cells, slot_of, columns, edges, base):
    side = columns.shape[0]
    turned = jnp.transpose(columns[...])
    for p in range(count):
        edges[base + 16 * p : base + 16 * p + 8, :] = turned[8 * p : 8 * p + 8, :]
        for f in range(4):
            row = base + 16 * p + 8 + 2 * f
            edges[row : row + 1, :] = cells[slot_of(p), f, side - 1 : side, :]
            edges[row + 1 : row + 2, :] = cells[slot_of(p), f, 0:1, :]


def loader(cells, i):
    side = cells.shape[3]
    return lambda f, j: cells[i, f, spread(j, side), :]


def update(cells, first, many, weights, put):
    loads = [loader(cells, first + n) for n in range(many)]
    inner_update(loads, lambda n, f, j, value: put(n, f, ROWS * j, value), cells.shape[3], weights)


def fetch(cells_hbm, first, cells, sems, parts):
    def copy(i):
        return pltpu.make_async_copy(cells_hbm.at[first + i], cells.at[i], sems.at[i])

    for start, count in parts:
        for i in range(count):
            copy(start + i).start()
    return copy


def outer_slot(cells_hbm, margin):
    _, odd = position()
    return odd * (cells_hbm.shape[0] - margin)


def outer_kernel(margin, cells_hbm, out, edges, cells, columns, weights, sems):
    side = columns.shape[0]
    copy = fetch(cells_hbm, outer_slot(cells_hbm, margin), cells, sems, [(0, margin)])
    fill_weights(weights)

    @pl.loop(0, margin // PAIR)
    def _(step):
        i = step * PAIR
        for n in range(PAIR):
            copy(i + n).wait()

        def put(n, f, row, value):
            out[i + n, f, row : row + ROWS, :] = value

        gather_columns([loader(cells, i + n) for n in range(PAIR)], columns, 8 * i, side)
        update(cells, i, PAIR, weights, put)

    take_edges(margin, cells, lambda p: p, columns, edges, 0)


def cost(patches, side):
    return pl.CostEstimate(
        flops=patches * side * side * 800,
        bytes_accessed=patches * side * side * 28,
        transcendentals=patches * side * side,
    )


def room(mebibytes):
    return pltpu.CompilerParams(vmem_limit_bytes=mebibytes << 20)


def outer_patches(old_cells, margin):
    side = old_cells.shape[3]
    return pl.pallas_call(
        functools.partial(outer_kernel, margin),
        in_specs=[HBM],
        out_specs=[VMEM, VMEM],
        out_shape=[
            jax.ShapeDtypeStruct((margin, 3, side, side), jnp.float32),
            jax.ShapeDtypeStruct((16 * margin, side), jnp.float32),
        ],
        scratch_shapes=[
            pltpu.VMEM((margin, 4, side, side), jnp.float32),
            pltpu.VMEM((side, side), jnp.float32),
            pltpu.VMEM((2 * side, 6 * side), jnp.bfloat16),
            pltpu.SemaphoreType.DMA((margin,)),
        ],
        cost_estimate=cost(margin, side),
        compiler_params=room(48),
        name="outer",
    )(old_cells)


def after(value, other):
    any_place = pl.BlockSpec(memory_space=pl.ANY)
    return pl.pallas_call(
        lambda value_ref, other_ref, out_ref: None,
        in_specs=[any_place, any_place],
        out_specs=any_place,
        out_shape=jax.ShapeDtypeStruct(value.shape, value.dtype),
        input_output_aliases={0: 0},
        compiler_params=room(4),
        name="after",
    )(value, other)


def layout(margin, per_device):
    home = 16 * margin
    limit = home + 16 * per_device
    brought = limit + 8
    return home, limit, brought, brought + 16 * margin


def home_kernel(margin, range_ref, cells_hbm, came, shared, inner, own, cells, columns, weights, sems):
    side = columns.shape[0]
    count = own.shape[0]
    home, limit, brought, total = layout(margin, count)
    _, odd = position()
    inner_at = (1 - odd) * count
    home_at = odd * margin
    parts = [(inner_at, margin), (home_at, count)]
    copy = fetch(cells_hbm, (1 - odd) * margin, cells, sems, parts)
    fill_weights(weights)

    for at, many, out, row in ((inner_at, margin, inner, 0), (home_at, count, own, home)):

        @pl.loop(0, many // PAIR)
        def _(step, at=at, out=out):
            i = step * PAIR
            for n in range(PAIR):
                copy(at + i + n).wait()

            def put(n, f, row, value):
                out[i + n, f, row : row + ROWS, :] = value

            gather_columns([loader(cells, at + i + n) for n in range(PAIR)], columns, 8 * i, side)
            update(cells, at + i, PAIR, weights, put)

        take_edges(many, cells, lambda p, at=at: at + p, columns, shared, row)

    outer_limit = jnp.where(odd == 1, range_ref[0, 1], range_ref[0, 0])
    shared[limit : limit + 8, :] = jnp.full((8, side), outer_limit, jnp.int32).astype(jnp.float32)
    shared[brought:total, :] = came[0 : total - brought, :]


def home_patches(old_range, old_cells, came, margin, per_device):
    side = old_cells.shape[3]
    total = layout(margin, per_device)[-1]
    return pl.pallas_call(
        functools.partial(home_kernel, margin),
        in_specs=[SMEM, HBM, VMEM],
        out_specs=[VMEM] * 3,
        out_shape=[
            jax.ShapeDtypeStruct((total, side), jnp.float32),
            jax.ShapeDtypeStruct((margin, 3, side, side), jnp.float32),
            jax.ShapeDtypeStruct((per_device, 3, side, side), jnp.float32),
        ],
        scratch_shapes=[
            pltpu.VMEM((margin + per_device, 4, side, side), jnp.float32),
            pltpu.VMEM((side, side), jnp.float32),
            pltpu.VMEM((2 * side, 6 * side), jnp.bfloat16),
            pltpu.SemaphoreType.DMA((margin + per_device,)),
        ],
        cost_estimate=cost(margin + per_device, side),
        compiler_params=room(48),
        name="home",
    )(old_range, old_cells, came)


def answer_kernel(margin, count, range_ref, rows_ref, mine, theirs, edges, message):
    side = edges.shape[1]
    home, limit, brought, _ = layout(margin, count)
    inner = 0
    me, odd = position()
    start, stop = range_ref[0, 0], range_ref[0, 1]
    even = odd == 0
    at_me = pl.multiple_of(16 * count * odd, 16)
    at_them = pl.multiple_of(16 * count * (1 - odd), 16)
    edges[pl.ds(at_me, 16 * count), :] = mine[home : home + 16 * count, :]
    edges[pl.ds(at_them, 16 * count), :] = theirs[home : home + 16 * count, :]
    their_limit = theirs[limit : limit + 8, :]
    low, high = 0, count - margin
    for m in range(margin):
        l = jnp.where(even, high, low) + m
        g = me * count + l
        taken = jnp.where(even, g >= stop, g < start)
        to = pl.multiple_of(at_me + 16 * l, 16)
        from_pair = theirs[inner + 16 * m : inner + 16 * (m + 1), :]
        edges[pl.ds(to, 16), :] = jnp.where(taken, from_pair, edges[pl.ds(to, 16), :])
        l = jnp.where(even, low, high) + m
        g = (me + 1 - 2 * odd) * count + l
        taken = jnp.where(even, g < stop, g >= start)
        to = pl.multiple_of(at_them + 16 * l, 16)
        from_pair = mine[inner + 16 * m : inner + 16 * (m + 1), :]
        edges[pl.ds(to, 16), :] = jnp.where(taken, from_pair, edges[pl.ds(to, 16), :])
        l = jnp.where(even, low, high) + m
        g = me * count + l
        taken = jnp.where(even, g < start, g >= stop)
        to = pl.multiple_of(at_me + 16 * l, 16)
        crossed = mine[brought + 16 * m : brought + 16 * (m + 1), :]
        edges[pl.ds(to, 16), :] = jnp.where(taken, crossed, edges[pl.ds(to, 16), :])
        l = jnp.where(even, high, low) + m
        g = ((me + 1 - 2 * odd) * count + l).astype(jnp.float32)
        to = pl.multiple_of(at_them + 16 * l, 16)
        taken = jnp.where(even, g - their_limit, their_limit - g - 1.0) >= 0.0
        for half in range(2):
            crossed = theirs[brought + 16 * m + 8 * half : brought + 16 * m + 8 * half + 8, :]
            at = pl.multiple_of(to + 8 * half, 8)
            edges[pl.ds(at, 8), :] = jnp.where(taken, crossed, edges[pl.ds(at, 8), :])
    for k in range(3):
        asked = range(k * CAP, (k + 1) * CAP)
        values = [edges[pl.ds(rows_ref[n], 4, stride=2), :] for n in asked]
        for n, value in zip(asked, values):
            message[pl.ds(8 * (n // 2) + n % 2, 4, stride=2), :] = value


def answers(old_range, rows, mine, theirs, margin, per_device):
    side = mine.shape[1]
    return pl.pallas_call(
        functools.partial(answer_kernel, margin, per_device),
        in_specs=[SMEM, SMEM, VMEM, VMEM],
        out_specs=[VMEM, VMEM],
        out_shape=[
            jax.ShapeDtypeStruct((32 * per_device, side), jnp.float32),
            jax.ShapeDtypeStruct((12 * CAP, side), jnp.float32),
        ],
        compiler_params=room(4),
        name="answers",
    )(old_range, rows, mine, theirs)


def rim_terms(rows_ref, edges, crossed, passed, columns, lines, source, ghost, turn, count, odd):
    total = edges.shape[0]
    step = crossed.shape[0]
    source[0:total, :] = edges[...]
    source[total : total + step, :] = crossed[...]
    source[total + step : total + 2 * step, :] = passed[...]
    field = lax.broadcasted_iota(jnp.int32, (4, edges.shape[1]), 0)
    group = 4
    for start in range(0, count, group):
        fetched = []
        for p in range(start, start + group):
            for s in range(4):
                row = rows_ref[4 * p + s]
                wall = row < 0
                value = source[pl.ds(jnp.where(wall, -1 - row, row), 4, stride=2), :]
                value = jnp.where((field == 1 + s // 2) & wall, -value, value)
                fetched.append((16 * p + 8 * (s // 2) + 1 - s % 2, value))
        for target, value in fetched:
            ghost[pl.ds(target, 4, stride=2), :] = value
    turn[...] = jnp.zeros_like(turn)
    lines[...] = jnp.zeros_like(lines)
    for s in range(4):
        parity = 1 - s % 2
        sign = 1.0 - 2.0 * parity
        axis = s // 2
        normal, across = (1, 2) if axis == 0 else (2, 1)

        def both(f):
            row = 8 * axis + 2 * f + parity
            own = source[pl.ds(16 * count * odd + row, count, stride=16), :]
            return own, ghost[pl.ds(row, count, stride=16), :]

        hc, hg = both(0)
        nc, ng = both(normal)
        ac, ag = both(across)
        bc, bg = both(3)
        rc, rg = lax.rsqrt(hc), lax.rsqrt(hg)
        uc, ug = nc * rc * rc, ng * rg * rg
        top = jnp.maximum(jnp.abs(uc) + hc * rc, jnp.abs(ug) + hg * rg)
        fc, fg = nc * uc + 0.5 * hc * hc, ng * ug + 0.5 * hg * hg
        c_h = -HALF * (sign * (nc + ng) - top * ((hg + bg) - (hc + bc)))
        c_n = -HALF * (sign * (fc + fg + hc * bg) - top * (ng - nc))
        c_t = -HALF * (sign * (ac * uc + ag * ug) - top * (ag - ac))
        for f, value in ((0, c_h), (normal, c_n), (across, c_t)):
            target = turn if axis == 0 else lines
            target[pl.ds(2 * f + parity, count, stride=8), :] = value
    turn[...] = jnp.transpose(turn[...])
    side = turn.shape[0]
    columns[...] = pieces(jnp.concatenate([turn[spread(j, side), :] for j in range(side // ROWS)], axis=0))


def fill_places(places):
    side = places.shape[0] // 2
    row = lax.broadcasted_iota(jnp.int32, (side, side), 0) % 8
    lane = lax.broadcasted_iota(jnp.int32, (side, side), 1)
    source = row - jnp.where(lane == 0, 1, jnp.where(lane == side - 1, 0, 1024))
    for f in range(3):
        block = jnp.where(source == 2 * f, 1.0, 0.0).astype(jnp.bfloat16)
        for half in range(2):
            places[half * side : (half + 1) * side, f * side : (f + 1) * side] = block


def final_kernel(
    margin, range_ref, rows_ref, edges, crossed, passed, own, theirs, arrived, out,
    result, source, ghost, turn, columns, lines, places, sems,
):
    count, side = own.shape[0], lines.shape[1]
    me, odd = position()
    even = odd == 0
    fill_places(places)
    rim_terms(rows_ref, edges, crossed, passed, columns, lines, source, ghost, turn, count, odd)
    start, stop = range_ref[0, 0], range_ref[0, 1]
    line = iota(0, side)
    lane = lax.broadcasted_iota(jnp.int32, (side, 2 * side), 1) % side
    steps = side // ROWS

    def copy(p):
        return pltpu.make_async_copy(result.at[p], out.at[p], sems.at[p])

    for group in range(0, count, margin):
        patches = range(group, group + margin)
        held = columns[...]
        masked = [held * jnp.where(lane // 8 == p, 1.0, 0.0).astype(jnp.bfloat16) for p in patches]
        terms = product(jnp.concatenate(masked, axis=0), places[...])
        for m, p in enumerate(patches):
            if group == 0:
                taken = me * count + p < start
            elif group == count - margin:
                taken = me * count + p >= stop
            else:
                taken = None
            near = even if group else odd == 1
            for f in range(3):
                for j in range(steps):
                    rows = slice(ROWS * j, ROWS * (j + 1))
                    value = own[p, f, rows, :]
                    if taken is not None:
                        moved = jnp.where(near, theirs[m, f, rows, :], arrived[m, f, rows, :])
                        value = jnp.where(taken, moved, value)
                    at = side * m + ROWS * j
                    value = value + terms[at : at + ROWS, f * side : (f + 1) * side]
                    if j == 0:
                        south = lines[8 * p + 2 * f + 1 : 8 * p + 2 * f + 2, :]
                        value = value + jnp.where(line == 0, south, 0.0)
                    if j == steps - 1:
                        north = lines[8 * p + 2 * f : 8 * p + 2 * f + 1, :]
                        value = value + jnp.where(line == ROWS - 1, north, 0.0)
                    result[p, f, spread(j, side), :] = value
            copy(p).start()
    for p in range(count):
        copy(p).wait()


def finished(old_range, rows, edges, crossed, passed, own, theirs, arrived, margin):
    count, _, side, _ = own.shape
    return pl.pallas_call(
        functools.partial(final_kernel, margin),
        in_specs=[SMEM, SMEM] + [VMEM] * 6,
        out_specs=HBM,
        out_shape=jax.ShapeDtypeStruct(own.shape, jnp.float32),
        scratch_shapes=[
            pltpu.VMEM(own.shape, jnp.float32),
            pltpu.VMEM((edges.shape[0] + 2 * crossed.shape[0], side), jnp.float32),
            pltpu.VMEM((16 * count, side), jnp.float32),
            pltpu.VMEM((side, side), jnp.float32),
            pltpu.VMEM((side, 2 * side), jnp.bfloat16),
            pltpu.VMEM((side, side), jnp.float32),
            pltpu.VMEM((2 * side, 3 * side), jnp.bfloat16),
            pltpu.SemaphoreType.DMA((count,)),
        ],
        compiler_params=room(12),
        name="final",
    )(old_range, rows, edges, crossed, passed, own, theirs, arrived)


def swapped(value, first):
    pairs = [(i, i + 1) for i in range(first, lax.axis_size(AXES) - 1, 2)]
    return lax.ppermute(value, AXES, pairs + [(j, i) for i, j in pairs])


def late(value, anchor):
    return lax.optimization_barrier((value, anchor))[0]


def ranks(named, entry):
    earlier = entry[:, None] < entry[None, :]
    return jnp.sum(jnp.where(named[..., :, None] & earlier, 1, 0), axis=-2)


def local(old_cells, old_range, neighbours):
    per_device = neighbours.shape[0]
    side = old_cells.shape[3]
    margin = (old_cells.shape[0] - per_device) // 2
    entries = 4 * per_device
    me, odd = position()

    their_table = swapped(neighbours, 0)
    leaving, leaving_edges = outer_patches(old_cells, margin)

    table = late(neighbours, leaving_edges).reshape(1, -1)
    their_table = their_table.reshape(1, -1)
    tables = jnp.where(
        odd == 0,
        jnp.concatenate([table, their_table], axis=1),
        jnp.concatenate([their_table, table], axis=1),
    ).astype(jnp.float32)
    tables = jnp.pad(tables, ((0, 7), (0, side - 2 * entries)))
    bundle = jnp.concatenate([leaving_edges, tables], axis=0)
    came = swapped(bundle, 1)

    arrived = swapped(after(leaving, bundle), 1)

    shared, inner, own = home_patches(old_range, old_cells, came, margin, per_device)
    their_edges = swapped(shared, 0)
    theirs = swapped(inner, 0)

    me, entry, asked_by = late((me, jnp.arange(entries, dtype=jnp.int32), came), shared)
    odd = lax.rem(me, 2)
    entry_side = entry % 4
    at_side = 8 * (entry_side // 2) + entry_side % 2
    asked_by = asked_by[16 * margin, : 2 * entries].astype(jnp.int32).reshape(2, entries)
    middle = jnp.where(odd == 0, asked_by[1], asked_by[0])
    listed = jnp.stack([asked_by[0], middle, asked_by[1]])
    owners = me + jnp.where(odd == 0, jnp.array([0, 0, 1], jnp.int32), jnp.array([-1, 0, 0], jnp.int32))
    asked = (listed >= 0) & (listed // per_device == owners[:, None])
    rows = 16 * (listed - 2 * per_device * (me // 2)) + at_side
    chosen = asked[:, None, :] & (ranks(asked, entry)[:, None, :] == jnp.arange(CAP)[None, :, None])
    send_rows = jnp.sum(jnp.where(chosen, rows[:, None, :], 0), axis=2).reshape(-1)

    edges, message = answers(old_range, send_rows, shared, their_edges, margin, per_device)
    crossed = swapped(message, 1)
    passed = swapped(crossed, 0)

    me, entry, listed = late((me, entry, neighbours), message)
    odd = lax.rem(me, 2)
    entry_side = entry % 4
    at_side = 8 * (entry_side // 2) + entry_side % 2
    listed = listed.reshape(-1)
    owner = listed // per_device
    mine, total, step = 32 * per_device, 16 * per_device, 12 * CAP
    lists = jnp.where(
        odd == 0,
        jnp.array([[-2, mine], [-1, mine + 4 * CAP], [2, mine + step]], jnp.int32),
        jnp.array([[-2, mine + step + 8 * CAP], [1, mine + 4 * CAP], [2, mine + 8 * CAP]], jnp.int32),
    )
    named = (listed >= 0) & (owner - me == lists[:, :1])
    place = ranks(named, entry)
    across = jnp.sum(jnp.where(named, lists[:, 1:] + 8 * (place // 2) + place % 2, 0), axis=0)
    within = 16 * (listed - 2 * per_device * (me // 2)) + at_side
    wall = total * odd + 16 * (entry // 4) + 8 * (entry_side // 2) + 1 - entry_side % 2
    ghost_rows = jnp.where(listed < 0, -1 - wall, jnp.where(owner // 2 == me // 2, within, across))

    return finished(old_range, ghost_rows, edges, crossed, passed, own, theirs, arrived, margin)


def solution(mesh):
    placed = (
        P(("member", "curve", "sub"), None, None, None),
        P(("member", "curve", "sub"), None),
        P(("member", "curve", "sub"), None),
    )
    return jax.shard_map(
        local,
        mesh=mesh,
        in_specs=placed,
        out_specs=P(("member", "curve", "sub"), None, None, None),
        check_vma=False,
    )
```

```python
import functools

import jax
import jax.numpy as jnp
from jax import lax
from jax.experimental import pallas as pl
from jax.experimental.pallas import tpu as pltpu
from jax.sharding import PartitionSpec as P

RATE_STEP = 0.1
HALF = 0.5 * RATE_STEP
AXES = ("curve", "sub")
CAP = 8
ROWS = 8
PAIR = 2
VMEM = pl.BlockSpec(memory_space=pltpu.VMEM)
SMEM = pl.BlockSpec(memory_space=pltpu.SMEM)
HBM = pl.BlockSpec(memory_space=pltpu.HBM)


def position():
    me = lax.axis_index(AXES)
    return me, lax.rem(me, 2)


def iota(axis, side):
    return lax.broadcasted_iota(jnp.int32, (ROWS, side), axis)


def spread(j, side):
    return pl.ds(j, ROWS, stride=side // ROWS)


def pieces(x):
    high = x.astype(jnp.bfloat16)
    low = (x - high.astype(jnp.float32)).astype(jnp.bfloat16)
    return jnp.concatenate([high, low], axis=1)


def product(parts, weights):
    return jnp.dot(parts, weights, preferred_element_type=jnp.float32)


AHEAD, EAST, SUMS, SLOPE = slice(0, 2), slice(2, 4), slice(4, 5), slice(5, 6)


def fill_weights(weights):
    side = weights.shape[0] // 2
    row = lax.broadcasted_iota(jnp.int32, (side, side), 0)
    lane = lax.broadcasted_iota(jnp.int32, (side, side), 1)
    one = lambda where: jnp.where(where, 1.0, 0.0)
    after, here, before = one(row == lane + 1), one(row == lane), one(row == lane - 1)
    inner_e, inner_w = lane != side - 1, lane != 0
    east = jnp.where(inner_e, after + here, 0.0)
    west = jnp.where(inner_w, here + before, 0.0)
    blocks = (
        after,
        before,
        jnp.where(inner_e, after - here, 0.0),
        jnp.where(inner_w, here - before, 0.0),
        east - west,
        after - before,
    )
    for n, block in enumerate(blocks):
        for half in range(2):
            weights[half * side : (half + 1) * side, n * side : (n + 1) * side] = block.astype(jnp.bfloat16)


def inner_update(loads, store, side, weights):
    line = iota(0, side)
    first, last = line == 0, line == ROWS - 1
    steps = side // ROWS
    many = len(loads)

    def cell(h, mx, my, bed):
        root = lax.rsqrt(h)
        celerity = h * root
        inverse = root * root
        u = mx * inverse
        v = my * inverse
        half_sq = 0.5 * h * h
        cross = my * u
        rate_y = jnp.abs(v) + celerity
        rate_x = jnp.abs(u) + celerity
        return (rate_y, h + bed, mx, my, cross, my * v + half_sq, bed), rate_x, mx * u + half_sq, h

    def face_y(low, high):
        top = jnp.maximum(low[0], high[0])
        return [
            (high[3] + low[3]) - top * (high[1] - low[1]),
            (high[4] + low[4]) - top * (high[2] - low[2]),
            (high[5] + low[5]) - top * (high[3] - low[3]),
        ]

    def taken(block):
        return weights[:, block.start * side : block.stop * side]

    cells = [cell(*[load(f, j) for f in range(4)]) for load in loads for j in range(steps)]
    stack = lambda pick: pieces(jnp.concatenate([pick(c) for c in cells], axis=0))
    eta, mx, my, cross, bed = (stack(lambda c, n=n: c[0][n]) for n in (1, 2, 3, 4, 6))
    fx = stack(lambda c: c[2])
    rates = product(stack(lambda c: c[1]), taken(AHEAD))
    jumps = product(jnp.concatenate([eta, mx, my], axis=0), taken(EAST))
    sums = product(jnp.concatenate([mx, fx, cross], axis=0), taken(SUMS))
    slopes = product(bed, taken(SLOPE))
    for n in range(many):
        mine = cells[n * steps : (n + 1) * steps]
        low = [pltpu.roll(each, 1, 0) for each in mine[steps - 1][0]]
        faces = []
        for j in range(steps):
            faces.append(face_y(low, mine[j][0]))
            low = mine[j][0]
        faces[0] = [jnp.where(first, 0.0, each) for each in faces[0]]
        beds = [c[0][6] for c in mine]
        under = jnp.where(first, 0.0, pltpu.roll(beds[-1], 1, 0))
        over = jnp.where(last, 0.0, pltpu.roll(beds[0], ROWS - 1, 0))
        faces.append([jnp.where(last, 0.0, pltpu.roll(each, ROWS - 1, 0)) for each in faces[0]])
        for j in range(steps):
            (_, _, mx, my, _, _, _), rate, _, h = mine[j]
            at = [(q * many + n) * side + ROWS * j for q in range(3)]
            rows = [slice(r, r + ROWS) for r in at]
            top_e = jnp.maximum(rate, rates[rows[0], :side])
            top_w = jnp.maximum(rate, rates[rows[0], side:])
            x = [sums[r] - (top_e * jumps[r, :side] - top_w * jumps[r, side:]) for r in rows]
            south, north = faces[j], faces[j + 1]
            slope_y = (beds[j + 1] if j + 1 < steps else over) - (beds[j - 1] if j else under)
            store(n, 0, j, h - HALF * (x[0] + (north[0] - south[0])))
            store(n, 1, j, mx - HALF * (x[1] + h * slopes[rows[0]] + (north[1] - south[1])))
            store(n, 2, j, my - HALF * (x[2] + h * slope_y + (north[2] - south[2])))


def gather_columns(loads, columns, first_at, side):
    pair = iota(1, side) // 2
    for j in range(side // ROWS):
        held = columns[spread(j, side), :]
        for n, load in enumerate(loads):
            at = first_at + 8 * n
            for f in range(4):
                held = jnp.where(pair == at // 2 + f, pltpu.roll(load(f, j), at + 2 * f + 1, 1), held)
        columns[spread(j, side), :] = held


def take_edges(count, cells, slot_of, columns, edges, base):
    side = columns.shape[0]
    turned = jnp.transpose(columns[...])
    for p in range(count):
        edges[base + 16 * p : base + 16 * p + 8, :] = turned[8 * p : 8 * p + 8, :]
        for f in range(4):
            row = base + 16 * p + 8 + 2 * f
            edges[row : row + 1, :] = cells[slot_of(p), f, side - 1 : side, :]
            edges[row + 1 : row + 2, :] = cells[slot_of(p), f, 0:1, :]


def loader(cells, i):
    side = cells.shape[3]
    return lambda f, j: cells[i, f, spread(j, side), :]


def update(cells, first, many, weights, put):
    loads = [loader(cells, first + n) for n in range(many)]
    inner_update(loads, lambda n, f, j, value: put(n, f, ROWS * j, value), cells.shape[3], weights)


def fetch(cells_hbm, first, cells, sems, parts):
    def copy(i):
        return pltpu.make_async_copy(cells_hbm.at[first + i], cells.at[i], sems.at[i])

    for start, count in parts:
        for i in range(count):
            copy(start + i).start()
    return copy


def outer_slot(cells_hbm, margin):
    _, odd = position()
    return odd * (cells_hbm.shape[0] - margin)


def outer_kernel(margin, cells_hbm, table, their_table, out, bundle, cells, columns, weights, sems):
    side = columns.shape[0]
    _, odd = position()
    copy = fetch(cells_hbm, outer_slot(cells_hbm, margin), cells, sems, [(0, margin)])
    fill_weights(weights)
    count, sides = table.shape
    at = 16 * margin
    bundle[at : at + 2 * count, :] = jnp.zeros((2 * count, side), jnp.float32)
    for which, ref in ((odd, table), (1 - odd, their_table)):
        start = pl.multiple_of(at + which * count, 8)
        bundle[pl.ds(start, count), 0:sides] = ref[...].astype(jnp.float32)

    @pl.loop(0, margin // PAIR)
    def _(step):
        i = step * PAIR
        for n in range(PAIR):
            copy(i + n).wait()

        def put(n, f, row, value):
            out[i + n, f, row : row + ROWS, :] = value

        gather_columns([loader(cells, i + n) for n in range(PAIR)], columns, 8 * i, side)
        update(cells, i, PAIR, weights, put)

    take_edges(margin, cells, lambda p: p, columns, bundle, 0)


def cost(patches, side):
    return pl.CostEstimate(
        flops=patches * side * side * 800,
        bytes_accessed=patches * side * side * 28,
        transcendentals=patches * side * side,
    )


def room(mebibytes):
    return pltpu.CompilerParams(vmem_limit_bytes=mebibytes << 20)


def outer_patches(old_cells, table, their_table, margin):
    side = old_cells.shape[3]
    return pl.pallas_call(
        functools.partial(outer_kernel, margin),
        in_specs=[HBM, VMEM, VMEM],
        out_specs=[VMEM, VMEM],
        out_shape=[
            jax.ShapeDtypeStruct((margin, 3, side, side), jnp.float32),
            jax.ShapeDtypeStruct((16 * margin + 2 * table.shape[0], side), jnp.float32),
        ],
        scratch_shapes=[
            pltpu.VMEM((margin, 4, side, side), jnp.float32),
            pltpu.VMEM((side, side), jnp.float32),
            pltpu.VMEM((2 * side, 6 * side), jnp.bfloat16),
            pltpu.SemaphoreType.DMA((margin,)),
        ],
        cost_estimate=cost(margin, side),
        compiler_params=room(48),
        name="outer",
    )(old_cells, table, their_table)


def after(value, other):
    any_place = pl.BlockSpec(memory_space=pl.ANY)
    return pl.pallas_call(
        lambda value_ref, other_ref, out_ref: None,
        in_specs=[any_place, any_place],
        out_specs=any_place,
        out_shape=jax.ShapeDtypeStruct(value.shape, value.dtype),
        input_output_aliases={0: 0},
        compiler_params=room(4),
        name="after",
    )(value, other)


def layout(margin, per_device):
    home = 16 * margin
    limit = home + 16 * per_device
    brought = limit + 8
    return home, limit, brought, brought + 16 * margin


def home_kernel(margin, range_ref, cells_hbm, came, shared, inner, own, cells, columns, weights, sems):
    side = columns.shape[0]
    count = own.shape[0]
    home, limit, brought, total = layout(margin, count)
    _, odd = position()
    inner_at = (1 - odd) * count
    home_at = odd * margin
    parts = [(inner_at, margin), (home_at, count)]
    copy = fetch(cells_hbm, (1 - odd) * margin, cells, sems, parts)
    fill_weights(weights)

    for at, many, out, row in ((inner_at, margin, inner, 0), (home_at, count, own, home)):

        @pl.loop(0, many // PAIR)
        def _(step, at=at, out=out):
            i = step * PAIR
            for n in range(PAIR):
                copy(at + i + n).wait()

            def put(n, f, row, value):
                out[i + n, f, row : row + ROWS, :] = value

            gather_columns([loader(cells, at + i + n) for n in range(PAIR)], columns, 8 * i, side)
            update(cells, at + i, PAIR, weights, put)

        take_edges(many, cells, lambda p, at=at: at + p, columns, shared, row)

    outer_limit = jnp.where(odd == 1, range_ref[0, 1], range_ref[0, 0])
    shared[limit : limit + 8, :] = jnp.full((8, side), outer_limit, jnp.int32).astype(jnp.float32)
    shared[brought:total, :] = came[0 : total - brought, :]


def home_patches(old_range, old_cells, came, margin, per_device):
    side = old_cells.shape[3]
    total = layout(margin, per_device)[-1]
    return pl.pallas_call(
        functools.partial(home_kernel, margin),
        in_specs=[SMEM, HBM, VMEM],
        out_specs=[VMEM] * 3,
        out_shape=[
            jax.ShapeDtypeStruct((total, side), jnp.float32),
            jax.ShapeDtypeStruct((margin, 3, side, side), jnp.float32),
            jax.ShapeDtypeStruct((per_device, 3, side, side), jnp.float32),
        ],
        scratch_shapes=[
            pltpu.VMEM((margin + per_device, 4, side, side), jnp.float32),
            pltpu.VMEM((side, side), jnp.float32),
            pltpu.VMEM((2 * side, 6 * side), jnp.bfloat16),
            pltpu.SemaphoreType.DMA((margin + per_device,)),
        ],
        cost_estimate=cost(margin + per_device, side),
        compiler_params=room(48),
        name="home",
    )(old_range, old_cells, came)


def entries_of(table, sides, lanes):
    count = table.shape[0]
    return jnp.concatenate([jnp.broadcast_to(table[:, s : s + 1], (count, lanes)) for s in range(sides)], axis=0)


def grid_iota(rows, lanes, axis):
    return lax.broadcasted_iota(jnp.int32, (rows, lanes), axis)


def flag(where):
    return jnp.where(where, 1.0, 0.0)


def ranks(masks):
    rows, lanes = masks[0].shape
    earlier = flag(grid_iota(rows, lanes, 1) < grid_iota(rows, lanes, 0)).astype(jnp.bfloat16)
    stacked = jnp.concatenate(masks, axis=1).astype(jnp.bfloat16)
    if rows < lanes:
        stacked = jnp.concatenate([stacked, jnp.zeros((lanes - rows, stacked.shape[1]), jnp.bfloat16)], axis=0)
    counted = product(earlier, stacked)
    return [counted[:, n * lanes : (n + 1) * lanes] for n in range(len(masks))]


def edge_places(row, count, patch):
    s = row // count
    return 4 * count * (s % 2) + s // 2, 2.0 * patch


def edges_of_field(edges, f):
    tiles = edges.shape[0] // 8
    return [edges[pl.ds(2 * f + parity, tiles, stride=8), :] for parity in range(2)]


def answer_kernel(margin, count, range_ref, mine, theirs, came, edges, message):
    side = edges.shape[1]
    home, limit, brought, _ = layout(margin, count)
    inner = 0
    me, odd = position()
    start, stop = range_ref[0, 0], range_ref[0, 1]
    even = odd == 0
    at_me = pl.multiple_of(16 * count * odd, 16)
    at_them = pl.multiple_of(16 * count * (1 - odd), 16)
    edges[pl.ds(at_me, 16 * count), :] = mine[home : home + 16 * count, :]
    edges[pl.ds(at_them, 16 * count), :] = theirs[home : home + 16 * count, :]
    their_limit = theirs[limit : limit + 8, :]
    low, high = 0, count - margin
    for m in range(margin):
        l = jnp.where(even, high, low) + m
        g = me * count + l
        taken = jnp.where(even, g >= stop, g < start)
        to = pl.multiple_of(at_me + 16 * l, 16)
        from_pair = theirs[inner + 16 * m : inner + 16 * (m + 1), :]
        edges[pl.ds(to, 16), :] = jnp.where(taken, from_pair, edges[pl.ds(to, 16), :])
        l = jnp.where(even, low, high) + m
        g = (me + 1 - 2 * odd) * count + l
        taken = jnp.where(even, g < stop, g >= start)
        to = pl.multiple_of(at_them + 16 * l, 16)
        from_pair = mine[inner + 16 * m : inner + 16 * (m + 1), :]
        edges[pl.ds(to, 16), :] = jnp.where(taken, from_pair, edges[pl.ds(to, 16), :])
        l = jnp.where(even, low, high) + m
        g = me * count + l
        taken = jnp.where(even, g < start, g >= stop)
        to = pl.multiple_of(at_me + 16 * l, 16)
        crossed = mine[brought + 16 * m : brought + 16 * (m + 1), :]
        edges[pl.ds(to, 16), :] = jnp.where(taken, crossed, edges[pl.ds(to, 16), :])
        l = jnp.where(even, high, low) + m
        g = ((me + 1 - 2 * odd) * count + l).astype(jnp.float32)
        to = pl.multiple_of(at_them + 16 * l, 16)
        taken = jnp.where(even, g - their_limit, their_limit - g - 1.0) >= 0.0
        for half in range(2):
            crossed = theirs[brought + 16 * m + 8 * half : brought + 16 * m + 8 * half + 8, :]
            at = pl.multiple_of(to + 8 * half, 8)
            edges[pl.ds(at, 8), :] = jnp.where(taken, crossed, edges[pl.ds(at, 8), :])
    sides, total = 4, 8 * count
    row = grid_iota(total, side, 0)
    lane = grid_iota(total, side, 1)
    which, within = row // (sides * count), row % (sides * count)
    at = 16 * margin
    tables = [came[at + n * count : at + (n + 1) * count, :] for n in range(2)]
    listed = jnp.concatenate([entries_of(table, sides, side) for table in tables], axis=0)
    patch = listed - (2 * count * (me // 2)).astype(jnp.float32)
    held = [(patch >= n * count) & (patch < (n + 1) * count) for n in range(2)]
    masks = [
        flag((which == 0) & held[0]),
        jnp.where(even, flag((which == 1) & held[0]), flag((which == 0) & held[1])),
        flag((which == 1) & held[1]),
    ]
    chosen = jnp.zeros((total, side), jnp.float32)
    for k, (mask, rank) in enumerate(zip(masks, ranks(masks))):
        slot = (lane - k * CAP).astype(jnp.float32)
        chosen = chosen + jnp.where((lane // CAP == k) & (rank == slot), mask, 0.0)
    place, twice = edge_places(within, count, patch)
    hot = flag(lane.astype(jnp.float32) == place.astype(jnp.float32) + twice).astype(jnp.bfloat16)
    slots = jnp.transpose(chosen)[0:32, :].astype(jnp.bfloat16)
    picked = product(slots, hot).astype(jnp.bfloat16)
    picked = jnp.concatenate([picked] * 3, axis=1)
    for f in range(4):
        values = jnp.concatenate(edges_of_field(edges, f), axis=0)
        high = values.astype(jnp.bfloat16)
        left = values - high.astype(jnp.float32)
        mid = left.astype(jnp.bfloat16)
        low = (left - mid.astype(jnp.float32)).astype(jnp.bfloat16)
        taken = product(picked, jnp.concatenate([high, mid, low], axis=0))
        message[3 * CAP * f : 3 * CAP * (f + 1), :] = taken[0 : 3 * CAP, :]


def answers(old_range, mine, theirs, came, margin, per_device):
    side = mine.shape[1]
    return pl.pallas_call(
        functools.partial(answer_kernel, margin, per_device),
        in_specs=[SMEM, VMEM, VMEM, VMEM],
        out_specs=[VMEM, VMEM],
        out_shape=[
            jax.ShapeDtypeStruct((32 * per_device, side), jnp.float32),
            jax.ShapeDtypeStruct((12 * CAP, side), jnp.float32),
        ],
        compiler_params=room(4),
        name="answers",
    )(old_range, mine, theirs, came)


def ghosts(table, edges, crossed, passed, me, odd):
    count, sides = table.shape
    side = edges.shape[1]
    total = sides * count
    even = odd == 0
    row, lane = grid_iota(total, side, 0), grid_iota(total, side, 1)
    s, p = row // count, row % count
    listed = entries_of(table[...].astype(jnp.float32), sides, side)
    wall = listed < 0.0
    patch = listed - (2 * count * (me // 2)).astype(jnp.float32)
    distance = listed - (count * me).astype(jnp.float32)
    first = 4 * count * 2
    step = 3 * CAP
    lists = (
        (-2, -2, first, first + step + 2 * CAP),
        (-1, 1, first + CAP, first + CAP),
        (2, 2, first + step, first + 2 * CAP),
    )
    masks, starts = [], []
    for far_even, far_odd, at_even, at_odd in lists:
        low = (count * jnp.where(even, far_even, far_odd)).astype(jnp.float32)
        masks.append(flag(~wall & (distance >= low) & (distance < low + count)))
        starts.append(jnp.where(even, at_even, at_odd).astype(jnp.float32))
    across = jnp.zeros((total, side), jnp.float32)
    for mask, rank, start in zip(masks, ranks(masks), starts):
        across = across + mask * (rank + start)
    place, twice = edge_places(row, count, patch)
    own = 4 * count * (1 - s % 2) + 2 * (count * odd + p) + s // 2
    inside = (patch >= 0.0) & (patch < 2.0 * count)
    index = jnp.where(inside, place.astype(jnp.float32) + twice, across)
    index = jnp.where(wall, own.astype(jnp.float32), index)
    lane = lane.astype(jnp.float32)
    hot = jnp.concatenate([flag(lane == index), flag(lane + side == index)], axis=1).astype(jnp.bfloat16)
    hot = jnp.concatenate([hot, hot], axis=1)
    fields = []
    for f in range(4):
        parts = edges_of_field(edges, f)
        parts += [ref[step * f : step * (f + 1), :] for ref in (crossed, passed)]
        parts.append(jnp.zeros((2 * side - first - 2 * step, side), jnp.float32))
        values = jnp.concatenate(parts, axis=0)
        high = values.astype(jnp.bfloat16)
        low = (values - high.astype(jnp.float32)).astype(jnp.bfloat16)
        fields.append(product(hot, jnp.concatenate([high, low], axis=0)))
    return fields, wall


def rim_terms(table, edges, crossed, passed, columns, lines, turn, me, odd):
    count = table.shape[0]
    outside, wall = ghosts(table, edges, crossed, passed, me, odd)
    turn[...] = jnp.zeros_like(turn)
    lines[...] = jnp.zeros_like(lines)
    for s in range(4):
        parity = 1 - s % 2
        sign = 1.0 - 2.0 * parity
        axis = s // 2
        normal, across = (1, 2) if axis == 0 else (2, 1)

        at = slice(count * s, count * (s + 1))

        def both(f):
            row = 8 * axis + 2 * f + parity
            return edges[pl.ds(16 * count * odd + row, count, stride=16), :], outside[f][at]

        hc, hg = both(0)
        nc, ng = both(normal)
        ng = jnp.where(wall[at], -ng, ng)
        ac, ag = both(across)
        bc, bg = both(3)
        rc, rg = lax.rsqrt(hc), lax.rsqrt(hg)
        uc, ug = nc * rc * rc, ng * rg * rg
        top = jnp.maximum(jnp.abs(uc) + hc * rc, jnp.abs(ug) + hg * rg)
        fc, fg = nc * uc + 0.5 * hc * hc, ng * ug + 0.5 * hg * hg
        c_h = -HALF * (sign * (nc + ng) - top * ((hg + bg) - (hc + bc)))
        c_n = -HALF * (sign * (fc + fg + hc * bg) - top * (ng - nc))
        c_t = -HALF * (sign * (ac * uc + ag * ug) - top * (ag - ac))
        for f, value in ((0, c_h), (normal, c_n), (across, c_t)):
            target = turn if axis == 0 else lines
            target[pl.ds(2 * f + parity, count, stride=8), :] = value
    turn[...] = jnp.transpose(turn[...])
    side = turn.shape[0]
    columns[...] = pieces(jnp.concatenate([turn[spread(j, side), :] for j in range(side // ROWS)], axis=0))


def fill_places(places):
    side = places.shape[0] // 2
    row = lax.broadcasted_iota(jnp.int32, (side, side), 0) % 8
    lane = lax.broadcasted_iota(jnp.int32, (side, side), 1)
    source = row - jnp.where(lane == 0, 1, jnp.where(lane == side - 1, 0, 1024))
    for f in range(3):
        block = jnp.where(source == 2 * f, 1.0, 0.0).astype(jnp.bfloat16)
        for half in range(2):
            places[half * side : (half + 1) * side, f * side : (f + 1) * side] = block


def final_kernel(
    margin, range_ref, table, edges, crossed, passed, own, theirs, arrived, out,
    result, turn, columns, lines, places, sems,
):
    count, side = own.shape[0], lines.shape[1]
    me, odd = position()
    even = odd == 0
    fill_places(places)
    rim_terms(table, edges, crossed, passed, columns, lines, turn, me, odd)
    start, stop = range_ref[0, 0], range_ref[0, 1]
    line = iota(0, side)
    lane = lax.broadcasted_iota(jnp.int32, (side, 2 * side), 1) % side
    steps = side // ROWS

    def copy(p):
        return pltpu.make_async_copy(result.at[p], out.at[p], sems.at[p])

    for group in range(0, count, margin):
        patches = range(group, group + margin)
        held = columns[...]
        masked = [held * jnp.where(lane // 8 == p, 1.0, 0.0).astype(jnp.bfloat16) for p in patches]
        terms = product(jnp.concatenate(masked, axis=0), places[...])
        for m, p in enumerate(patches):
            if group == 0:
                taken = me * count + p < start
            elif group == count - margin:
                taken = me * count + p >= stop
            else:
                taken = None
            near = even if group else odd == 1
            for f in range(3):
                for j in range(steps):
                    rows = slice(ROWS * j, ROWS * (j + 1))
                    value = own[p, f, rows, :]
                    if taken is not None:
                        moved = jnp.where(near, theirs[m, f, rows, :], arrived[m, f, rows, :])
                        value = jnp.where(taken, moved, value)
                    at = side * m + ROWS * j
                    value = value + terms[at : at + ROWS, f * side : (f + 1) * side]
                    if j == 0:
                        south = lines[8 * p + 2 * f + 1 : 8 * p + 2 * f + 2, :]
                        value = value + jnp.where(line == 0, south, 0.0)
                    if j == steps - 1:
                        north = lines[8 * p + 2 * f : 8 * p + 2 * f + 1, :]
                        value = value + jnp.where(line == ROWS - 1, north, 0.0)
                    result[p, f, spread(j, side), :] = value
            copy(p).start()
    for p in range(count):
        copy(p).wait()


def finished(old_range, table, edges, crossed, passed, own, theirs, arrived, margin):
    count, _, side, _ = own.shape
    return pl.pallas_call(
        functools.partial(final_kernel, margin),
        in_specs=[SMEM] + [VMEM] * 7,
        out_specs=HBM,
        out_shape=jax.ShapeDtypeStruct(own.shape, jnp.float32),
        scratch_shapes=[
            pltpu.VMEM(own.shape, jnp.float32),
            pltpu.VMEM((side, side), jnp.float32),
            pltpu.VMEM((side, 2 * side), jnp.bfloat16),
            pltpu.VMEM((side, side), jnp.float32),
            pltpu.VMEM((2 * side, 3 * side), jnp.bfloat16),
            pltpu.SemaphoreType.DMA((count,)),
        ],
        compiler_params=room(12),
        name="final",
    )(old_range, table, edges, crossed, passed, own, theirs, arrived)


def swapped(value, first):
    pairs = [(i, i + 1) for i in range(first, lax.axis_size(AXES) - 1, 2)]
    return lax.ppermute(value, AXES, pairs + [(j, i) for i, j in pairs])


def local(old_cells, old_range, neighbours):
    per_device = neighbours.shape[0]
    margin = (old_cells.shape[0] - per_device) // 2
    their_table = swapped(neighbours, 0)
    leaving, bundle = outer_patches(old_cells, neighbours, their_table, margin)
    came = swapped(bundle, 1)
    arrived = swapped(after(leaving, bundle), 1)
    shared, inner, own = home_patches(old_range, old_cells, came, margin, per_device)
    their_edges = swapped(shared, 0)
    theirs = swapped(inner, 0)
    edges, message = answers(old_range, shared, their_edges, came, margin, per_device)
    crossed = swapped(message, 1)
    passed = swapped(crossed, 0)
    return finished(old_range, neighbours, edges, crossed, passed, own, theirs, arrived, margin)


def solution(mesh):
    placed = (
        P(("member", "curve", "sub"), None, None, None),
        P(("member", "curve", "sub"), None),
        P(("member", "curve", "sub"), None),
    )
    return jax.shard_map(
        local,
        mesh=mesh,
        in_specs=placed,
        out_specs=P(("member", "curve", "sub"), None, None, None),
        check_vma=False,
    )
```

```python
import functools

import jax
import jax.numpy as jnp
from jax import lax
from jax.experimental import pallas as pl
from jax.experimental.pallas import tpu as pltpu
from jax.sharding import PartitionSpec as P

RATE_STEP = 0.1
HALF = 0.5 * RATE_STEP
AXES = ("curve", "sub")
CAP = 8
ROWS = 8
PAIR = 2
FIRST = 0
VMEM = pl.BlockSpec(memory_space=pltpu.VMEM)
SMEM = pl.BlockSpec(memory_space=pltpu.SMEM)
HBM = pl.BlockSpec(memory_space=pltpu.HBM)


def position():
    me = lax.axis_index(AXES)
    return me, lax.rem(me, 2)


def iota(axis, side):
    return lax.broadcasted_iota(jnp.int32, (ROWS, side), axis)


def spread(j, side):
    return pl.ds(j, ROWS, stride=side // ROWS)


def pieces(x):
    high = x.astype(jnp.bfloat16)
    low = (x - high.astype(jnp.float32)).astype(jnp.bfloat16)
    return jnp.concatenate([high, low], axis=1)


def product(parts, weights):
    return jnp.dot(parts, weights, preferred_element_type=jnp.float32)


AHEAD, EAST, SUMS, SLOPE = slice(0, 2), slice(2, 4), slice(4, 5), slice(5, 6)


def fill_weights(weights):
    side = weights.shape[0] // 2
    row = lax.broadcasted_iota(jnp.int32, (side, side), 0)
    lane = lax.broadcasted_iota(jnp.int32, (side, side), 1)
    one = lambda where: jnp.where(where, 1.0, 0.0)
    after, here, before = one(row == lane + 1), one(row == lane), one(row == lane - 1)
    inner_e, inner_w = lane != side - 1, lane != 0
    east = jnp.where(inner_e, after + here, 0.0)
    west = jnp.where(inner_w, here + before, 0.0)
    blocks = (
        after,
        before,
        jnp.where(inner_e, after - here, 0.0),
        jnp.where(inner_w, here - before, 0.0),
        east - west,
        after - before,
    )
    for n, block in enumerate(blocks):
        for half in range(2):
            weights[half * side : (half + 1) * side, n * side : (n + 1) * side] = block.astype(jnp.bfloat16)


def inner_update(loads, store, side, weights):
    line, lane = iota(0, side), iota(1, side)
    first, last = line == 0, line == ROWS - 1
    rim = jnp.where(lane == 0, 2.0, jnp.where(lane == side - 1, -2.0, 0.0))
    steps = side // ROWS
    many = len(loads)

    def cell(h, mx, my, bed):
        root = lax.rsqrt(h)
        celerity = h * root
        inverse = root * root
        u = mx * inverse
        v = my * inverse
        half_sq = 0.5 * h * h
        cross = my * u
        rate_y = jnp.abs(v) + celerity
        rate_x = jnp.abs(u) + celerity
        return (rate_y, h + bed, mx, my, cross, my * v + half_sq, bed), rate_x, mx * u + half_sq, h

    def face_y(low, high):
        top = jnp.maximum(low[0], high[0])
        return [
            (high[3] + low[3]) - top * (high[1] - low[1]),
            (high[4] + low[4]) - top * (high[2] - low[2]),
            (high[5] + low[5]) - top * (high[3] - low[3]),
        ]

    def taken(block):
        return weights[:, block.start * side : block.stop * side]

    cells = [cell(*[load(f, j) for f in range(4)]) for load in loads for j in range(steps)]
    stack = lambda pick: pieces(jnp.concatenate([pick(c) for c in cells], axis=0))
    eta, mx, my, cross, bed = (stack(lambda c, n=n: c[0][n]) for n in (1, 2, 3, 4, 6))
    fx = stack(lambda c: c[2])
    rates = product(stack(lambda c: c[1]), taken(AHEAD))
    jumps = product(jnp.concatenate([eta, mx, my], axis=0), taken(EAST))
    sums = product(jnp.concatenate([fx, cross], axis=0), taken(SUMS))
    slopes = product(bed, taken(SLOPE))
    for n in range(many):
        mine = cells[n * steps : (n + 1) * steps]
        low = [pltpu.roll(each, 1, 0) for each in mine[steps - 1][0]]
        faces = []
        for j in range(steps):
            faces.append(face_y(low, mine[j][0]))
            low = mine[j][0]
        faces[0] = [jnp.where(first, 0.0, each) for each in faces[0]]
        beds = [c[0][6] for c in mine]
        under = jnp.where(first, 0.0, pltpu.roll(beds[-1], 1, 0))
        over = jnp.where(last, 0.0, pltpu.roll(beds[0], ROWS - 1, 0))
        faces.append([jnp.where(last, 0.0, pltpu.roll(each, ROWS - 1, 0)) for each in faces[0]])
        for j in range(steps):
            (_, _, mx, my, _, _, _), rate, _, h = mine[j]
            at = [(q * many + n) * side + ROWS * j for q in range(3)]
            rows = [slice(r, r + ROWS) for r in at]
            top_e = jnp.maximum(rate, rates[rows[0], :side])
            top_w = jnp.maximum(rate, rates[rows[0], side:])
            total = [jumps[rows[1], :side] + jumps[rows[1], side:] + rim * mx, sums[rows[0]], sums[rows[1]]]
            x = [t - (top_e * jumps[r, :side] - top_w * jumps[r, side:]) for t, r in zip(total, rows)]
            south, north = faces[j], faces[j + 1]
            slope_y = (beds[j + 1] if j + 1 < steps else over) - (beds[j - 1] if j else under)
            store(n, 0, j, h - HALF * (x[0] + (north[0] - south[0])))
            store(n, 1, j, mx - HALF * (x[1] + h * slopes[rows[0]] + (north[1] - south[1])))
            store(n, 2, j, my - HALF * (x[2] + h * slope_y + (north[2] - south[2])))


def gather_columns(loads, columns, first_at, side):
    pair = iota(1, side) // 2
    for j in range(side // ROWS):
        held = columns[spread(j, side), :]
        for n, load in enumerate(loads):
            at = first_at + 8 * n
            for f in range(4):
                held = jnp.where(pair == at // 2 + f, pltpu.roll(load(f, j), at + 2 * f + 1, 1), held)
        columns[spread(j, side), :] = held


def take_edges(count, cells, slot_of, columns, edges, base):
    side = columns.shape[0]
    turned = jnp.transpose(columns[...])
    for p in range(count):
        edges[base + 16 * p : base + 16 * p + 8, :] = turned[8 * p : 8 * p + 8, :]
        for f in range(4):
            row = base + 16 * p + 8 + 2 * f
            edges[row : row + 1, :] = cells[slot_of(p), f, side - 1 : side, :]
            edges[row + 1 : row + 2, :] = cells[slot_of(p), f, 0:1, :]


def loader(cells, i):
    side = cells.shape[3]
    return lambda f, j: cells[i, f, spread(j, side), :]


def update(cells, first, many, weights, put):
    loads = [loader(cells, first + n) for n in range(many)]
    inner_update(loads, lambda n, f, j, value: put(n, f, ROWS * j, value), cells.shape[3], weights)


def fetch(cells_hbm, first, cells, sems, parts):
    def copy(i):
        return pltpu.make_async_copy(cells_hbm.at[first + i], cells.at[i], sems.at[i])

    for start, count in parts:
        for i in range(count):
            copy(start + i).start()
    return copy


def outer_slot(cells_hbm, margin):
    _, odd = position()
    return odd * (cells_hbm.shape[0] - margin)


def bundle_layout(margin):
    tables = 16 * margin
    return tables, tables + 16


def outer_kernel(margin, cells_hbm, table, rest, bundle, cells, columns, weights, sems):
    side = columns.shape[0]
    _, odd = position()
    copy = fetch(cells_hbm, outer_slot(cells_hbm, margin), cells, sems, [(0, margin)])
    fill_weights(weights)
    tables, results = bundle_layout(margin)
    sides, count = table.shape
    bundle[tables:results, :] = jnp.zeros((results - tables, side), jnp.float32)
    bundle[pl.ds(pl.multiple_of(tables + 8 * odd, 8), sides), 0:count] = table[...].astype(jnp.float32)
    for i in range(0, margin, PAIR):
        for n in range(PAIR):
            copy(i + n).wait()

        def put(n, f, row, value, i=i):
            if i + n < FIRST:
                at = results + (3 * (i + n) + f) * side + row
                bundle[at : at + ROWS, :] = value
            else:
                rest[i + n - FIRST, f, row : row + ROWS, :] = value

        gather_columns([loader(cells, i + n) for n in range(PAIR)], columns, 8 * i, side)
        update(cells, i, PAIR, weights, put)

    take_edges(margin, cells, lambda p: p, columns, bundle, 0)


def cost(patches, side):
    return pl.CostEstimate(flops=patches * side, bytes_accessed=patches * side, transcendentals=0)


def room(mebibytes):
    return pltpu.CompilerParams(vmem_limit_bytes=mebibytes << 20)


def outer_patches(old_cells, table, margin):
    side = old_cells.shape[3]
    return pl.pallas_call(
        functools.partial(outer_kernel, margin),
        in_specs=[HBM, VMEM],
        out_specs=[VMEM, VMEM],
        out_shape=[
            jax.ShapeDtypeStruct((margin - FIRST, 3, side, side), jnp.float32),
            jax.ShapeDtypeStruct((bundle_layout(margin)[1] + 3 * FIRST * side, side), jnp.float32),
        ],
        scratch_shapes=[
            pltpu.VMEM((margin, 4, side, side), jnp.float32),
            pltpu.VMEM((side, side), jnp.float32),
            pltpu.VMEM((2 * side, 6 * side), jnp.bfloat16),
            pltpu.SemaphoreType.DMA((margin,)),
        ],
        cost_estimate=cost(margin, side),
        compiler_params=room(48),
        name="outer",
    )(old_cells, table)


def placed_rows(rows, start_of, bundle, extra, name):
    any_place = pl.BlockSpec(memory_space=pl.ANY)
    small = rows == 8

    def kernel(bundle_ref, extra_ref, out_ref, held, sem):
        source = extra_ref
        if small:
            held[...] = jnp.zeros_like(held)
            held[0 : extra_ref.shape[0], 0 : extra_ref.shape[1]] = extra_ref[...].astype(jnp.float32)
            source = held
        start = pl.multiple_of(start_of(), 8)
        copy = pltpu.make_async_copy(source.at[pl.ds(0, rows), :], out_ref.at[pl.ds(start, rows), :], sem)
        copy.start()
        copy.wait()

    return pl.pallas_call(
        kernel,
        in_specs=[any_place, VMEM if small else any_place],
        out_specs=any_place,
        out_shape=jax.ShapeDtypeStruct(bundle.shape, bundle.dtype),
        scratch_shapes=[pltpu.VMEM((8, bundle.shape[1]), jnp.float32), pltpu.SemaphoreType.DMA],
        input_output_aliases={0: 0},
        compiler_params=room(4),
        name=name,
    )(bundle, extra)


def after(value, other):
    any_place = pl.BlockSpec(memory_space=pl.ANY)
    return pl.pallas_call(
        lambda value_ref, other_ref, out_ref: None,
        in_specs=[any_place, any_place],
        out_specs=any_place,
        out_shape=jax.ShapeDtypeStruct(value.shape, value.dtype),
        input_output_aliases={0: 0},
        compiler_params=room(4),
        name="after",
    )(value, other)


def layout(margin, per_device):
    home = 16 * margin
    limit = home + 16 * per_device
    brought = limit + 8
    return home, limit, brought, brought + 16 * margin


def home_kernel(margin, range_ref, cells_hbm, came, shared, inner, own, cells, columns, weights, sems):
    side = columns.shape[0]
    count = own.shape[0]
    home, limit, brought, total = layout(margin, count)
    _, odd = position()
    inner_at = (1 - odd) * count
    home_at = odd * margin
    parts = [(inner_at, margin), (home_at, count)]
    copy = fetch(cells_hbm, (1 - odd) * margin, cells, sems, parts)
    fill_weights(weights)

    for at, many, out, row in ((inner_at, margin, inner, 0), (home_at, count, own, home)):

        @pl.loop(0, many // PAIR)
        def _(step, at=at, out=out):
            i = step * PAIR
            for n in range(PAIR):
                copy(at + i + n).wait()

            def put(n, f, row, value):
                out[i + n, f, row : row + ROWS, :] = value

            gather_columns([loader(cells, at + i + n) for n in range(PAIR)], columns, 8 * i, side)
            update(cells, at + i, PAIR, weights, put)

        take_edges(many, cells, lambda p, at=at: at + p, columns, shared, row)

    outer_limit = jnp.where(odd == 1, range_ref[0, 1], range_ref[0, 0])
    shared[limit : limit + 8, :] = jnp.full((8, side), outer_limit, jnp.int32).astype(jnp.float32)
    shared[brought:total, :] = came[0 : total - brought, :]


def home_patches(old_range, old_cells, came, margin, per_device):
    side = old_cells.shape[3]
    total = layout(margin, per_device)[-1]
    return pl.pallas_call(
        functools.partial(home_kernel, margin),
        in_specs=[SMEM, HBM, VMEM],
        out_specs=[VMEM] * 3,
        out_shape=[
            jax.ShapeDtypeStruct((total, side), jnp.float32),
            jax.ShapeDtypeStruct((margin, 3, side, side), jnp.float32),
            jax.ShapeDtypeStruct((per_device, 3, side, side), jnp.float32),
        ],
        scratch_shapes=[
            pltpu.VMEM((margin + per_device, 4, side, side), jnp.float32),
            pltpu.VMEM((side, side), jnp.float32),
            pltpu.VMEM((2 * side, 6 * side), jnp.bfloat16),
            pltpu.SemaphoreType.DMA((margin + per_device,)),
        ],
        cost_estimate=cost(margin + per_device, side),
        compiler_params=room(48),
        name="home",
    )(old_range, old_cells, came)


def entries_of(table, sides, lanes):
    count = table.shape[0]
    return jnp.concatenate([jnp.broadcast_to(table[:, s : s + 1], (count, lanes)) for s in range(sides)], axis=0)


def grid_iota(rows, lanes, axis):
    return lax.broadcasted_iota(jnp.int32, (rows, lanes), axis)


def flag(where):
    return jnp.where(where, 1.0, 0.0)


def ranks(masks):
    rows, lanes = masks[0].shape
    earlier = flag(grid_iota(rows, lanes, 1) < grid_iota(rows, lanes, 0)).astype(jnp.bfloat16)
    stacked = jnp.concatenate(masks, axis=1).astype(jnp.bfloat16)
    if rows < lanes:
        stacked = jnp.concatenate([stacked, jnp.zeros((lanes - rows, stacked.shape[1]), jnp.bfloat16)], axis=0)
    counted = product(earlier, stacked)
    return [counted[:, n * lanes : (n + 1) * lanes] for n in range(len(masks))]


def edge_places(row, count, patch):
    s = row // count
    return 4 * count * (s % 2) + s // 2, 2.0 * patch


def edges_of_field(edges, f):
    tiles = edges.shape[0] // 8
    return [edges[pl.ds(2 * f + parity, tiles, stride=8), :] for parity in range(2)]


def answer_kernel(margin, count, range_ref, mine, theirs, came, edges, message):
    side = edges.shape[1]
    home, limit, brought, _ = layout(margin, count)
    inner = 0
    me, odd = position()
    start, stop = range_ref[0, 0], range_ref[0, 1]
    even = odd == 0
    at_me = pl.multiple_of(16 * count * odd, 16)
    at_them = pl.multiple_of(16 * count * (1 - odd), 16)
    edges[pl.ds(at_me, 16 * count), :] = mine[home : home + 16 * count, :]
    edges[pl.ds(at_them, 16 * count), :] = theirs[home : home + 16 * count, :]
    their_limit = theirs[limit : limit + 8, :]
    low, high = 0, count - margin
    for m in range(margin):
        l = jnp.where(even, high, low) + m
        g = me * count + l
        taken = jnp.where(even, g >= stop, g < start)
        to = pl.multiple_of(at_me + 16 * l, 16)
        from_pair = theirs[inner + 16 * m : inner + 16 * (m + 1), :]
        edges[pl.ds(to, 16), :] = jnp.where(taken, from_pair, edges[pl.ds(to, 16), :])
        l = jnp.where(even, low, high) + m
        g = (me + 1 - 2 * odd) * count + l
        taken = jnp.where(even, g < stop, g >= start)
        to = pl.multiple_of(at_them + 16 * l, 16)
        from_pair = mine[inner + 16 * m : inner + 16 * (m + 1), :]
        edges[pl.ds(to, 16), :] = jnp.where(taken, from_pair, edges[pl.ds(to, 16), :])
        l = jnp.where(even, low, high) + m
        g = me * count + l
        taken = jnp.where(even, g < start, g >= stop)
        to = pl.multiple_of(at_me + 16 * l, 16)
        crossed = mine[brought + 16 * m : brought + 16 * (m + 1), :]
        edges[pl.ds(to, 16), :] = jnp.where(taken, crossed, edges[pl.ds(to, 16), :])
        l = jnp.where(even, high, low) + m
        g = ((me + 1 - 2 * odd) * count + l).astype(jnp.float32)
        to = pl.multiple_of(at_them + 16 * l, 16)
        taken = jnp.where(even, g - their_limit, their_limit - g - 1.0) >= 0.0
        for half in range(2):
            crossed = theirs[brought + 16 * m + 8 * half : brought + 16 * m + 8 * half + 8, :]
            at = pl.multiple_of(to + 8 * half, 8)
            edges[pl.ds(at, 8), :] = jnp.where(taken, crossed, edges[pl.ds(at, 8), :])
    sides, total = 4, 8 * count
    row = grid_iota(total, side, 0)
    lane = grid_iota(total, side, 1)
    which, within = row // (sides * count), row % (sides * count)
    at = 16 * margin
    turned = jnp.transpose(jnp.concatenate([came[at : at + 16, :], jnp.zeros((side - 16, side), jnp.float32)], axis=0))
    tables = [turned[0:count, 8 * n : 8 * n + sides] for n in range(2)]
    listed = jnp.concatenate([entries_of(table, sides, side) for table in tables], axis=0)
    patch = listed - (2 * count * (me // 2)).astype(jnp.float32)
    held = [(patch >= n * count) & (patch < (n + 1) * count) for n in range(2)]
    masks = [
        flag((which == 0) & held[0]),
        jnp.where(even, flag((which == 1) & held[0]), flag((which == 0) & held[1])),
        flag((which == 1) & held[1]),
    ]
    chosen = jnp.zeros((total, side), jnp.float32)
    for k, (mask, rank) in enumerate(zip(masks, ranks(masks))):
        slot = (lane - k * CAP).astype(jnp.float32)
        chosen = chosen + jnp.where((lane // CAP == k) & (rank == slot), mask, 0.0)
    place, twice = edge_places(within, count, patch)
    hot = flag(lane.astype(jnp.float32) == place.astype(jnp.float32) + twice).astype(jnp.bfloat16)
    slots = jnp.transpose(chosen)[0:32, :].astype(jnp.bfloat16)
    picked = product(slots, hot).astype(jnp.bfloat16)
    picked = jnp.concatenate([picked] * 3, axis=1)
    for f in range(4):
        values = jnp.concatenate(edges_of_field(edges, f), axis=0)
        high = values.astype(jnp.bfloat16)
        left = values - high.astype(jnp.float32)
        mid = left.astype(jnp.bfloat16)
        low = (left - mid.astype(jnp.float32)).astype(jnp.bfloat16)
        taken = product(picked, jnp.concatenate([high, mid, low], axis=0))
        message[3 * CAP * f : 3 * CAP * (f + 1), :] = taken[0 : 3 * CAP, :]


def answers(old_range, mine, theirs, came, margin, per_device):
    side = mine.shape[1]
    return pl.pallas_call(
        functools.partial(answer_kernel, margin, per_device),
        in_specs=[SMEM, VMEM, VMEM, VMEM],
        out_specs=[VMEM, VMEM],
        out_shape=[
            jax.ShapeDtypeStruct((32 * per_device, side), jnp.float32),
            jax.ShapeDtypeStruct((12 * CAP, side), jnp.float32),
        ],
        compiler_params=room(4),
        name="answers",
    )(old_range, mine, theirs, came)


def ghosts(table, edges, crossed, passed, turn, me, odd):
    sides, count = table.shape
    side = edges.shape[1]
    total = sides * count
    even = odd == 0
    row, lane = grid_iota(total, side, 0), grid_iota(total, side, 1)
    s, p = row // count, row % count
    turn[...] = jnp.zeros_like(turn)
    turn[0:sides, 0:count] = table[...].astype(jnp.float32)
    listed = entries_of(jnp.transpose(turn[...])[0:count, :], sides, side)
    wall = listed < 0.0
    patch = listed - (2 * count * (me // 2)).astype(jnp.float32)
    distance = listed - (count * me).astype(jnp.float32)
    first = 4 * count * 2
    step = 3 * CAP
    lists = (
        (-2, -2, first, first + step + 2 * CAP),
        (-1, 1, first + CAP, first + CAP),
        (2, 2, first + step, first + 2 * CAP),
    )
    masks, starts = [], []
    for far_even, far_odd, at_even, at_odd in lists:
        low = (count * jnp.where(even, far_even, far_odd)).astype(jnp.float32)
        masks.append(flag(~wall & (distance >= low) & (distance < low + count)))
        starts.append(jnp.where(even, at_even, at_odd).astype(jnp.float32))
    across = jnp.zeros((total, side), jnp.float32)
    for mask, rank, start in zip(masks, ranks(masks), starts):
        across = across + mask * (rank + start)
    place, twice = edge_places(row, count, patch)
    own = 4 * count * (1 - s % 2) + 2 * (count * odd + p) + s // 2
    inside = (patch >= 0.0) & (patch < 2.0 * count)
    index = jnp.where(inside, place.astype(jnp.float32) + twice, across)
    index = jnp.where(wall, own.astype(jnp.float32), index)
    lane = lane.astype(jnp.float32)
    hot = jnp.concatenate([flag(lane == index), flag(lane + side == index)], axis=1).astype(jnp.bfloat16)
    hot = jnp.concatenate([hot, hot], axis=1)
    fields = []
    for f in range(4):
        parts = edges_of_field(edges, f)
        parts += [ref[step * f : step * (f + 1), :] for ref in (crossed, passed)]
        parts.append(jnp.zeros((2 * side - first - 2 * step, side), jnp.float32))
        values = jnp.concatenate(parts, axis=0)
        high = values.astype(jnp.bfloat16)
        low = (values - high.astype(jnp.float32)).astype(jnp.bfloat16)
        fields.append(product(hot, jnp.concatenate([high, low], axis=0)))
    return fields, wall


def rim_terms(table, edges, crossed, passed, columns, lines, turn, me, odd):
    count = table.shape[1]
    outside, wall = ghosts(table, edges, crossed, passed, turn, me, odd)
    turn[...] = jnp.zeros_like(turn)
    lines[...] = jnp.zeros_like(lines)
    for s in range(4):
        parity = 1 - s % 2
        sign = 1.0 - 2.0 * parity
        axis = s // 2
        normal, across = (1, 2) if axis == 0 else (2, 1)

        at = slice(count * s, count * (s + 1))

        def both(f):
            row = 8 * axis + 2 * f + parity
            return edges[pl.ds(16 * count * odd + row, count, stride=16), :], outside[f][at]

        hc, hg = both(0)
        nc, ng = both(normal)
        ng = jnp.where(wall[at], -ng, ng)
        ac, ag = both(across)
        bc, bg = both(3)
        rc, rg = lax.rsqrt(hc), lax.rsqrt(hg)
        uc, ug = nc * rc * rc, ng * rg * rg
        top = jnp.maximum(jnp.abs(uc) + hc * rc, jnp.abs(ug) + hg * rg)
        fc, fg = nc * uc + 0.5 * hc * hc, ng * ug + 0.5 * hg * hg
        c_h = -HALF * (sign * (nc + ng) - top * ((hg + bg) - (hc + bc)))
        c_n = -HALF * (sign * (fc + fg + hc * bg) - top * (ng - nc))
        c_t = -HALF * (sign * (ac * uc + ag * ug) - top * (ag - ac))
        for f, value in ((0, c_h), (normal, c_n), (across, c_t)):
            target = turn if axis == 0 else lines
            target[pl.ds(2 * f + parity, count, stride=8), :] = value
    turn[...] = jnp.transpose(turn[...])
    side = turn.shape[0]
    columns[...] = pieces(jnp.concatenate([turn[spread(j, side), :] for j in range(side // ROWS)], axis=0))


def fill_places(places):
    side = places.shape[0] // 2
    row = lax.broadcasted_iota(jnp.int32, (side, side), 0) % 8
    lane = lax.broadcasted_iota(jnp.int32, (side, side), 1)
    source = row - jnp.where(lane == 0, 1, jnp.where(lane == side - 1, 0, 1024))
    for f in range(3):
        block = jnp.where(source == 2 * f, 1.0, 0.0).astype(jnp.bfloat16)
        for half in range(2):
            places[half * side : (half + 1) * side, f * side : (f + 1) * side] = block


def final_kernel(
    margin, range_ref, table, edges, crossed, passed, own, theirs, came, arrived, out,
    result, turn, columns, lines, places, sems,
):
    count, side = own.shape[0], lines.shape[1]
    me, odd = position()
    even = odd == 0
    fill_places(places)
    rim_terms(table, edges, crossed, passed, columns, lines, turn, me, odd)
    start, stop = range_ref[0, 0], range_ref[0, 1]
    line = iota(0, side)
    lane = lax.broadcasted_iota(jnp.int32, (side, 2 * side), 1) % side
    steps = side // ROWS
    results = bundle_layout(margin)[1]

    def copy(p):
        return pltpu.make_async_copy(result.at[p], out.at[p], sems.at[p])

    for group in range(0, count, margin):
        patches = range(group, group + margin)
        held = columns[...]
        masked = [held * jnp.where(lane // 8 == p, 1.0, 0.0).astype(jnp.bfloat16) for p in patches]
        terms = product(jnp.concatenate(masked, axis=0), places[...])
        for m, p in enumerate(patches):
            if group == 0:
                taken = me * count + p < start
            elif group == count - margin:
                taken = me * count + p >= stop
            else:
                taken = None
            near = even if group else odd == 1
            for f in range(3):
                for j in range(steps):
                    rows = slice(ROWS * j, ROWS * (j + 1))
                    value = own[p, f, rows, :]
                    if taken is not None:
                        if m < FIRST:
                            at = results + (3 * m + f) * side + ROWS * j
                            crossing = came[at : at + ROWS, :]
                        else:
                            crossing = arrived[m - FIRST, f, rows, :]
                        moved = jnp.where(near, theirs[m, f, rows, :], crossing)
                        value = jnp.where(taken, moved, value)
                    at = side * m + ROWS * j
                    value = value + terms[at : at + ROWS, f * side : (f + 1) * side]
                    if j == 0:
                        south = lines[8 * p + 2 * f + 1 : 8 * p + 2 * f + 2, :]
                        value = value + jnp.where(line == 0, south, 0.0)
                    if j == steps - 1:
                        north = lines[8 * p + 2 * f : 8 * p + 2 * f + 1, :]
                        value = value + jnp.where(line == ROWS - 1, north, 0.0)
                    result[p, f, spread(j, side), :] = value
            copy(p).start()
    for p in range(count):
        copy(p).wait()


def finished(old_range, table, edges, crossed, passed, own, theirs, came, arrived, margin):
    count, _, side, _ = own.shape
    return pl.pallas_call(
        functools.partial(final_kernel, margin),
        in_specs=[SMEM] + [VMEM] * 8,
        out_specs=HBM,
        out_shape=jax.ShapeDtypeStruct(own.shape, jnp.float32),
        scratch_shapes=[
            pltpu.VMEM(own.shape, jnp.float32),
            pltpu.VMEM((side, side), jnp.float32),
            pltpu.VMEM((side, 2 * side), jnp.bfloat16),
            pltpu.VMEM((side, side), jnp.float32),
            pltpu.VMEM((2 * side, 3 * side), jnp.bfloat16),
            pltpu.SemaphoreType.DMA((count,)),
        ],
        compiler_params=room(12),
        name="final",
    )(old_range, table, edges, crossed, passed, own, theirs, came, arrived)


def swapped(value, first):
    pairs = [(i, i + 1) for i in range(first, lax.axis_size(AXES) - 1, 2)]
    return lax.ppermute(value, AXES, pairs + [(j, i) for i, j in pairs])


def local(old_cells, old_range, neighbours):
    per_device = neighbours.shape[0]
    margin = (old_cells.shape[0] - per_device) // 2
    table = neighbours.T
    their_table = swapped(table, 0)
    rest, bundle = outer_patches(old_cells, table, margin)
    their_row = lambda: bundle_layout(margin)[0] + 8 * (1 - position()[1])
    bundle = placed_rows(8, their_row, bundle, their_table, "tables")
    came = swapped(bundle, 1)
    arrived = swapped(after(rest, bundle), 1)
    shared, inner, own = home_patches(old_range, old_cells, came, margin, per_device)
    their_edges = swapped(shared, 0)
    theirs = swapped(after(inner, their_edges), 0)
    edges, message = answers(old_range, shared, their_edges, came, margin, per_device)
    crossed = swapped(message, 1)
    passed = swapped(crossed, 0)
    return finished(old_range, table, edges, crossed, passed, own, theirs, came, arrived, margin)


def solution(mesh):
    placed = (
        P(("member", "curve", "sub"), None, None, None),
        P(("member", "curve", "sub"), None),
        P(("member", "curve", "sub"), None),
    )
    return jax.shard_map(
        local,
        mesh=mesh,
        in_specs=placed,
        out_specs=P(("member", "curve", "sub"), None, None, None),
        check_vma=False,
    )
```

```python
import functools

import jax
import jax.numpy as jnp
from jax import lax
from jax.experimental import pallas as pl
from jax.experimental.pallas import tpu as pltpu
from jax.sharding import PartitionSpec as P

RATE_STEP = 0.1
HALF = 0.5 * RATE_STEP
AXES = ("curve", "sub")
CAP = 8
ROWS = 8
PAIR = 2
FIRST = 0
VMEM = pl.BlockSpec(memory_space=pltpu.VMEM)
SMEM = pl.BlockSpec(memory_space=pltpu.SMEM)
HBM = pl.BlockSpec(memory_space=pltpu.HBM)


def position():
    me = lax.axis_index(AXES)
    return me, lax.rem(me, 2)


def iota(axis, side):
    return lax.broadcasted_iota(jnp.int32, (ROWS, side), axis)


def spread(j, side):
    return pl.ds(j, ROWS, stride=side // ROWS)


def pieces(x):
    high = x.astype(jnp.bfloat16)
    low = (x - high.astype(jnp.float32)).astype(jnp.bfloat16)
    return jnp.concatenate([high, low], axis=1)


def product(parts, weights):
    return jnp.dot(parts, weights, preferred_element_type=jnp.float32)


AHEAD, EAST, SUMS, SLOPE = slice(0, 2), slice(2, 4), slice(4, 5), slice(5, 6)


def fill_weights(weights):
    side = weights.shape[0] // 2
    row = lax.broadcasted_iota(jnp.int32, (side, side), 0)
    lane = lax.broadcasted_iota(jnp.int32, (side, side), 1)
    one = lambda where: jnp.where(where, 1.0, 0.0)
    after, here, before = one(row == lane + 1), one(row == lane), one(row == lane - 1)
    inner_e, inner_w = lane != side - 1, lane != 0
    east = jnp.where(inner_e, after + here, 0.0)
    west = jnp.where(inner_w, here + before, 0.0)
    blocks = (
        after,
        before,
        jnp.where(inner_e, after - here, 0.0),
        jnp.where(inner_w, here - before, 0.0),
        east - west,
        after - before,
    )
    for n, block in enumerate(blocks):
        for half in range(2):
            weights[half * side : (half + 1) * side, n * side : (n + 1) * side] = block.astype(jnp.bfloat16)


def inner_update(loads, store, side, weights):
    line, lane = iota(0, side), iota(1, side)
    first, last = line == 0, line == ROWS - 1
    rim = jnp.where(lane == 0, 2.0, jnp.where(lane == side - 1, -2.0, 0.0))
    steps = side // ROWS
    many = len(loads)

    def cell(h, mx, my, bed):
        root = lax.rsqrt(h)
        celerity = h * root
        inverse = root * root
        u = mx * inverse
        v = my * inverse
        half_sq = 0.5 * h * h
        cross = my * u
        rate_y = jnp.abs(v) + celerity
        rate_x = jnp.abs(u) + celerity
        return (rate_y, h + bed, mx, my, cross, my * v + half_sq, bed), rate_x, mx * u + half_sq, h

    def face_y(low, high):
        top = jnp.maximum(low[0], high[0])
        return [
            (high[3] + low[3]) - top * (high[1] - low[1]),
            (high[4] + low[4]) - top * (high[2] - low[2]),
            (high[5] + low[5]) - top * (high[3] - low[3]),
        ]

    def taken(block):
        return weights[:, block.start * side : block.stop * side]

    cells = [cell(*[load(f, j) for f in range(4)]) for load in loads for j in range(steps)]
    stack = lambda pick: pieces(jnp.concatenate([pick(c) for c in cells], axis=0))
    eta, mx, my, cross, bed = (stack(lambda c, n=n: c[0][n]) for n in (1, 2, 3, 4, 6))
    fx = stack(lambda c: c[2])
    rates = product(stack(lambda c: c[1]), taken(AHEAD))
    jumps = product(jnp.concatenate([eta, mx, my], axis=0), taken(EAST))
    sums = product(jnp.concatenate([fx, cross], axis=0), taken(SUMS))
    slopes = product(bed, taken(SLOPE))
    for n in range(many):
        mine = cells[n * steps : (n + 1) * steps]
        low = [pltpu.roll(each, 1, 0) for each in mine[steps - 1][0]]
        faces = []
        for j in range(steps):
            faces.append(face_y(low, mine[j][0]))
            low = mine[j][0]
        faces[0] = [jnp.where(first, 0.0, each) for each in faces[0]]
        beds = [c[0][6] for c in mine]
        under = jnp.where(first, 0.0, pltpu.roll(beds[-1], 1, 0))
        over = jnp.where(last, 0.0, pltpu.roll(beds[0], ROWS - 1, 0))
        faces.append([jnp.where(last, 0.0, pltpu.roll(each, ROWS - 1, 0)) for each in faces[0]])
        for j in range(steps):
            (_, _, mx, my, _, _, _), rate, _, h = mine[j]
            at = [(q * many + n) * side + ROWS * j for q in range(3)]
            rows = [slice(r, r + ROWS) for r in at]
            top_e = jnp.maximum(rate, rates[rows[0], :side])
            top_w = jnp.maximum(rate, rates[rows[0], side:])
            total = [jumps[rows[1], :side] + jumps[rows[1], side:] + rim * mx, sums[rows[0]], sums[rows[1]]]
            x = [t - (top_e * jumps[r, :side] - top_w * jumps[r, side:]) for t, r in zip(total, rows)]
            south, north = faces[j], faces[j + 1]
            slope_y = (beds[j + 1] if j + 1 < steps else over) - (beds[j - 1] if j else under)
            store(n, 0, j, h - HALF * (x[0] + (north[0] - south[0])))
            store(n, 1, j, mx - HALF * (x[1] + h * slopes[rows[0]] + (north[1] - south[1])))
            store(n, 2, j, my - HALF * (x[2] + h * slope_y + (north[2] - south[2])))


def gather_columns(loads, columns, first_at, side):
    pair = iota(1, side) // 2
    for j in range(side // ROWS):
        held = columns[spread(j, side), :]
        for n, load in enumerate(loads):
            at = first_at + 8 * n
            for f in range(4):
                held = jnp.where(pair == at // 2 + f, pltpu.roll(load(f, j), at + 2 * f + 1, 1), held)
        columns[spread(j, side), :] = held


def take_edges(count, cells, slot_of, columns, edges, base):
    side = columns.shape[0]
    turned = jnp.transpose(columns[...])
    for p in range(count):
        edges[base + 16 * p : base + 16 * p + 8, :] = turned[8 * p : 8 * p + 8, :]
        for f in range(4):
            row = base + 16 * p + 8 + 2 * f
            edges[row : row + 1, :] = cells[slot_of(p), f, side - 1 : side, :]
            edges[row + 1 : row + 2, :] = cells[slot_of(p), f, 0:1, :]


def loader(cells, i):
    side = cells.shape[3]
    return lambda f, j: cells[i, f, spread(j, side), :]


def update(cells, first, many, weights, put):
    loads = [loader(cells, first + n) for n in range(many)]
    inner_update(loads, lambda n, f, j, value: put(n, f, ROWS * j, value), cells.shape[3], weights)


def fetch(cells_hbm, first, cells, sems, parts):
    def copy(i):
        return pltpu.make_async_copy(cells_hbm.at[first + i], cells.at[i], sems.at[i])

    for start, count in parts:
        for i in range(count):
            copy(start + i).start()
    return copy


def outer_slot(cells_hbm, margin):
    _, odd = position()
    return odd * (cells_hbm.shape[0] - margin)


def bundle_layout(margin):
    tables = 16 * margin
    return tables, tables + 16


def outer_kernel(margin, cells_hbm, table, rest, bundle, cells, columns, weights, sems):
    side = columns.shape[0]
    _, odd = position()
    copy = fetch(cells_hbm, outer_slot(cells_hbm, margin), cells, sems, [(0, margin)])
    fill_weights(weights)
    tables, results = bundle_layout(margin)
    sides, count = table.shape
    bundle[tables:results, :] = jnp.zeros((results - tables, side), jnp.float32)
    bundle[pl.ds(pl.multiple_of(tables + 8 * odd, 8), sides), 0:count] = table[...].astype(jnp.float32)
    for i in range(0, margin, PAIR):
        for n in range(PAIR):
            copy(i + n).wait()

        def put(n, f, row, value, i=i):
            if i + n < FIRST:
                at = results + (3 * (i + n) + f) * side + row
                bundle[at : at + ROWS, :] = value
            else:
                rest[i + n - FIRST, f, row : row + ROWS, :] = value

        gather_columns([loader(cells, i + n) for n in range(PAIR)], columns, 8 * i, side)
        update(cells, i, PAIR, weights, put)

    take_edges(margin, cells, lambda p: p, columns, bundle, 0)


def cost(patches, side):
    return pl.CostEstimate(
        flops=patches * side * side * 800,
        bytes_accessed=patches * side * side * 28,
        transcendentals=patches * side * side,
    )


def room(mebibytes):
    return pltpu.CompilerParams(vmem_limit_bytes=mebibytes << 20)


def outer_patches(old_cells, table, margin):
    side = old_cells.shape[3]
    return pl.pallas_call(
        functools.partial(outer_kernel, margin),
        in_specs=[HBM, VMEM],
        out_specs=[VMEM, VMEM],
        out_shape=[
            jax.ShapeDtypeStruct((margin - FIRST, 3, side, side), jnp.float32),
            jax.ShapeDtypeStruct((bundle_layout(margin)[1] + 3 * FIRST * side, side), jnp.float32),
        ],
        scratch_shapes=[
            pltpu.VMEM((margin, 4, side, side), jnp.float32),
            pltpu.VMEM((side, side), jnp.float32),
            pltpu.VMEM((2 * side, 6 * side), jnp.bfloat16),
            pltpu.SemaphoreType.DMA((margin,)),
        ],
        cost_estimate=cost(margin, side),
        compiler_params=room(48),
        name="outer",
    )(old_cells, table)


def placed_rows(rows, start_of, bundle, extra, name):
    any_place = pl.BlockSpec(memory_space=pl.ANY)
    small = rows == 8

    def kernel(bundle_ref, extra_ref, out_ref, held, sem):
        source = extra_ref
        if small:
            held[...] = jnp.zeros_like(held)
            held[0 : extra_ref.shape[0], 0 : extra_ref.shape[1]] = extra_ref[...].astype(jnp.float32)
            source = held
        start = pl.multiple_of(start_of(), 8)
        copy = pltpu.make_async_copy(source.at[pl.ds(0, rows), :], out_ref.at[pl.ds(start, rows), :], sem)
        copy.start()
        copy.wait()

    return pl.pallas_call(
        kernel,
        in_specs=[any_place, VMEM if small else any_place],
        out_specs=any_place,
        out_shape=jax.ShapeDtypeStruct(bundle.shape, bundle.dtype),
        scratch_shapes=[pltpu.VMEM((8, bundle.shape[1]), jnp.float32), pltpu.SemaphoreType.DMA],
        input_output_aliases={0: 0},
        compiler_params=room(4),
        name=name,
    )(bundle, extra)


def after(value, other):
    any_place = pl.BlockSpec(memory_space=pl.ANY)
    return pl.pallas_call(
        lambda value_ref, other_ref, out_ref: None,
        in_specs=[any_place, any_place],
        out_specs=any_place,
        out_shape=jax.ShapeDtypeStruct(value.shape, value.dtype),
        input_output_aliases={0: 0},
        compiler_params=room(4),
        name="after",
    )(value, other)


def layout(margin, per_device):
    home = 16 * margin
    limit = home + 16 * per_device
    brought = limit + 8
    return home, limit, brought, brought + 16 * margin


def home_kernel(margin, range_ref, cells_hbm, came, shared, inner, own, cells, columns, weights, sems):
    side = columns.shape[0]
    count = own.shape[0]
    home, limit, brought, total = layout(margin, count)
    _, odd = position()
    inner_at = (1 - odd) * count
    home_at = odd * margin
    parts = [(inner_at, margin), (home_at, count)]
    copy = fetch(cells_hbm, (1 - odd) * margin, cells, sems, parts)
    fill_weights(weights)

    for at, many, out, row in ((inner_at, margin, inner, 0), (home_at, count, own, home)):

        @pl.loop(0, many // PAIR)
        def _(step, at=at, out=out):
            i = step * PAIR
            for n in range(PAIR):
                copy(at + i + n).wait()

            def put(n, f, row, value):
                out[i + n, f, row : row + ROWS, :] = value

            gather_columns([loader(cells, at + i + n) for n in range(PAIR)], columns, 8 * i, side)
            update(cells, at + i, PAIR, weights, put)

        take_edges(many, cells, lambda p, at=at: at + p, columns, shared, row)

    outer_limit = jnp.where(odd == 1, range_ref[0, 1], range_ref[0, 0])
    shared[limit : limit + 8, :] = jnp.full((8, side), outer_limit, jnp.int32).astype(jnp.float32)
    shared[brought:total, :] = came[0 : total - brought, :]


def home_patches(old_range, old_cells, came, margin, per_device):
    side = old_cells.shape[3]
    total = layout(margin, per_device)[-1]
    return pl.pallas_call(
        functools.partial(home_kernel, margin),
        in_specs=[SMEM, HBM, VMEM],
        out_specs=[VMEM] * 3,
        out_shape=[
            jax.ShapeDtypeStruct((total, side), jnp.float32),
            jax.ShapeDtypeStruct((margin, 3, side, side), jnp.float32),
            jax.ShapeDtypeStruct((per_device, 3, side, side), jnp.float32),
        ],
        scratch_shapes=[
            pltpu.VMEM((margin + per_device, 4, side, side), jnp.float32),
            pltpu.VMEM((side, side), jnp.float32),
            pltpu.VMEM((2 * side, 6 * side), jnp.bfloat16),
            pltpu.SemaphoreType.DMA((margin + per_device,)),
        ],
        cost_estimate=cost(margin + per_device, side),
        compiler_params=room(48),
        name="home",
    )(old_range, old_cells, came)


def entries_of(table, sides, lanes):
    count = table.shape[0]
    return jnp.concatenate([jnp.broadcast_to(table[:, s : s + 1], (count, lanes)) for s in range(sides)], axis=0)


def grid_iota(rows, lanes, axis):
    return lax.broadcasted_iota(jnp.int32, (rows, lanes), axis)


def flag(where):
    return jnp.where(where, 1.0, 0.0)


def ranks(masks):
    rows, lanes = masks[0].shape
    earlier = flag(grid_iota(rows, lanes, 1) < grid_iota(rows, lanes, 0)).astype(jnp.bfloat16)
    stacked = jnp.concatenate(masks, axis=1).astype(jnp.bfloat16)
    if rows < lanes:
        stacked = jnp.concatenate([stacked, jnp.zeros((lanes - rows, stacked.shape[1]), jnp.bfloat16)], axis=0)
    counted = product(earlier, stacked)
    return [counted[:, n * lanes : (n + 1) * lanes] for n in range(len(masks))]


def edge_places(row, count, patch):
    s = row // count
    return 4 * count * (s % 2) + s // 2, 2.0 * patch


def edges_of_field(edges, f):
    tiles = edges.shape[0] // 8
    return [edges[pl.ds(2 * f + parity, tiles, stride=8), :] for parity in range(2)]


def answer_kernel(margin, count, range_ref, mine, theirs, came, edges, message):
    side = edges.shape[1]
    home, limit, brought, _ = layout(margin, count)
    inner = 0
    me, odd = position()
    start, stop = range_ref[0, 0], range_ref[0, 1]
    even = odd == 0
    at_me = pl.multiple_of(16 * count * odd, 16)
    at_them = pl.multiple_of(16 * count * (1 - odd), 16)
    edges[pl.ds(at_me, 16 * count), :] = mine[home : home + 16 * count, :]
    edges[pl.ds(at_them, 16 * count), :] = theirs[home : home + 16 * count, :]
    their_limit = theirs[limit : limit + 8, :]
    low, high = 0, count - margin
    for m in range(margin):
        l = jnp.where(even, high, low) + m
        g = me * count + l
        taken = jnp.where(even, g >= stop, g < start)
        to = pl.multiple_of(at_me + 16 * l, 16)
        from_pair = theirs[inner + 16 * m : inner + 16 * (m + 1), :]
        edges[pl.ds(to, 16), :] = jnp.where(taken, from_pair, edges[pl.ds(to, 16), :])
        l = jnp.where(even, low, high) + m
        g = (me + 1 - 2 * odd) * count + l
        taken = jnp.where(even, g < stop, g >= start)
        to = pl.multiple_of(at_them + 16 * l, 16)
        from_pair = mine[inner + 16 * m : inner + 16 * (m + 1), :]
        edges[pl.ds(to, 16), :] = jnp.where(taken, from_pair, edges[pl.ds(to, 16), :])
        l = jnp.where(even, low, high) + m
        g = me * count + l
        taken = jnp.where(even, g < start, g >= stop)
        to = pl.multiple_of(at_me + 16 * l, 16)
        crossed = mine[brought + 16 * m : brought + 16 * (m + 1), :]
        edges[pl.ds(to, 16), :] = jnp.where(taken, crossed, edges[pl.ds(to, 16), :])
        l = jnp.where(even, high, low) + m
        g = ((me + 1 - 2 * odd) * count + l).astype(jnp.float32)
        to = pl.multiple_of(at_them + 16 * l, 16)
        taken = jnp.where(even, g - their_limit, their_limit - g - 1.0) >= 0.0
        for half in range(2):
            crossed = theirs[brought + 16 * m + 8 * half : brought + 16 * m + 8 * half + 8, :]
            at = pl.multiple_of(to + 8 * half, 8)
            edges[pl.ds(at, 8), :] = jnp.where(taken, crossed, edges[pl.ds(at, 8), :])
    sides, total = 4, 8 * count
    row = grid_iota(total, side, 0)
    lane = grid_iota(total, side, 1)
    which, within = row // (sides * count), row % (sides * count)
    at = 16 * margin
    turned = jnp.transpose(jnp.concatenate([came[at : at + 16, :], jnp.zeros((side - 16, side), jnp.float32)], axis=0))
    tables = [turned[0:count, 8 * n : 8 * n + sides] for n in range(2)]
    listed = jnp.concatenate([entries_of(table, sides, side) for table in tables], axis=0)
    patch = listed - (2 * count * (me // 2)).astype(jnp.float32)
    held = [(patch >= n * count) & (patch < (n + 1) * count) for n in range(2)]
    masks = [
        flag((which == 0) & held[0]),
        jnp.where(even, flag((which == 1) & held[0]), flag((which == 0) & held[1])),
        flag((which == 1) & held[1]),
    ]
    chosen = jnp.zeros((total, side), jnp.float32)
    for k, (mask, rank) in enumerate(zip(masks, ranks(masks))):
        slot = (lane - k * CAP).astype(jnp.float32)
        chosen = chosen + jnp.where((lane // CAP == k) & (rank == slot), mask, 0.0)
    place, twice = edge_places(within, count, patch)
    hot = flag(lane.astype(jnp.float32) == place.astype(jnp.float32) + twice).astype(jnp.bfloat16)
    slots = jnp.transpose(chosen)[0:32, :].astype(jnp.bfloat16)
    picked = product(slots, hot).astype(jnp.bfloat16)
    picked = jnp.concatenate([picked] * 3, axis=1)
    for f in range(4):
        values = jnp.concatenate(edges_of_field(edges, f), axis=0)
        high = values.astype(jnp.bfloat16)
        left = values - high.astype(jnp.float32)
        mid = left.astype(jnp.bfloat16)
        low = (left - mid.astype(jnp.float32)).astype(jnp.bfloat16)
        taken = product(picked, jnp.concatenate([high, mid, low], axis=0))
        message[3 * CAP * f : 3 * CAP * (f + 1), :] = taken[0 : 3 * CAP, :]


def answers(old_range, mine, theirs, came, margin, per_device):
    side = mine.shape[1]
    return pl.pallas_call(
        functools.partial(answer_kernel, margin, per_device),
        in_specs=[SMEM, VMEM, VMEM, VMEM],
        out_specs=[VMEM, VMEM],
        out_shape=[
            jax.ShapeDtypeStruct((32 * per_device, side), jnp.float32),
            jax.ShapeDtypeStruct((12 * CAP, side), jnp.float32),
        ],
        compiler_params=room(4),
        name="answers",
    )(old_range, mine, theirs, came)


def ghosts(table, edges, crossed, passed, turn, me, odd):
    sides, count = table.shape
    side = edges.shape[1]
    total = sides * count
    even = odd == 0
    row, lane = grid_iota(total, side, 0), grid_iota(total, side, 1)
    s, p = row // count, row % count
    turn[...] = jnp.zeros_like(turn)
    turn[0:sides, 0:count] = table[...].astype(jnp.float32)
    listed = entries_of(jnp.transpose(turn[...])[0:count, :], sides, side)
    wall = listed < 0.0
    patch = listed - (2 * count * (me // 2)).astype(jnp.float32)
    distance = listed - (count * me).astype(jnp.float32)
    first = 4 * count * 2
    step = 3 * CAP
    lists = (
        (-2, -2, first, first + step + 2 * CAP),
        (-1, 1, first + CAP, first + CAP),
        (2, 2, first + step, first + 2 * CAP),
    )
    masks, starts = [], []
    for far_even, far_odd, at_even, at_odd in lists:
        low = (count * jnp.where(even, far_even, far_odd)).astype(jnp.float32)
        masks.append(flag(~wall & (distance >= low) & (distance < low + count)))
        starts.append(jnp.where(even, at_even, at_odd).astype(jnp.float32))
    across = jnp.zeros((total, side), jnp.float32)
    for mask, rank, start in zip(masks, ranks(masks), starts):
        across = across + mask * (rank + start)
    place, twice = edge_places(row, count, patch)
    own = 4 * count * (1 - s % 2) + 2 * (count * odd + p) + s // 2
    inside = (patch >= 0.0) & (patch < 2.0 * count)
    index = jnp.where(inside, place.astype(jnp.float32) + twice, across)
    index = jnp.where(wall, own.astype(jnp.float32), index)
    lane = lane.astype(jnp.float32)
    hot = jnp.concatenate([flag(lane == index), flag(lane + side == index)], axis=1).astype(jnp.bfloat16)
    hot = jnp.concatenate([hot, hot], axis=1)
    fields = []
    for f in range(4):
        parts = edges_of_field(edges, f)
        parts += [ref[step * f : step * (f + 1), :] for ref in (crossed, passed)]
        parts.append(jnp.zeros((2 * side - first - 2 * step, side), jnp.float32))
        values = jnp.concatenate(parts, axis=0)
        high = values.astype(jnp.bfloat16)
        low = (values - high.astype(jnp.float32)).astype(jnp.bfloat16)
        fields.append(product(hot, jnp.concatenate([high, low], axis=0)))
    return fields, wall


def rim_terms(table, edges, crossed, passed, columns, lines, turn, me, odd):
    count = table.shape[1]
    outside, wall = ghosts(table, edges, crossed, passed, turn, me, odd)
    turn[...] = jnp.zeros_like(turn)
    lines[...] = jnp.zeros_like(lines)
    for s in range(4):
        parity = 1 - s % 2
        sign = 1.0 - 2.0 * parity
        axis = s // 2
        normal, across = (1, 2) if axis == 0 else (2, 1)

        at = slice(count * s, count * (s + 1))

        def both(f):
            row = 8 * axis + 2 * f + parity
            return edges[pl.ds(16 * count * odd + row, count, stride=16), :], outside[f][at]

        hc, hg = both(0)
        nc, ng = both(normal)
        ng = jnp.where(wall[at], -ng, ng)
        ac, ag = both(across)
        bc, bg = both(3)
        rc, rg = lax.rsqrt(hc), lax.rsqrt(hg)
        uc, ug = nc * rc * rc, ng * rg * rg
        top = jnp.maximum(jnp.abs(uc) + hc * rc, jnp.abs(ug) + hg * rg)
        fc, fg = nc * uc + 0.5 * hc * hc, ng * ug + 0.5 * hg * hg
        c_h = -HALF * (sign * (nc + ng) - top * ((hg + bg) - (hc + bc)))
        c_n = -HALF * (sign * (fc + fg + hc * bg) - top * (ng - nc))
        c_t = -HALF * (sign * (ac * uc + ag * ug) - top * (ag - ac))
        for f, value in ((0, c_h), (normal, c_n), (across, c_t)):
            target = turn if axis == 0 else lines
            target[pl.ds(2 * f + parity, count, stride=8), :] = value
    turn[...] = jnp.transpose(turn[...])
    side = turn.shape[0]
    columns[...] = pieces(jnp.concatenate([turn[spread(j, side), :] for j in range(side // ROWS)], axis=0))


def fill_places(places):
    side = places.shape[0] // 2
    row = lax.broadcasted_iota(jnp.int32, (side, side), 0) % 8
    lane = lax.broadcasted_iota(jnp.int32, (side, side), 1)
    source = row - jnp.where(lane == 0, 1, jnp.where(lane == side - 1, 0, 1024))
    for f in range(3):
        block = jnp.where(source == 2 * f, 1.0, 0.0).astype(jnp.bfloat16)
        for half in range(2):
            places[half * side : (half + 1) * side, f * side : (f + 1) * side] = block


def final_kernel(
    margin, range_ref, table, edges, crossed, passed, own, theirs, came, arrived, out,
    result, turn, columns, lines, places, sems,
):
    count, side = own.shape[0], lines.shape[1]
    me, odd = position()
    even = odd == 0
    fill_places(places)
    rim_terms(table, edges, crossed, passed, columns, lines, turn, me, odd)
    start, stop = range_ref[0, 0], range_ref[0, 1]
    line = iota(0, side)
    lane = lax.broadcasted_iota(jnp.int32, (side, 2 * side), 1) % side
    steps = side // ROWS
    results = bundle_layout(margin)[1]

    def copy(p):
        return pltpu.make_async_copy(result.at[p], out.at[p], sems.at[p])

    for group in range(0, count, margin):
        patches = range(group, group + margin)
        held = columns[...]
        masked = [held * jnp.where(lane // 8 == p, 1.0, 0.0).astype(jnp.bfloat16) for p in patches]
        terms = product(jnp.concatenate(masked, axis=0), places[...])
        for m, p in enumerate(patches):
            if group == 0:
                taken = me * count + p < start
            elif group == count - margin:
                taken = me * count + p >= stop
            else:
                taken = None
            near = even if group else odd == 1
            for f in range(3):
                for j in range(steps):
                    rows = slice(ROWS * j, ROWS * (j + 1))
                    value = own[p, f, rows, :]
                    if taken is not None:
                        if m < FIRST:
                            at = results + (3 * m + f) * side + ROWS * j
                            crossing = came[at : at + ROWS, :]
                        else:
                            crossing = arrived[m - FIRST, f, rows, :]
                        moved = jnp.where(near, theirs[m, f, rows, :], crossing)
                        value = jnp.where(taken, moved, value)
                    at = side * m + ROWS * j
                    value = value + terms[at : at + ROWS, f * side : (f + 1) * side]
                    if j == 0:
                        south = lines[8 * p + 2 * f + 1 : 8 * p + 2 * f + 2, :]
                        value = value + jnp.where(line == 0, south, 0.0)
                    if j == steps - 1:
                        north = lines[8 * p + 2 * f : 8 * p + 2 * f + 1, :]
                        value = value + jnp.where(line == ROWS - 1, north, 0.0)
                    result[p, f, spread(j, side), :] = value
            copy(p).start()
    for p in range(count):
        copy(p).wait()


def finished(old_range, table, edges, crossed, passed, own, theirs, came, arrived, margin):
    count, _, side, _ = own.shape
    return pl.pallas_call(
        functools.partial(final_kernel, margin),
        in_specs=[SMEM] + [VMEM] * 8,
        out_specs=HBM,
        out_shape=jax.ShapeDtypeStruct(own.shape, jnp.float32),
        scratch_shapes=[
            pltpu.VMEM(own.shape, jnp.float32),
            pltpu.VMEM((side, side), jnp.float32),
            pltpu.VMEM((side, 2 * side), jnp.bfloat16),
            pltpu.VMEM((side, side), jnp.float32),
            pltpu.VMEM((2 * side, 3 * side), jnp.bfloat16),
            pltpu.SemaphoreType.DMA((count,)),
        ],
        compiler_params=room(12),
        name="final",
    )(old_range, table, edges, crossed, passed, own, theirs, came, arrived)


def swapped(value, first):
    pairs = [(i, i + 1) for i in range(first, lax.axis_size(AXES) - 1, 2)]
    return lax.ppermute(value, AXES, pairs + [(j, i) for i, j in pairs])


def local(old_cells, old_range, neighbours):
    per_device = neighbours.shape[0]
    margin = (old_cells.shape[0] - per_device) // 2
    table = neighbours.T
    their_table = swapped(table, 0)
    rest, bundle = outer_patches(old_cells, table, margin)
    their_row = lambda: bundle_layout(margin)[0] + 8 * (1 - position()[1])
    bundle = placed_rows(8, their_row, bundle, their_table, "tables")
    came = swapped(bundle, 1)
    arrived = swapped(after(rest, bundle), 1)
    shared, inner, own = home_patches(old_range, old_cells, came, margin, per_device)
    their_edges = swapped(shared, 0)
    theirs = swapped(inner, 0)
    edges, message = answers(old_range, shared, their_edges, came, margin, per_device)
    crossed = swapped(message, 1)
    passed = swapped(crossed, 0)
    return finished(old_range, table, edges, crossed, passed, own, theirs, came, arrived, margin)


def solution(mesh):
    placed = (
        P(("member", "curve", "sub"), None, None, None),
        P(("member", "curve", "sub"), None),
        P(("member", "curve", "sub"), None),
    )
    return jax.shard_map(
        local,
        mesh=mesh,
        in_specs=placed,
        out_specs=P(("member", "curve", "sub"), None, None, None),
        check_vma=False,
    )
```

```python
import functools

import jax
import jax.numpy as jnp
from jax import lax
from jax.experimental import pallas as pl
from jax.experimental.pallas import tpu as pltpu
from jax.sharding import PartitionSpec as P

RATE_STEP = 0.1
HALF = 0.5 * RATE_STEP
AXES = ("curve", "sub")
CAP = 8
ROWS = 8
PAIR = 2
FIRST = 0
VMEM = pl.BlockSpec(memory_space=pltpu.VMEM)
SMEM = pl.BlockSpec(memory_space=pltpu.SMEM)
HBM = pl.BlockSpec(memory_space=pltpu.HBM)


def position():
    me = lax.axis_index(AXES)
    return me, lax.rem(me, 2)


def iota(axis, side):
    return lax.broadcasted_iota(jnp.int32, (ROWS, side), axis)


def spread(j, side):
    return pl.ds(j, ROWS, stride=side // ROWS)


def pieces(x):
    high = x.astype(jnp.bfloat16)
    low = (x - high.astype(jnp.float32)).astype(jnp.bfloat16)
    return jnp.concatenate([high, low], axis=1)


def product(parts, weights):
    return jnp.dot(parts, weights, preferred_element_type=jnp.float32)


AHEAD, EAST, SUMS, SLOPE = slice(0, 2), slice(2, 4), slice(4, 5), slice(5, 6)


def fill_weights(weights):
    side = weights.shape[0] // 2
    row = lax.broadcasted_iota(jnp.int32, (side, side), 0)
    lane = lax.broadcasted_iota(jnp.int32, (side, side), 1)
    one = lambda where: jnp.where(where, 1.0, 0.0)
    after, here, before = one(row == lane + 1), one(row == lane), one(row == lane - 1)
    inner_e, inner_w = lane != side - 1, lane != 0
    east = jnp.where(inner_e, after + here, 0.0)
    west = jnp.where(inner_w, here + before, 0.0)
    blocks = (
        after,
        before,
        jnp.where(inner_e, after - here, 0.0),
        jnp.where(inner_w, here - before, 0.0),
        east - west,
        after - before,
    )
    for n, block in enumerate(blocks):
        for half in range(2):
            weights[half * side : (half + 1) * side, n * side : (n + 1) * side] = block.astype(jnp.bfloat16)


def inner_update(loads, store, side, weights):
    line, lane = iota(0, side), iota(1, side)
    first, last = line == 0, line == ROWS - 1
    rim = jnp.where(lane == 0, 2.0, jnp.where(lane == side - 1, -2.0, 0.0))
    steps = side // ROWS
    many = len(loads)

    def cell(h, mx, my, bed):
        root = lax.rsqrt(h)
        celerity = h * root
        inverse = root * root
        u = mx * inverse
        v = my * inverse
        half_sq = 0.5 * h * h
        cross = my * u
        rate_y = jnp.abs(v) + celerity
        rate_x = jnp.abs(u) + celerity
        return (rate_y, h + bed, mx, my, cross, my * v + half_sq, bed), rate_x, mx * u + half_sq, h

    def face_y(low, high):
        top = jnp.maximum(low[0], high[0])
        return [
            (high[3] + low[3]) - top * (high[1] - low[1]),
            (high[4] + low[4]) - top * (high[2] - low[2]),
            (high[5] + low[5]) - top * (high[3] - low[3]),
        ]

    def taken(block):
        return weights[:, block.start * side : block.stop * side]

    cells = [cell(*[load(f, j) for f in range(4)]) for load in loads for j in range(steps)]
    stack = lambda pick: pieces(jnp.concatenate([pick(c) for c in cells], axis=0))
    eta, mx, my, cross, bed = (stack(lambda c, n=n: c[0][n]) for n in (1, 2, 3, 4, 6))
    fx = stack(lambda c: c[2])
    rates = product(stack(lambda c: c[1]), taken(AHEAD))
    jumps = product(jnp.concatenate([eta, mx, my], axis=0), taken(EAST))
    sums = product(jnp.concatenate([fx, cross], axis=0), taken(SUMS))
    slopes = product(bed, taken(SLOPE))
    for n in range(many):
        mine = cells[n * steps : (n + 1) * steps]
        low = [pltpu.roll(each, 1, 0) for each in mine[steps - 1][0]]
        faces = []
        for j in range(steps):
            faces.append(face_y(low, mine[j][0]))
            low = mine[j][0]
        faces[0] = [jnp.where(first, 0.0, each) for each in faces[0]]
        beds = [c[0][6] for c in mine]
        under = jnp.where(first, 0.0, pltpu.roll(beds[-1], 1, 0))
        over = jnp.where(last, 0.0, pltpu.roll(beds[0], ROWS - 1, 0))
        faces.append([jnp.where(last, 0.0, pltpu.roll(each, ROWS - 1, 0)) for each in faces[0]])
        for j in range(steps):
            (_, _, mx, my, _, _, _), rate, _, h = mine[j]
            at = [(q * many + n) * side + ROWS * j for q in range(3)]
            rows = [slice(r, r + ROWS) for r in at]
            top_e = jnp.maximum(rate, rates[rows[0], :side])
            top_w = jnp.maximum(rate, rates[rows[0], side:])
            total = [jumps[rows[1], :side] + jumps[rows[1], side:] + rim * mx, sums[rows[0]], sums[rows[1]]]
            x = [t - (top_e * jumps[r, :side] - top_w * jumps[r, side:]) for t, r in zip(total, rows)]
            south, north = faces[j], faces[j + 1]
            slope_y = (beds[j + 1] if j + 1 < steps else over) - (beds[j - 1] if j else under)
            store(n, 0, j, h - HALF * (x[0] + (north[0] - south[0])))
            store(n, 1, j, mx - HALF * (x[1] + h * slopes[rows[0]] + (north[1] - south[1])))
            store(n, 2, j, my - HALF * (x[2] + h * slope_y + (north[2] - south[2])))


def gather_columns(loads, columns, first_at, side):
    pair = iota(1, side) // 2
    for j in range(side // ROWS):
        held = columns[spread(j, side), :]
        for n, load in enumerate(loads):
            at = first_at + 8 * n
            for f in range(4):
                held = jnp.where(pair == at // 2 + f, pltpu.roll(load(f, j), at + 2 * f + 1, 1), held)
        columns[spread(j, side), :] = held


def take_edges(count, cells, slot_of, columns, edges, base):
    side = columns.shape[0]
    turned = jnp.transpose(columns[...])
    for p in range(count):
        edges[base + 16 * p : base + 16 * p + 8, :] = turned[8 * p : 8 * p + 8, :]
        for f in range(4):
            row = base + 16 * p + 8 + 2 * f
            edges[row : row + 1, :] = cells[slot_of(p), f, side - 1 : side, :]
            edges[row + 1 : row + 2, :] = cells[slot_of(p), f, 0:1, :]


def loader(cells, i):
    side = cells.shape[3]
    return lambda f, j: cells[i, f, spread(j, side), :]


def update(cells, first, many, weights, put):
    loads = [loader(cells, first + n) for n in range(many)]
    inner_update(loads, lambda n, f, j, value: put(n, f, ROWS * j, value), cells.shape[3], weights)


def fetch(cells_hbm, first, cells, sems, parts):
    def copy(i):
        return pltpu.make_async_copy(cells_hbm.at[first + i], cells.at[i], sems.at[i])

    for start, count in parts:
        for i in range(count):
            copy(start + i).start()
    return copy


def outer_slot(cells_hbm, margin):
    _, odd = position()
    return odd * (cells_hbm.shape[0] - margin)


def bundle_layout(margin):
    tables = 16 * margin
    return tables, tables + 16


def outer_kernel(margin, cells_hbm, table, rest, bundle, cells, columns, weights, sems):
    side = columns.shape[0]
    _, odd = position()
    copy = fetch(cells_hbm, outer_slot(cells_hbm, margin), cells, sems, [(0, margin)])
    fill_weights(weights)
    tables, results = bundle_layout(margin)
    sides, count = table.shape
    bundle[tables:results, :] = jnp.zeros((results - tables, side), jnp.float32)
    bundle[pl.ds(pl.multiple_of(tables + 8 * odd, 8), sides), 0:count] = table[...].astype(jnp.float32)
    for i in range(0, margin, PAIR):
        for n in range(PAIR):
            copy(i + n).wait()

        def put(n, f, row, value, i=i):
            if i + n < FIRST:
                at = results + (3 * (i + n) + f) * side + row
                bundle[at : at + ROWS, :] = value
            else:
                rest[i + n - FIRST, f, row : row + ROWS, :] = value

        gather_columns([loader(cells, i + n) for n in range(PAIR)], columns, 8 * i, side)
        update(cells, i, PAIR, weights, put)

    take_edges(margin, cells, lambda p: p, columns, bundle, 0)


def cost(patches, side):
    return pl.CostEstimate(
        flops=patches * side * side * 800,
        bytes_accessed=patches * side * side * 28,
        transcendentals=patches * side * side,
    )


def room(mebibytes):
    return pltpu.CompilerParams(vmem_limit_bytes=mebibytes << 20)


def outer_patches(old_cells, table, margin):
    side = old_cells.shape[3]
    return pl.pallas_call(
        functools.partial(outer_kernel, margin),
        in_specs=[HBM, VMEM],
        out_specs=[VMEM, VMEM],
        out_shape=[
            jax.ShapeDtypeStruct((margin - FIRST, 3, side, side), jnp.float32),
            jax.ShapeDtypeStruct((bundle_layout(margin)[1] + 3 * FIRST * side, side), jnp.float32),
        ],
        scratch_shapes=[
            pltpu.VMEM((margin, 4, side, side), jnp.float32),
            pltpu.VMEM((side, side), jnp.float32),
            pltpu.VMEM((2 * side, 6 * side), jnp.bfloat16),
            pltpu.SemaphoreType.DMA((margin,)),
        ],
        cost_estimate=cost(margin, side),
        compiler_params=room(48),
        name="outer",
    )(old_cells, table)


def placed_rows(rows, start_of, bundle, extra, name):
    any_place = pl.BlockSpec(memory_space=pl.ANY)
    small = rows == 8

    def kernel(bundle_ref, extra_ref, out_ref, held, sem):
        source = extra_ref
        if small:
            held[...] = jnp.zeros_like(held)
            held[0 : extra_ref.shape[0], 0 : extra_ref.shape[1]] = extra_ref[...].astype(jnp.float32)
            source = held
        start = pl.multiple_of(start_of(), 8)
        copy = pltpu.make_async_copy(source.at[pl.ds(0, rows), :], out_ref.at[pl.ds(start, rows), :], sem)
        copy.start()
        copy.wait()

    return pl.pallas_call(
        kernel,
        in_specs=[any_place, VMEM if small else any_place],
        out_specs=any_place,
        out_shape=jax.ShapeDtypeStruct(bundle.shape, bundle.dtype),
        scratch_shapes=[pltpu.VMEM((8, bundle.shape[1]), jnp.float32), pltpu.SemaphoreType.DMA],
        input_output_aliases={0: 0},
        compiler_params=room(4),
        name=name,
    )(bundle, extra)


def after(value, other):
    any_place = pl.BlockSpec(memory_space=pl.ANY)
    return pl.pallas_call(
        lambda value_ref, other_ref, out_ref: None,
        in_specs=[any_place, any_place],
        out_specs=any_place,
        out_shape=jax.ShapeDtypeStruct(value.shape, value.dtype),
        input_output_aliases={0: 0},
        compiler_params=room(4),
        name="after",
    )(value, other)


def layout(margin, per_device):
    home = 16 * margin
    limit = home + 16 * per_device
    brought = limit + 8
    return home, limit, brought, brought + 16 * margin


def home_kernel(margin, range_ref, cells_hbm, came, shared, inner, own, cells, columns, weights, sems):
    side = columns.shape[0]
    count = own.shape[0]
    home, limit, brought, total = layout(margin, count)
    _, odd = position()
    inner_at = (1 - odd) * count
    home_at = odd * margin
    parts = [(inner_at, margin), (home_at, count)]
    copy = fetch(cells_hbm, (1 - odd) * margin, cells, sems, parts)
    fill_weights(weights)

    for at, many, out, row in ((inner_at, margin, inner, 0), (home_at, count, own, home)):

        @pl.loop(0, many // PAIR)
        def _(step, at=at, out=out):
            i = step * PAIR
            for n in range(PAIR):
                copy(at + i + n).wait()

            def put(n, f, row, value):
                out[i + n, f, row : row + ROWS, :] = value

            gather_columns([loader(cells, at + i + n) for n in range(PAIR)], columns, 8 * i, side)
            update(cells, at + i, PAIR, weights, put)

        take_edges(many, cells, lambda p, at=at: at + p, columns, shared, row)

    outer_limit = jnp.where(odd == 1, range_ref[0, 1], range_ref[0, 0])
    shared[limit : limit + 8, :] = jnp.full((8, side), outer_limit, jnp.int32).astype(jnp.float32)
    shared[brought:total, :] = came[0 : total - brought, :]


def home_patches(old_range, old_cells, came, margin, per_device):
    side = old_cells.shape[3]
    total = layout(margin, per_device)[-1]
    return pl.pallas_call(
        functools.partial(home_kernel, margin),
        in_specs=[SMEM, HBM, VMEM],
        out_specs=[VMEM] * 3,
        out_shape=[
            jax.ShapeDtypeStruct((total, side), jnp.float32),
            jax.ShapeDtypeStruct((margin, 3, side, side), jnp.float32),
            jax.ShapeDtypeStruct((per_device, 3, side, side), jnp.float32),
        ],
        scratch_shapes=[
            pltpu.VMEM((margin + per_device, 4, side, side), jnp.float32),
            pltpu.VMEM((side, side), jnp.float32),
            pltpu.VMEM((2 * side, 6 * side), jnp.bfloat16),
            pltpu.SemaphoreType.DMA((margin + per_device,)),
        ],
        cost_estimate=cost(margin + per_device, side),
        compiler_params=room(48),
        name="home",
    )(old_range, old_cells, came)


def entries_of(table, sides, lanes):
    count = table.shape[0]
    return jnp.concatenate([jnp.broadcast_to(table[:, s : s + 1], (count, lanes)) for s in range(sides)], axis=0)


def grid_iota(rows, lanes, axis):
    return lax.broadcasted_iota(jnp.int32, (rows, lanes), axis)


def flag(where):
    return jnp.where(where, 1.0, 0.0)


def ranks(masks):
    rows, lanes = masks[0].shape
    earlier = flag(grid_iota(rows, lanes, 1) < grid_iota(rows, lanes, 0)).astype(jnp.bfloat16)
    stacked = jnp.concatenate(masks, axis=1).astype(jnp.bfloat16)
    if rows < lanes:
        stacked = jnp.concatenate([stacked, jnp.zeros((lanes - rows, stacked.shape[1]), jnp.bfloat16)], axis=0)
    counted = product(earlier, stacked)
    return [counted[:, n * lanes : (n + 1) * lanes] for n in range(len(masks))]


def edge_places(row, count, patch):
    s = row // count
    return 4 * count * (s % 2) + s // 2, 2.0 * patch


def edges_of_field(edges, f):
    tiles = edges.shape[0] // 8
    return [edges[pl.ds(2 * f + parity, tiles, stride=8), :] for parity in range(2)]


def answer_kernel(margin, count, range_ref, mine, theirs, came, edges, message):
    side = edges.shape[1]
    home, limit, brought, _ = layout(margin, count)
    inner = 0
    me, odd = position()
    start, stop = range_ref[0, 0], range_ref[0, 1]
    even = odd == 0
    at_me = pl.multiple_of(16 * count * odd, 16)
    at_them = pl.multiple_of(16 * count * (1 - odd), 16)
    edges[pl.ds(at_me, 16 * count), :] = mine[home : home + 16 * count, :]
    edges[pl.ds(at_them, 16 * count), :] = theirs[home : home + 16 * count, :]
    their_limit = theirs[limit : limit + 8, :]
    low, high = 0, count - margin
    for m in range(margin):
        l = jnp.where(even, high, low) + m
        g = me * count + l
        taken = jnp.where(even, g >= stop, g < start)
        to = pl.multiple_of(at_me + 16 * l, 16)
        from_pair = theirs[inner + 16 * m : inner + 16 * (m + 1), :]
        edges[pl.ds(to, 16), :] = jnp.where(taken, from_pair, edges[pl.ds(to, 16), :])
        l = jnp.where(even, low, high) + m
        g = (me + 1 - 2 * odd) * count + l
        taken = jnp.where(even, g < stop, g >= start)
        to = pl.multiple_of(at_them + 16 * l, 16)
        from_pair = mine[inner + 16 * m : inner + 16 * (m + 1), :]
        edges[pl.ds(to, 16), :] = jnp.where(taken, from_pair, edges[pl.ds(to, 16), :])
        l = jnp.where(even, low, high) + m
        g = me * count + l
        taken = jnp.where(even, g < start, g >= stop)
        to = pl.multiple_of(at_me + 16 * l, 16)
        crossed = mine[brought + 16 * m : brought + 16 * (m + 1), :]
        edges[pl.ds(to, 16), :] = jnp.where(taken, crossed, edges[pl.ds(to, 16), :])
        l = jnp.where(even, high, low) + m
        g = ((me + 1 - 2 * odd) * count + l).astype(jnp.float32)
        to = pl.multiple_of(at_them + 16 * l, 16)
        taken = jnp.where(even, g - their_limit, their_limit - g - 1.0) >= 0.0
        for half in range(2):
            crossed = theirs[brought + 16 * m + 8 * half : brought + 16 * m + 8 * half + 8, :]
            at = pl.multiple_of(to + 8 * half, 8)
            edges[pl.ds(at, 8), :] = jnp.where(taken, crossed, edges[pl.ds(at, 8), :])
    sides, total = 4, 8 * count
    row = grid_iota(total, side, 0)
    lane = grid_iota(total, side, 1)
    which, within = row // (sides * count), row % (sides * count)
    at = 16 * margin
    turned = jnp.transpose(jnp.concatenate([came[at : at + 16, :], jnp.zeros((side - 16, side), jnp.float32)], axis=0))
    tables = [turned[0:count, 8 * n : 8 * n + sides] for n in range(2)]
    listed = jnp.concatenate([entries_of(table, sides, side) for table in tables], axis=0)
    patch = listed - (2 * count * (me // 2)).astype(jnp.float32)
    held = [(patch >= n * count) & (patch < (n + 1) * count) for n in range(2)]
    masks = [
        flag((which == 0) & held[0]),
        jnp.where(even, flag((which == 1) & held[0]), flag((which == 0) & held[1])),
        flag((which == 1) & held[1]),
    ]
    chosen = jnp.zeros((total, side), jnp.float32)
    for k, (mask, rank) in enumerate(zip(masks, ranks(masks))):
        slot = (lane - k * CAP).astype(jnp.float32)
        chosen = chosen + jnp.where((lane // CAP == k) & (rank == slot), mask, 0.0)
    place, twice = edge_places(within, count, patch)
    hot = flag(lane.astype(jnp.float32) == place.astype(jnp.float32) + twice).astype(jnp.bfloat16)
    slots = jnp.transpose(chosen)[0:32, :].astype(jnp.bfloat16)
    picked = product(slots, hot).astype(jnp.bfloat16)
    picked = jnp.concatenate([picked] * 3, axis=1)
    for f in range(4):
        values = jnp.concatenate(edges_of_field(edges, f), axis=0)
        high = values.astype(jnp.bfloat16)
        left = values - high.astype(jnp.float32)
        mid = left.astype(jnp.bfloat16)
        low = (left - mid.astype(jnp.float32)).astype(jnp.bfloat16)
        taken = product(picked, jnp.concatenate([high, mid, low], axis=0))
        message[3 * CAP * f : 3 * CAP * (f + 1), :] = taken[0 : 3 * CAP, :]


def answers(old_range, mine, theirs, came, margin, per_device):
    side = mine.shape[1]
    return pl.pallas_call(
        functools.partial(answer_kernel, margin, per_device),
        in_specs=[SMEM, VMEM, VMEM, VMEM],
        out_specs=[VMEM, VMEM],
        out_shape=[
            jax.ShapeDtypeStruct((32 * per_device, side), jnp.float32),
            jax.ShapeDtypeStruct((12 * CAP, side), jnp.float32),
        ],
        compiler_params=room(4),
        name="answers",
    )(old_range, mine, theirs, came)


def prepare_kernel(table, edges, places, hot, near, walls, turn):
    me, odd = position()
    fill_places(places)
    sides, count = table.shape
    side = edges.shape[1]
    total = sides * count
    even = odd == 0
    row, lane = grid_iota(total, side, 0), grid_iota(total, side, 1)
    s, p = row // count, row % count
    turn[...] = jnp.zeros_like(turn)
    turn[0:sides, 0:count] = table[...].astype(jnp.float32)
    listed = entries_of(jnp.transpose(turn[...])[0:count, :], sides, side)
    wall = listed < 0.0
    patch = listed - (2 * count * (me // 2)).astype(jnp.float32)
    distance = listed - (count * me).astype(jnp.float32)
    first = 4 * count * 2
    step = 3 * CAP
    lists = (
        (-2, -2, first, first + step + 2 * CAP),
        (-1, 1, first + CAP, first + CAP),
        (2, 2, first + step, first + 2 * CAP),
    )
    masks, starts = [], []
    for far_even, far_odd, at_even, at_odd in lists:
        low = (count * jnp.where(even, far_even, far_odd)).astype(jnp.float32)
        masks.append(flag(~wall & (distance >= low) & (distance < low + count)))
        starts.append(jnp.where(even, at_even, at_odd).astype(jnp.float32))
    across = jnp.zeros((total, side), jnp.float32)
    for mask, rank, start in zip(masks, ranks(masks), starts):
        across = across + mask * (rank + start)
    place, twice = edge_places(row, count, patch)
    own = 4 * count * (1 - s % 2) + 2 * (count * odd + p) + s // 2
    inside = (patch >= 0.0) & (patch < 2.0 * count)
    index = jnp.where(inside, place.astype(jnp.float32) + twice, across)
    index = jnp.where(wall, own.astype(jnp.float32), index)
    lane = lane.astype(jnp.float32)
    walls[...] = flag(wall)
    far = flag(lane + first == index)
    hot[...] = jnp.concatenate([far, far], axis=1).astype(jnp.bfloat16)
    at_home = flag(lane == index)
    at_home = jnp.concatenate([at_home, at_home], axis=1).astype(jnp.bfloat16)
    for f in range(4):
        near[total * f : total * (f + 1), :] = product(at_home, halves(jnp.concatenate(edges_of_field(edges, f), axis=0)))


def halves(values):
    high = values.astype(jnp.bfloat16)
    low = (values - high.astype(jnp.float32)).astype(jnp.bfloat16)
    return jnp.concatenate([high, low], axis=0)


def prepared(table, edges):
    side = edges.shape[1]
    total = table.shape[0] * table.shape[1]
    return pl.pallas_call(
        prepare_kernel,
        in_specs=[VMEM] * 2,
        out_specs=[VMEM] * 4,
        out_shape=[
            jax.ShapeDtypeStruct((2 * side, 6 * side), jnp.bfloat16),
            jax.ShapeDtypeStruct((total, 2 * side), jnp.bfloat16),
            jax.ShapeDtypeStruct((4 * total, side), jnp.float32),
            jax.ShapeDtypeStruct((total, side), jnp.float32),
        ],
        scratch_shapes=[pltpu.VMEM((side, side), jnp.float32)],
        compiler_params=room(4),
        name="prepare",
    )(table, edges)


def rim_terms(hot, near, walls, edges, crossed, passed, columns, lines, turn, count, odd):
    side = edges.shape[1]
    total, step = walls.shape[0], 3 * CAP
    outside = []
    for f in range(4):
        parts = [ref[step * f : step * (f + 1), :] for ref in (crossed, passed)]
        parts.append(jnp.zeros((side - 2 * step, side), jnp.float32))
        far = product(hot[...], halves(jnp.concatenate(parts, axis=0)))
        outside.append(near[total * f : total * (f + 1), :] + far)
    wall = walls[...] > 0.0
    turn[...] = jnp.zeros_like(turn)
    lines[...] = jnp.zeros_like(lines)
    for s in range(4):
        parity = 1 - s % 2
        sign = 1.0 - 2.0 * parity
        axis = s // 2
        normal, across = (1, 2) if axis == 0 else (2, 1)

        at = slice(count * s, count * (s + 1))

        def both(f):
            row = 8 * axis + 2 * f + parity
            return edges[pl.ds(16 * count * odd + row, count, stride=16), :], outside[f][at]

        hc, hg = both(0)
        nc, ng = both(normal)
        ng = jnp.where(wall[at], -ng, ng)
        ac, ag = both(across)
        bc, bg = both(3)
        rc, rg = lax.rsqrt(hc), lax.rsqrt(hg)
        uc, ug = nc * rc * rc, ng * rg * rg
        top = jnp.maximum(jnp.abs(uc) + hc * rc, jnp.abs(ug) + hg * rg)
        fc, fg = nc * uc + 0.5 * hc * hc, ng * ug + 0.5 * hg * hg
        c_h = -HALF * (sign * (nc + ng) - top * ((hg + bg) - (hc + bc)))
        c_n = -HALF * (sign * (fc + fg + hc * bg) - top * (ng - nc))
        c_t = -HALF * (sign * (ac * uc + ag * ug) - top * (ag - ac))
        for f, value in ((0, c_h), (normal, c_n), (across, c_t)):
            target = turn if axis == 0 else lines
            target[pl.ds(2 * f + parity, count, stride=8), :] = value
    turn[...] = jnp.transpose(turn[...])
    side = turn.shape[0]
    columns[...] = pieces(jnp.concatenate([turn[spread(j, side), :] for j in range(side // ROWS)], axis=0))


def fill_places(places):
    side = places.shape[0] // 2
    row = lax.broadcasted_iota(jnp.int32, (side, side), 0) % 16
    lane = lax.broadcasted_iota(jnp.int32, (side, side), 1)
    source = row - jnp.where(lane == 0, 1, jnp.where(lane == side - 1, 0, 1024))
    for u in range(2):
        for f in range(3):
            block = jnp.where(source == 8 * u + 2 * f, 1.0, 0.0).astype(jnp.bfloat16)
            for half in range(2):
                at = (3 * u + f) * side
                places[half * side : (half + 1) * side, at : at + side] = block


def final_kernel(
    margin, range_ref, places, hot, near, walls, edges, crossed, passed, own, theirs, came, arrived, out,
    result, turn, columns, lines, sems,
):
    count, side = own.shape[0], lines.shape[1]
    me, odd = position()
    even = odd == 0
    rim_terms(hot, near, walls, edges, crossed, passed, columns, lines, turn, count, odd)
    start, stop = range_ref[0, 0], range_ref[0, 1]
    line = iota(0, side)
    lane = lax.broadcasted_iota(jnp.int32, (side, 2 * side), 1) % side
    steps = side // ROWS
    results = bundle_layout(margin)[1]

    def copy(p):
        return pltpu.make_async_copy(result.at[p], out.at[p], sems.at[p])

    for group in range(0, count, margin):
        patches = range(group, group + margin)
        held = columns[...]
        masked = [held * jnp.where(lane // 16 == p // 2, 1.0, 0.0).astype(jnp.bfloat16) for p in patches[::2]]
        terms = product(jnp.concatenate(masked, axis=0), places[...])
        for m, p in enumerate(patches):
            if group == 0:
                taken = me * count + p < start
            elif group == count - margin:
                taken = me * count + p >= stop
            else:
                taken = None
            beside = even if group else odd == 1
            for f in range(3):
                for j in range(steps):
                    rows = slice(ROWS * j, ROWS * (j + 1))
                    value = own[p, f, rows, :]
                    if taken is not None:
                        if m < FIRST:
                            at = results + (3 * m + f) * side + ROWS * j
                            crossing = came[at : at + ROWS, :]
                        else:
                            crossing = arrived[m - FIRST, f, rows, :]
                        moved = jnp.where(beside, theirs[m, f, rows, :], crossing)
                        value = jnp.where(taken, moved, value)
                    at = side * (m // 2) + ROWS * j
                    block = 3 * (m % 2) + f
                    value = value + terms[at : at + ROWS, block * side : (block + 1) * side]
                    if j == 0:
                        south = lines[8 * p + 2 * f + 1 : 8 * p + 2 * f + 2, :]
                        value = value + jnp.where(line == 0, south, 0.0)
                    if j == steps - 1:
                        north = lines[8 * p + 2 * f : 8 * p + 2 * f + 1, :]
                        value = value + jnp.where(line == ROWS - 1, north, 0.0)
                    result[p, f, spread(j, side), :] = value
            copy(p).start()
    for p in range(count):
        copy(p).wait()


def finished(old_range, ready, edges, crossed, passed, own, theirs, came, arrived, margin):
    count, _, side, _ = own.shape
    return pl.pallas_call(
        functools.partial(final_kernel, margin),
        in_specs=[SMEM] + [VMEM] * 11,
        out_specs=HBM,
        out_shape=jax.ShapeDtypeStruct(own.shape, jnp.float32),
        scratch_shapes=[
            pltpu.VMEM(own.shape, jnp.float32),
            pltpu.VMEM((side, side), jnp.float32),
            pltpu.VMEM((side, 2 * side), jnp.bfloat16),
            pltpu.VMEM((side, side), jnp.float32),
            pltpu.SemaphoreType.DMA((count,)),
        ],
        compiler_params=room(12),
        name="final",
    )(old_range, *ready, edges, crossed, passed, own, theirs, came, arrived)


def swapped(value, first):
    pairs = [(i, i + 1) for i in range(first, lax.axis_size(AXES) - 1, 2)]
    return lax.ppermute(value, AXES, pairs + [(j, i) for i, j in pairs])


def local(old_cells, old_range, neighbours):
    per_device = neighbours.shape[0]
    margin = (old_cells.shape[0] - per_device) // 2
    table = neighbours.T
    their_table = swapped(table, 0)
    rest, bundle = outer_patches(old_cells, table, margin)
    their_row = lambda: bundle_layout(margin)[0] + 8 * (1 - position()[1])
    bundle = placed_rows(8, their_row, bundle, their_table, "tables")
    came = swapped(bundle, 1)
    arrived = swapped(after(rest, bundle), 1)
    shared, inner, own = home_patches(old_range, old_cells, came, margin, per_device)
    their_edges = swapped(shared, 0)
    theirs = swapped(inner, 0)
    edges, message = answers(old_range, shared, their_edges, came, margin, per_device)
    crossed = swapped(message, 1)
    passed = swapped(crossed, 0)
    return finished(old_range, prepared(table, edges), edges, crossed, passed, own, theirs, came, arrived, margin)


def solution(mesh):
    placed = (
        P(("member", "curve", "sub"), None, None, None),
        P(("member", "curve", "sub"), None),
        P(("member", "curve", "sub"), None),
    )
    return jax.shard_map(
        local,
        mesh=mesh,
        in_specs=placed,
        out_specs=P(("member", "curve", "sub"), None, None, None),
        check_vma=False,
    )
```

```python
import functools

import jax
import jax.numpy as jnp
from jax import lax
from jax.experimental import pallas as pl
from jax.experimental.pallas import tpu as pltpu
from jax.sharding import PartitionSpec as P

RATE_STEP = 0.1
HALF = 0.5 * RATE_STEP
AXES = ("curve", "sub")
CAP = 8
ROWS = 8
PAIR = 2
FIRST = 0
VMEM = pl.BlockSpec(memory_space=pltpu.VMEM)
SMEM = pl.BlockSpec(memory_space=pltpu.SMEM)
HBM = pl.BlockSpec(memory_space=pltpu.HBM)


def position():
    me = lax.axis_index(AXES)
    return me, lax.rem(me, 2)


def iota(axis, side):
    return lax.broadcasted_iota(jnp.int32, (ROWS, side), axis)


def spread(j, side):
    return pl.ds(j, ROWS, stride=side // ROWS)


def pieces(x):
    high = x.astype(jnp.bfloat16)
    low = (x - high.astype(jnp.float32)).astype(jnp.bfloat16)
    return jnp.concatenate([high, low], axis=1)


def product(parts, weights):
    return jnp.dot(parts, weights, preferred_element_type=jnp.float32)


AHEAD, EAST, SUMS, SLOPE = slice(0, 2), slice(2, 4), slice(4, 5), slice(5, 6)


def fill_weights(weights):
    side = weights.shape[0] // 2
    row = lax.broadcasted_iota(jnp.int32, (side, side), 0)
    lane = lax.broadcasted_iota(jnp.int32, (side, side), 1)
    one = lambda where: jnp.where(where, 1.0, 0.0)
    after, here, before = one(row == lane + 1), one(row == lane), one(row == lane - 1)
    inner_e, inner_w = lane != side - 1, lane != 0
    east = jnp.where(inner_e, after + here, 0.0)
    west = jnp.where(inner_w, here + before, 0.0)
    blocks = (
        after,
        before,
        jnp.where(inner_e, after - here, 0.0),
        jnp.where(inner_w, here - before, 0.0),
        east - west,
        after - before,
    )
    for n, block in enumerate(blocks):
        for half in range(2):
            weights[half * side : (half + 1) * side, n * side : (n + 1) * side] = block.astype(jnp.bfloat16)


def inner_update(loads, store, side, weights):
    line, lane = iota(0, side), iota(1, side)
    first, last = line == 0, line == ROWS - 1
    rim = jnp.where(lane == 0, 2.0, jnp.where(lane == side - 1, -2.0, 0.0))
    steps = side // ROWS
    many = len(loads)

    def cell(h, mx, my, bed):
        root = lax.rsqrt(h)
        celerity = h * root
        inverse = root * root
        u = mx * inverse
        v = my * inverse
        half_sq = 0.5 * h * h
        cross = my * u
        rate_y = jnp.abs(v) + celerity
        rate_x = jnp.abs(u) + celerity
        return (rate_y, h + bed, mx, my, cross, my * v + half_sq, bed), rate_x, mx * u + half_sq, h

    def face_y(low, high):
        top = jnp.maximum(low[0], high[0])
        return [
            (high[3] + low[3]) - top * (high[1] - low[1]),
            (high[4] + low[4]) - top * (high[2] - low[2]),
            (high[5] + low[5]) - top * (high[3] - low[3]),
        ]

    def taken(block):
        return weights[:, block.start * side : block.stop * side]

    cells = [cell(*[load(f, j) for f in range(4)]) for load in loads for j in range(steps)]
    stack = lambda pick: pieces(jnp.concatenate([pick(c) for c in cells], axis=0))
    eta, mx, my, cross, bed = (stack(lambda c, n=n: c[0][n]) for n in (1, 2, 3, 4, 6))
    fx = stack(lambda c: c[2])
    rates = product(stack(lambda c: c[1]), taken(AHEAD))
    jumps = product(jnp.concatenate([eta, mx, my], axis=0), taken(EAST))
    sums = product(jnp.concatenate([fx, cross], axis=0), taken(SUMS))
    slopes = product(bed, taken(SLOPE))
    for n in range(many):
        mine = cells[n * steps : (n + 1) * steps]
        low = [pltpu.roll(each, 1, 0) for each in mine[steps - 1][0]]
        faces = []
        for j in range(steps):
            faces.append(face_y(low, mine[j][0]))
            low = mine[j][0]
        faces[0] = [jnp.where(first, 0.0, each) for each in faces[0]]
        beds = [c[0][6] for c in mine]
        under = jnp.where(first, 0.0, pltpu.roll(beds[-1], 1, 0))
        over = jnp.where(last, 0.0, pltpu.roll(beds[0], ROWS - 1, 0))
        faces.append([jnp.where(last, 0.0, pltpu.roll(each, ROWS - 1, 0)) for each in faces[0]])
        for j in range(steps):
            (_, _, mx, my, _, _, _), rate, _, h = mine[j]
            at = [(q * many + n) * side + ROWS * j for q in range(3)]
            rows = [slice(r, r + ROWS) for r in at]
            top_e = jnp.maximum(rate, rates[rows[0], :side])
            top_w = jnp.maximum(rate, rates[rows[0], side:])
            total = [jumps[rows[1], :side] + jumps[rows[1], side:] + rim * mx, sums[rows[0]], sums[rows[1]]]
            x = [t - (top_e * jumps[r, :side] - top_w * jumps[r, side:]) for t, r in zip(total, rows)]
            south, north = faces[j], faces[j + 1]
            slope_y = (beds[j + 1] if j + 1 < steps else over) - (beds[j - 1] if j else under)
            store(n, 0, j, h - HALF * (x[0] + (north[0] - south[0])))
            store(n, 1, j, mx - HALF * (x[1] + h * slopes[rows[0]] + (north[1] - south[1])))
            store(n, 2, j, my - HALF * (x[2] + h * slope_y + (north[2] - south[2])))


def gather_columns(loads, columns, first_at, side):
    pair = iota(1, side) // 2
    for j in range(side // ROWS):
        held = columns[spread(j, side), :]
        for n, load in enumerate(loads):
            at = first_at + 8 * n
            for f in range(4):
                held = jnp.where(pair == at // 2 + f, pltpu.roll(load(f, j), at + 2 * f + 1, 1), held)
        columns[spread(j, side), :] = held


def take_edges(count, cells, slot_of, columns, edges, base):
    side = columns.shape[0]
    turned = jnp.transpose(columns[...])
    for p in range(count):
        edges[base + 16 * p : base + 16 * p + 8, :] = turned[8 * p : 8 * p + 8, :]
        for f in range(4):
            row = base + 16 * p + 8 + 2 * f
            edges[row : row + 1, :] = cells[slot_of(p), f, side - 1 : side, :]
            edges[row + 1 : row + 2, :] = cells[slot_of(p), f, 0:1, :]


def loader(cells, i):
    side = cells.shape[3]
    return lambda f, j: cells[i, f, spread(j, side), :]


def update(cells, first, many, weights, put):
    loads = [loader(cells, first + n) for n in range(many)]
    inner_update(loads, lambda n, f, j, value: put(n, f, ROWS * j, value), cells.shape[3], weights)


def fetch(cells_hbm, first, cells, sems, parts):
    def copy(i):
        return pltpu.make_async_copy(cells_hbm.at[first + i], cells.at[i], sems.at[i])

    for start, count in parts:
        for i in range(count):
            copy(start + i).start()
    return copy


def outer_slot(cells_hbm, margin):
    _, odd = position()
    return odd * (cells_hbm.shape[0] - margin)


def bundle_layout(margin):
    tables = 16 * margin
    return tables, tables + 16


def outer_kernel(margin, cells_hbm, rest, bundle, cells, columns, weights, sems):
    side = columns.shape[0]
    copy = fetch(cells_hbm, outer_slot(cells_hbm, margin), cells, sems, [(0, margin)])
    fill_weights(weights)
    results = bundle_layout(margin)[1]
    for i in range(0, margin, PAIR):
        for n in range(PAIR):
            copy(i + n).wait()

        def put(n, f, row, value, i=i):
            if i + n < FIRST:
                at = results + (3 * (i + n) + f) * side + row
                bundle[at : at + ROWS, :] = value
            else:
                rest[i + n - FIRST, f, row : row + ROWS, :] = value

        gather_columns([loader(cells, i + n) for n in range(PAIR)], columns, 8 * i, side)
        update(cells, i, PAIR, weights, put)

    take_edges(margin, cells, lambda p: p, columns, bundle, 0)


def cost(patches, side):
    return pl.CostEstimate(
        flops=patches * side * side * 800,
        bytes_accessed=patches * side * side * 28,
        transcendentals=patches * side * side,
    )


def room(mebibytes):
    return pltpu.CompilerParams(vmem_limit_bytes=mebibytes << 20)


def outer_patches(old_cells, margin):
    side = old_cells.shape[3]
    return pl.pallas_call(
        functools.partial(outer_kernel, margin),
        in_specs=[HBM],
        out_specs=[VMEM, VMEM],
        out_shape=[
            jax.ShapeDtypeStruct((margin - FIRST, 3, side, side), jnp.float32),
            jax.ShapeDtypeStruct((bundle_layout(margin)[1] + 3 * FIRST * side, side), jnp.float32),
        ],
        scratch_shapes=[
            pltpu.VMEM((margin, 4, side, side), jnp.float32),
            pltpu.VMEM((side, side), jnp.float32),
            pltpu.VMEM((2 * side, 6 * side), jnp.bfloat16),
            pltpu.SemaphoreType.DMA((margin,)),
        ],
        cost_estimate=cost(margin, side),
        compiler_params=room(48),
        name="outer",
    )(old_cells)


def with_tables(bundle, table, their_table, margin):
    any_place = pl.BlockSpec(memory_space=pl.ANY)
    start, end = bundle_layout(margin)
    sides, count = table.shape

    def kernel(bundle_ref, table_ref, their_ref, out_ref, held, sem):
        _, odd = position()
        held[...] = jnp.zeros_like(held)
        for which, ref in ((odd, table_ref), (1 - odd, their_ref)):
            held[pl.ds(pl.multiple_of(8 * which, 8), sides), 0:count] = ref[...].astype(jnp.float32)
        copy = pltpu.make_async_copy(held, out_ref.at[start:end, :], sem)
        copy.start()
        copy.wait()

    return pl.pallas_call(
        kernel,
        in_specs=[any_place, VMEM, VMEM],
        out_specs=any_place,
        out_shape=jax.ShapeDtypeStruct(bundle.shape, bundle.dtype),
        scratch_shapes=[pltpu.VMEM((end - start, bundle.shape[1]), jnp.float32), pltpu.SemaphoreType.DMA],
        input_output_aliases={0: 0},
        compiler_params=room(4),
        name="tables",
    )(bundle, table, their_table)


def after(value, other):
    any_place = pl.BlockSpec(memory_space=pl.ANY)
    return pl.pallas_call(
        lambda value_ref, other_ref, out_ref: None,
        in_specs=[any_place, any_place],
        out_specs=any_place,
        out_shape=jax.ShapeDtypeStruct(value.shape, value.dtype),
        input_output_aliases={0: 0},
        compiler_params=room(4),
        name="after",
    )(value, other)


def layout(margin, per_device):
    home = 16 * margin
    limit = home + 16 * per_device
    brought = limit + 8
    return home, limit, brought, brought + 16 * margin


def home_kernel(margin, range_ref, cells_hbm, came, shared, inner, own, cells, columns, weights, sems):
    side = columns.shape[0]
    count = own.shape[0]
    home, limit, brought, total = layout(margin, count)
    _, odd = position()
    inner_at = (1 - odd) * count
    home_at = odd * margin
    parts = [(inner_at, margin), (home_at, count)]
    copy = fetch(cells_hbm, (1 - odd) * margin, cells, sems, parts)
    fill_weights(weights)

    for at, many, out, row in ((inner_at, margin, inner, 0), (home_at, count, own, home)):

        @pl.loop(0, many // PAIR)
        def _(step, at=at, out=out):
            i = step * PAIR
            for n in range(PAIR):
                copy(at + i + n).wait()

            def put(n, f, row, value):
                out[i + n, f, row : row + ROWS, :] = value

            gather_columns([loader(cells, at + i + n) for n in range(PAIR)], columns, 8 * i, side)
            update(cells, at + i, PAIR, weights, put)

        take_edges(many, cells, lambda p, at=at: at + p, columns, shared, row)

    outer_limit = jnp.where(odd == 1, range_ref[0, 1], range_ref[0, 0])
    shared[limit : limit + 8, :] = jnp.full((8, side), outer_limit, jnp.int32).astype(jnp.float32)
    shared[brought:total, :] = came[0 : total - brought, :]


def home_patches(old_range, old_cells, came, margin, per_device):
    side = old_cells.shape[3]
    total = layout(margin, per_device)[-1]
    return pl.pallas_call(
        functools.partial(home_kernel, margin),
        in_specs=[SMEM, HBM, VMEM],
        out_specs=[VMEM] * 3,
        out_shape=[
            jax.ShapeDtypeStruct((total, side), jnp.float32),
            jax.ShapeDtypeStruct((margin, 3, side, side), jnp.float32),
            jax.ShapeDtypeStruct((per_device, 3, side, side), jnp.float32),
        ],
        scratch_shapes=[
            pltpu.VMEM((margin + per_device, 4, side, side), jnp.float32),
            pltpu.VMEM((side, side), jnp.float32),
            pltpu.VMEM((2 * side, 6 * side), jnp.bfloat16),
            pltpu.SemaphoreType.DMA((margin + per_device,)),
        ],
        cost_estimate=cost(margin + per_device, side),
        compiler_params=room(48),
        name="home",
    )(old_range, old_cells, came)


def entries_of(table, sides, lanes):
    count = table.shape[0]
    return jnp.concatenate([jnp.broadcast_to(table[:, s : s + 1], (count, lanes)) for s in range(sides)], axis=0)


def grid_iota(rows, lanes, axis):
    return lax.broadcasted_iota(jnp.int32, (rows, lanes), axis)


def flag(where):
    return jnp.where(where, 1.0, 0.0)


def ranks(masks):
    rows, lanes = masks[0].shape
    earlier = flag(grid_iota(rows, lanes, 1) < grid_iota(rows, lanes, 0)).astype(jnp.bfloat16)
    stacked = jnp.concatenate(masks, axis=1).astype(jnp.bfloat16)
    if rows < lanes:
        stacked = jnp.concatenate([stacked, jnp.zeros((lanes - rows, stacked.shape[1]), jnp.bfloat16)], axis=0)
    counted = product(earlier, stacked)
    return [counted[:, n * lanes : (n + 1) * lanes] for n in range(len(masks))]


def edge_places(row, count, patch):
    s = row // count
    return 4 * count * (s % 2) + s // 2, 2.0 * patch


def edges_of_field(edges, f):
    tiles = edges.shape[0] // 8
    return [edges[pl.ds(2 * f + parity, tiles, stride=8), :] for parity in range(2)]


def answer_kernel(margin, count, range_ref, mine, theirs, came, edges, message):
    side = edges.shape[1]
    home, limit, brought, _ = layout(margin, count)
    inner = 0
    me, odd = position()
    start, stop = range_ref[0, 0], range_ref[0, 1]
    even = odd == 0
    at_me = pl.multiple_of(16 * count * odd, 16)
    at_them = pl.multiple_of(16 * count * (1 - odd), 16)
    edges[pl.ds(at_me, 16 * count), :] = mine[home : home + 16 * count, :]
    edges[pl.ds(at_them, 16 * count), :] = theirs[home : home + 16 * count, :]
    their_limit = theirs[limit : limit + 8, :]
    low, high = 0, count - margin
    for m in range(margin):
        l = jnp.where(even, high, low) + m
        g = me * count + l
        taken = jnp.where(even, g >= stop, g < start)
        to = pl.multiple_of(at_me + 16 * l, 16)
        from_pair = theirs[inner + 16 * m : inner + 16 * (m + 1), :]
        edges[pl.ds(to, 16), :] = jnp.where(taken, from_pair, edges[pl.ds(to, 16), :])
        l = jnp.where(even, low, high) + m
        g = (me + 1 - 2 * odd) * count + l
        taken = jnp.where(even, g < stop, g >= start)
        to = pl.multiple_of(at_them + 16 * l, 16)
        from_pair = mine[inner + 16 * m : inner + 16 * (m + 1), :]
        edges[pl.ds(to, 16), :] = jnp.where(taken, from_pair, edges[pl.ds(to, 16), :])
        l = jnp.where(even, low, high) + m
        g = me * count + l
        taken = jnp.where(even, g < start, g >= stop)
        to = pl.multiple_of(at_me + 16 * l, 16)
        crossed = mine[brought + 16 * m : brought + 16 * (m + 1), :]
        edges[pl.ds(to, 16), :] = jnp.where(taken, crossed, edges[pl.ds(to, 16), :])
        l = jnp.where(even, high, low) + m
        g = ((me + 1 - 2 * odd) * count + l).astype(jnp.float32)
        to = pl.multiple_of(at_them + 16 * l, 16)
        taken = jnp.where(even, g - their_limit, their_limit - g - 1.0) >= 0.0
        for half in range(2):
            crossed = theirs[brought + 16 * m + 8 * half : brought + 16 * m + 8 * half + 8, :]
            at = pl.multiple_of(to + 8 * half, 8)
            edges[pl.ds(at, 8), :] = jnp.where(taken, crossed, edges[pl.ds(at, 8), :])
    sides, total = 4, 8 * count
    row = grid_iota(total, side, 0)
    lane = grid_iota(total, side, 1)
    which, within = row // (sides * count), row % (sides * count)
    at = 16 * margin
    turned = jnp.transpose(jnp.concatenate([came[at : at + 16, :], jnp.zeros((side - 16, side), jnp.float32)], axis=0))
    tables = [turned[0:count, 8 * n : 8 * n + sides] for n in range(2)]
    listed = jnp.concatenate([entries_of(table, sides, side) for table in tables], axis=0)
    patch = listed - (2 * count * (me // 2)).astype(jnp.float32)
    held = [(patch >= n * count) & (patch < (n + 1) * count) for n in range(2)]
    masks = [
        flag((which == 0) & held[0]),
        jnp.where(even, flag((which == 1) & held[0]), flag((which == 0) & held[1])),
        flag((which == 1) & held[1]),
    ]
    chosen = jnp.zeros((total, side), jnp.float32)
    for k, (mask, rank) in enumerate(zip(masks, ranks(masks))):
        slot = (lane - k * CAP).astype(jnp.float32)
        chosen = chosen + jnp.where((lane // CAP == k) & (rank == slot), mask, 0.0)
    place, twice = edge_places(within, count, patch)
    hot = flag(lane.astype(jnp.float32) == place.astype(jnp.float32) + twice).astype(jnp.bfloat16)
    slots = jnp.transpose(chosen)[0:32, :].astype(jnp.bfloat16)
    picked = product(slots, hot).astype(jnp.bfloat16)
    picked = jnp.concatenate([picked] * 3, axis=1)
    for f in range(4):
        values = jnp.concatenate(edges_of_field(edges, f), axis=0)
        high = values.astype(jnp.bfloat16)
        left = values - high.astype(jnp.float32)
        mid = left.astype(jnp.bfloat16)
        low = (left - mid.astype(jnp.float32)).astype(jnp.bfloat16)
        taken = product(picked, jnp.concatenate([high, mid, low], axis=0))
        message[3 * CAP * f : 3 * CAP * (f + 1), :] = taken[0 : 3 * CAP, :]


def answers(old_range, mine, theirs, came, margin, per_device):
    side = mine.shape[1]
    return pl.pallas_call(
        functools.partial(answer_kernel, margin, per_device),
        in_specs=[SMEM, VMEM, VMEM, VMEM],
        out_specs=[VMEM, VMEM],
        out_shape=[
            jax.ShapeDtypeStruct((32 * per_device, side), jnp.float32),
            jax.ShapeDtypeStruct((12 * CAP, side), jnp.float32),
        ],
        compiler_params=room(4),
        name="answers",
    )(old_range, mine, theirs, came)


def prepare_kernel(table, edges, places, hot, near, walls, turn):
    me, odd = position()
    fill_places(places)
    sides, count = table.shape
    side = edges.shape[1]
    total = sides * count
    even = odd == 0
    row, lane = grid_iota(total, side, 0), grid_iota(total, side, 1)
    s, p = row // count, row % count
    turn[...] = jnp.zeros_like(turn)
    turn[0:sides, 0:count] = table[...].astype(jnp.float32)
    listed = entries_of(jnp.transpose(turn[...])[0:count, :], sides, side)
    wall = listed < 0.0
    patch = listed - (2 * count * (me // 2)).astype(jnp.float32)
    distance = listed - (count * me).astype(jnp.float32)
    first = 4 * count * 2
    step = 3 * CAP
    lists = (
        (-2, -2, first, first + step + 2 * CAP),
        (-1, 1, first + CAP, first + CAP),
        (2, 2, first + step, first + 2 * CAP),
    )
    masks, starts = [], []
    for far_even, far_odd, at_even, at_odd in lists:
        low = (count * jnp.where(even, far_even, far_odd)).astype(jnp.float32)
        masks.append(flag(~wall & (distance >= low) & (distance < low + count)))
        starts.append(jnp.where(even, at_even, at_odd).astype(jnp.float32))
    across = jnp.zeros((total, side), jnp.float32)
    for mask, rank, start in zip(masks, ranks(masks), starts):
        across = across + mask * (rank + start)
    place, twice = edge_places(row, count, patch)
    own = 4 * count * (1 - s % 2) + 2 * (count * odd + p) + s // 2
    inside = (patch >= 0.0) & (patch < 2.0 * count)
    index = jnp.where(inside, place.astype(jnp.float32) + twice, across)
    index = jnp.where(wall, own.astype(jnp.float32), index)
    lane = lane.astype(jnp.float32)
    walls[...] = flag(wall)
    far = flag(lane + first == index)
    hot[...] = jnp.concatenate([far, far], axis=1).astype(jnp.bfloat16)
    at_home = flag(lane == index)
    at_home = jnp.concatenate([at_home, at_home], axis=1).astype(jnp.bfloat16)
    for f in range(4):
        near[total * f : total * (f + 1), :] = product(at_home, halves(jnp.concatenate(edges_of_field(edges, f), axis=0)))


def halves(values):
    high = values.astype(jnp.bfloat16)
    low = (values - high.astype(jnp.float32)).astype(jnp.bfloat16)
    return jnp.concatenate([high, low], axis=0)


def prepared(table, edges):
    side = edges.shape[1]
    total = table.shape[0] * table.shape[1]
    return pl.pallas_call(
        prepare_kernel,
        in_specs=[VMEM] * 2,
        out_specs=[VMEM] * 4,
        out_shape=[
            jax.ShapeDtypeStruct((2 * side, 6 * side), jnp.bfloat16),
            jax.ShapeDtypeStruct((total, 2 * side), jnp.bfloat16),
            jax.ShapeDtypeStruct((4 * total, side), jnp.float32),
            jax.ShapeDtypeStruct((total, side), jnp.float32),
        ],
        scratch_shapes=[pltpu.VMEM((side, side), jnp.float32)],
        compiler_params=room(4),
        name="prepare",
    )(table, edges)


def rim_terms(hot, near, walls, edges, crossed, passed, columns, lines, turn, count, odd):
    side = edges.shape[1]
    total, step = walls.shape[0], 3 * CAP
    outside = []
    for f in range(4):
        parts = [ref[step * f : step * (f + 1), :] for ref in (crossed, passed)]
        parts.append(jnp.zeros((side - 2 * step, side), jnp.float32))
        far = product(hot[...], halves(jnp.concatenate(parts, axis=0)))
        outside.append(near[total * f : total * (f + 1), :] + far)
    wall = walls[...] > 0.0
    turn[...] = jnp.zeros_like(turn)
    lines[...] = jnp.zeros_like(lines)
    for s in range(4):
        parity = 1 - s % 2
        sign = 1.0 - 2.0 * parity
        axis = s // 2
        normal, across = (1, 2) if axis == 0 else (2, 1)

        at = slice(count * s, count * (s + 1))

        def both(f):
            row = 8 * axis + 2 * f + parity
            return edges[pl.ds(16 * count * odd + row, count, stride=16), :], outside[f][at]

        hc, hg = both(0)
        nc, ng = both(normal)
        ng = jnp.where(wall[at], -ng, ng)
        ac, ag = both(across)
        bc, bg = both(3)
        rc, rg = lax.rsqrt(hc), lax.rsqrt(hg)
        uc, ug = nc * rc * rc, ng * rg * rg
        top = jnp.maximum(jnp.abs(uc) + hc * rc, jnp.abs(ug) + hg * rg)
        fc, fg = nc * uc + 0.5 * hc * hc, ng * ug + 0.5 * hg * hg
        c_h = -HALF * (sign * (nc + ng) - top * ((hg + bg) - (hc + bc)))
        c_n = -HALF * (sign * (fc + fg + hc * bg) - top * (ng - nc))
        c_t = -HALF * (sign * (ac * uc + ag * ug) - top * (ag - ac))
        for f, value in ((0, c_h), (normal, c_n), (across, c_t)):
            target = turn if axis == 0 else lines
            target[pl.ds(2 * f + parity, count, stride=8), :] = value
    turn[...] = jnp.transpose(turn[...])
    side = turn.shape[0]
    columns[...] = pieces(jnp.concatenate([turn[spread(j, side), :] for j in range(side // ROWS)], axis=0))


def fill_places(places):
    side = places.shape[0] // 2
    row = lax.broadcasted_iota(jnp.int32, (side, side), 0) % 16
    lane = lax.broadcasted_iota(jnp.int32, (side, side), 1)
    source = row - jnp.where(lane == 0, 1, jnp.where(lane == side - 1, 0, 1024))
    for u in range(2):
        for f in range(3):
            block = jnp.where(source == 8 * u + 2 * f, 1.0, 0.0).astype(jnp.bfloat16)
            for half in range(2):
                at = (3 * u + f) * side
                places[half * side : (half + 1) * side, at : at + side] = block


def final_kernel(
    margin, range_ref, places, hot, near, walls, edges, crossed, passed, own, theirs, came, arrived, out,
    result, turn, columns, lines, sems,
):
    count, side = own.shape[0], lines.shape[1]
    me, odd = position()
    even = odd == 0
    rim_terms(hot, near, walls, edges, crossed, passed, columns, lines, turn, count, odd)
    start, stop = range_ref[0, 0], range_ref[0, 1]
    line = iota(0, side)
    lane = lax.broadcasted_iota(jnp.int32, (side, 2 * side), 1) % side
    steps = side // ROWS
    results = bundle_layout(margin)[1]

    def copy(p):
        return pltpu.make_async_copy(result.at[p], out.at[p], sems.at[p])

    for group in range(0, count, margin):
        patches = range(group, group + margin)
        held = columns[...]
        masked = [held * jnp.where(lane // 16 == p // 2, 1.0, 0.0).astype(jnp.bfloat16) for p in patches[::2]]
        terms = product(jnp.concatenate(masked, axis=0), places[...])
        for m, p in enumerate(patches):
            if group == 0:
                taken = me * count + p < start
            elif group == count - margin:
                taken = me * count + p >= stop
            else:
                taken = None
            beside = even if group else odd == 1
            for f in range(3):
                for j in range(steps):
                    rows = slice(ROWS * j, ROWS * (j + 1))
                    value = own[p, f, rows, :]
                    if taken is not None:
                        if m < FIRST:
                            at = results + (3 * m + f) * side + ROWS * j
                            crossing = came[at : at + ROWS, :]
                        else:
                            crossing = arrived[m - FIRST, f, rows, :]
                        moved = jnp.where(beside, theirs[m, f, rows, :], crossing)
                        value = jnp.where(taken, moved, value)
                    at = side * (m // 2) + ROWS * j
                    block = 3 * (m % 2) + f
                    value = value + terms[at : at + ROWS, block * side : (block + 1) * side]
                    if j == 0:
                        south = lines[8 * p + 2 * f + 1 : 8 * p + 2 * f + 2, :]
                        value = value + jnp.where(line == 0, south, 0.0)
                    if j == steps - 1:
                        north = lines[8 * p + 2 * f : 8 * p + 2 * f + 1, :]
                        value = value + jnp.where(line == ROWS - 1, north, 0.0)
                    result[p, f, spread(j, side), :] = value
            copy(p).start()
    for p in range(count):
        copy(p).wait()


def finished(old_range, ready, edges, crossed, passed, own, theirs, came, arrived, margin):
    count, _, side, _ = own.shape
    return pl.pallas_call(
        functools.partial(final_kernel, margin),
        in_specs=[SMEM] + [VMEM] * 11,
        out_specs=HBM,
        out_shape=jax.ShapeDtypeStruct(own.shape, jnp.float32),
        scratch_shapes=[
            pltpu.VMEM(own.shape, jnp.float32),
            pltpu.VMEM((side, side), jnp.float32),
            pltpu.VMEM((side, 2 * side), jnp.bfloat16),
            pltpu.VMEM((side, side), jnp.float32),
            pltpu.SemaphoreType.DMA((count,)),
        ],
        compiler_params=room(12),
        name="final",
    )(old_range, *ready, edges, crossed, passed, own, theirs, came, arrived)


def swapped(value, first):
    pairs = [(i, i + 1) for i in range(first, lax.axis_size(AXES) - 1, 2)]
    return lax.ppermute(value, AXES, pairs + [(j, i) for i, j in pairs])


def local(old_cells, old_range, neighbours):
    per_device = neighbours.shape[0]
    margin = (old_cells.shape[0] - per_device) // 2
    table = neighbours.T
    their_table = swapped(table, 0)
    rest, bundle = outer_patches(old_cells, margin)
    bundle = with_tables(bundle, table, their_table, margin)
    came = swapped(bundle, 1)
    arrived = swapped(after(rest, bundle), 1)
    shared, inner, own = home_patches(old_range, old_cells, came, margin, per_device)
    their_edges = swapped(shared, 0)
    theirs = swapped(inner, 0)
    edges, message = answers(old_range, shared, their_edges, came, margin, per_device)
    crossed = swapped(message, 1)
    passed = swapped(crossed, 0)
    return finished(old_range, prepared(table, edges), edges, crossed, passed, own, theirs, came, arrived, margin)


def solution(mesh):
    placed = (
        P(("member", "curve", "sub"), None, None, None),
        P(("member", "curve", "sub"), None),
        P(("member", "curve", "sub"), None),
    )
    return jax.shard_map(
        local,
        mesh=mesh,
        in_specs=placed,
        out_specs=P(("member", "curve", "sub"), None, None, None),
        check_vma=False,
    )
```

```python
import functools

import jax
import jax.numpy as jnp
from jax import lax
from jax.experimental import pallas as pl
from jax.experimental.pallas import tpu as pltpu
from jax.sharding import PartitionSpec as P

RATE_STEP = 0.1
HALF = 0.5 * RATE_STEP
AXES = ("curve", "sub")
CAP = 8
ROWS = 8
PAIR = 2
GROUP = 4
FIRST = 0
VMEM = pl.BlockSpec(memory_space=pltpu.VMEM)
SMEM = pl.BlockSpec(memory_space=pltpu.SMEM)
HBM = pl.BlockSpec(memory_space=pltpu.HBM)


def position():
    me = lax.axis_index(AXES)
    return me, lax.rem(me, 2)


def iota(axis, side):
    return lax.broadcasted_iota(jnp.int32, (ROWS, side), axis)


def spread(j, side):
    return pl.ds(j, ROWS, stride=side // ROWS)


def pieces(x):
    high = x.astype(jnp.bfloat16)
    low = (x - high.astype(jnp.float32)).astype(jnp.bfloat16)
    return jnp.concatenate([high, low], axis=1)


def product(parts, weights):
    return jnp.dot(parts, weights, preferred_element_type=jnp.float32)


AHEAD, EAST, SUMS, SLOPE = slice(0, 2), slice(2, 4), slice(4, 5), slice(5, 6)


def fill_weights(weights):
    side = weights.shape[0] // 2
    row = lax.broadcasted_iota(jnp.int32, (side, side), 0)
    lane = lax.broadcasted_iota(jnp.int32, (side, side), 1)
    one = lambda where: jnp.where(where, 1.0, 0.0)
    after, here, before = one(row == lane + 1), one(row == lane), one(row == lane - 1)
    inner_e, inner_w = lane != side - 1, lane != 0
    east = jnp.where(inner_e, after + here, 0.0)
    west = jnp.where(inner_w, here + before, 0.0)
    blocks = (
        after,
        before,
        jnp.where(inner_e, after - here, 0.0),
        jnp.where(inner_w, here - before, 0.0),
        east - west,
        after - before,
    )
    for n, block in enumerate(blocks):
        for half in range(2):
            weights[half * side : (half + 1) * side, n * side : (n + 1) * side] = block.astype(jnp.bfloat16)


def inner_update(loads, store, side, weights):
    line, lane = iota(0, side), iota(1, side)
    first, last = line == 0, line == ROWS - 1
    rim = jnp.where(lane == 0, 2.0, jnp.where(lane == side - 1, -2.0, 0.0))
    steps = side // ROWS
    many = len(loads)

    def cell(h, mx, my, bed):
        root = lax.rsqrt(h)
        celerity = h * root
        inverse = root * root
        u = mx * inverse
        v = my * inverse
        half_sq = 0.5 * h * h
        cross = my * u
        rate_y = jnp.abs(v) + celerity
        rate_x = jnp.abs(u) + celerity
        return (rate_y, h + bed, mx, my, cross, my * v + half_sq, bed), rate_x, mx * u + half_sq, h

    def face_y(low, high):
        top = jnp.maximum(low[0], high[0])
        return [
            (high[3] + low[3]) - top * (high[1] - low[1]),
            (high[4] + low[4]) - top * (high[2] - low[2]),
            (high[5] + low[5]) - top * (high[3] - low[3]),
        ]

    def taken(block):
        return weights[:, block.start * side : block.stop * side]

    cells = [cell(*[load(f, j) for f in range(4)]) for load in loads for j in range(steps)]
    stack = lambda pick: pieces(jnp.concatenate([pick(c) for c in cells], axis=0))
    eta, mx, my, cross, bed = (stack(lambda c, n=n: c[0][n]) for n in (1, 2, 3, 4, 6))
    fx = stack(lambda c: c[2])
    rates = product(stack(lambda c: c[1]), taken(AHEAD))
    jumps = product(jnp.concatenate([eta, mx, my], axis=0), taken(EAST))
    sums = product(jnp.concatenate([fx, cross], axis=0), taken(SUMS))
    slopes = product(bed, taken(SLOPE))
    for n in range(many):
        mine = cells[n * steps : (n + 1) * steps]
        low = [pltpu.roll(each, 1, 0) for each in mine[steps - 1][0]]
        faces = []
        for j in range(steps):
            faces.append(face_y(low, mine[j][0]))
            low = mine[j][0]
        faces[0] = [jnp.where(first, 0.0, each) for each in faces[0]]
        beds = [c[0][6] for c in mine]
        under = jnp.where(first, 0.0, pltpu.roll(beds[-1], 1, 0))
        over = jnp.where(last, 0.0, pltpu.roll(beds[0], ROWS - 1, 0))
        faces.append([jnp.where(last, 0.0, pltpu.roll(each, ROWS - 1, 0)) for each in faces[0]])
        for j in range(steps):
            (_, _, mx, my, _, _, _), rate, _, h = mine[j]
            at = [(q * many + n) * side + ROWS * j for q in range(3)]
            rows = [slice(r, r + ROWS) for r in at]
            top_e = jnp.maximum(rate, rates[rows[0], :side])
            top_w = jnp.maximum(rate, rates[rows[0], side:])
            total = [jumps[rows[1], :side] + jumps[rows[1], side:] + rim * mx, sums[rows[0]], sums[rows[1]]]
            x = [t - (top_e * jumps[r, :side] - top_w * jumps[r, side:]) for t, r in zip(total, rows)]
            south, north = faces[j], faces[j + 1]
            slope_y = (beds[j + 1] if j + 1 < steps else over) - (beds[j - 1] if j else under)
            store(n, 0, j, h - HALF * (x[0] + (north[0] - south[0])))
            store(n, 1, j, mx - HALF * (x[1] + h * slopes[rows[0]] + (north[1] - south[1])))
            store(n, 2, j, my - HALF * (x[2] + h * slope_y + (north[2] - south[2])))


def gather_columns(loads, columns, first_at, side):
    pair = iota(1, side) // 2
    for j in range(side // ROWS):
        held = columns[spread(j, side), :]
        for n, load in enumerate(loads):
            at = first_at + 8 * n
            for f in range(4):
                held = jnp.where(pair == at // 2 + f, pltpu.roll(load(f, j), at + 2 * f + 1, 1), held)
        columns[spread(j, side), :] = held


def take_edges(count, cells, slot_of, columns, edges, base):
    side = columns.shape[0]
    turned = jnp.transpose(columns[...])
    for p in range(count):
        edges[base + 16 * p : base + 16 * p + 8, :] = turned[8 * p : 8 * p + 8, :]
        for f in range(4):
            row = base + 16 * p + 8 + 2 * f
            edges[row : row + 1, :] = cells[slot_of(p), f, side - 1 : side, :]
            edges[row + 1 : row + 2, :] = cells[slot_of(p), f, 0:1, :]


def loader(cells, i):
    side = cells.shape[3]
    return lambda f, j: cells[i, f, spread(j, side), :]


def update(cells, first, many, weights, put):
    loads = [loader(cells, first + n) for n in range(many)]
    inner_update(loads, lambda n, f, j, value: put(n, f, ROWS * j, value), cells.shape[3], weights)


def fetch(cells_hbm, first, cells, sems, parts):
    def copy(i):
        return pltpu.make_async_copy(cells_hbm.at[first + i], cells.at[i], sems.at[i])

    for start, count in parts:
        for i in range(count):
            copy(start + i).start()
    return copy


def outer_slot(cells_hbm, margin):
    _, odd = position()
    return odd * (cells_hbm.shape[0] - margin)


def bundle_layout(margin):
    tables = 16 * margin
    return tables, tables + 16


def outer_kernel(margin, cells_hbm, rest, bundle, cells, columns, weights, sems):
    side = columns.shape[0]
    copy = fetch(cells_hbm, outer_slot(cells_hbm, margin), cells, sems, [(0, margin)])
    fill_weights(weights)
    results = bundle_layout(margin)[1]
    for i in range(0, margin, PAIR):
        for n in range(PAIR):
            copy(i + n).wait()

        def put(n, f, row, value, i=i):
            if i + n < FIRST:
                at = results + (3 * (i + n) + f) * side + row
                bundle[at : at + ROWS, :] = value
            else:
                rest[i + n - FIRST, f, row : row + ROWS, :] = value

        gather_columns([loader(cells, i + n) for n in range(PAIR)], columns, 8 * i, side)
        update(cells, i, PAIR, weights, put)

    take_edges(margin, cells, lambda p: p, columns, bundle, 0)


def cost(patches, side):
    return pl.CostEstimate(
        flops=patches * side * side * 800,
        bytes_accessed=patches * side * side * 28,
        transcendentals=patches * side * side,
    )


def room(mebibytes):
    return pltpu.CompilerParams(vmem_limit_bytes=mebibytes << 20)


def outer_patches(old_cells, margin):
    side = old_cells.shape[3]
    return pl.pallas_call(
        functools.partial(outer_kernel, margin),
        in_specs=[HBM],
        out_specs=[VMEM, VMEM],
        out_shape=[
            jax.ShapeDtypeStruct((margin - FIRST, 3, side, side), jnp.float32),
            jax.ShapeDtypeStruct((bundle_layout(margin)[1] + 3 * FIRST * side, side), jnp.float32),
        ],
        scratch_shapes=[
            pltpu.VMEM((margin, 4, side, side), jnp.float32),
            pltpu.VMEM((side, side), jnp.float32),
            pltpu.VMEM((2 * side, 6 * side), jnp.bfloat16),
            pltpu.SemaphoreType.DMA((margin,)),
        ],
        cost_estimate=cost(margin, side),
        compiler_params=room(48),
        name="outer",
    )(old_cells)


def with_tables(bundle, table, their_table, margin):
    any_place = pl.BlockSpec(memory_space=pl.ANY)
    start, end = bundle_layout(margin)
    sides, count = table.shape

    def kernel(bundle_ref, table_ref, their_ref, out_ref, held, sem):
        _, odd = position()
        held[...] = jnp.zeros_like(held)
        for which, ref in ((odd, table_ref), (1 - odd, their_ref)):
            held[pl.ds(pl.multiple_of(8 * which, 8), sides), 0:count] = ref[...].astype(jnp.float32)
        copy = pltpu.make_async_copy(held, out_ref.at[start:end, :], sem)
        copy.start()
        copy.wait()

    return pl.pallas_call(
        kernel,
        in_specs=[any_place, VMEM, VMEM],
        out_specs=any_place,
        out_shape=jax.ShapeDtypeStruct(bundle.shape, bundle.dtype),
        scratch_shapes=[pltpu.VMEM((end - start, bundle.shape[1]), jnp.float32), pltpu.SemaphoreType.DMA],
        input_output_aliases={0: 0},
        compiler_params=room(4),
        name="tables",
    )(bundle, table, their_table)


def after(value, other):
    any_place = pl.BlockSpec(memory_space=pl.ANY)
    return pl.pallas_call(
        lambda value_ref, other_ref, out_ref: None,
        in_specs=[any_place, any_place],
        out_specs=any_place,
        out_shape=jax.ShapeDtypeStruct(value.shape, value.dtype),
        input_output_aliases={0: 0},
        compiler_params=room(4),
        name="after",
    )(value, other)


def layout(margin, per_device):
    home = 16 * margin
    limit = home + 16 * per_device
    brought = limit + 8
    return home, limit, brought, brought + 16 * margin


def home_kernel(margin, range_ref, cells_hbm, came, shared, inner, own, cells, columns, weights, sems):
    side = columns.shape[0]
    count = own.shape[0]
    home, limit, brought, total = layout(margin, count)
    _, odd = position()
    inner_at = (1 - odd) * count
    home_at = odd * margin
    parts = [(inner_at, margin), (home_at, count)]
    copy = fetch(cells_hbm, (1 - odd) * margin, cells, sems, parts)
    fill_weights(weights)

    for at, many, out, row in ((inner_at, margin, inner, 0), (home_at, count, own, home)):

        @pl.loop(0, many // GROUP)
        def _(step, at=at, out=out):
            i = step * GROUP
            for n in range(GROUP):
                copy(at + i + n).wait()

            def put(n, f, row, value):
                out[i + n, f, row : row + ROWS, :] = value

            gather_columns([loader(cells, at + i + n) for n in range(GROUP)], columns, 8 * i, side)
            update(cells, at + i, GROUP, weights, put)

        take_edges(many, cells, lambda p, at=at: at + p, columns, shared, row)

    outer_limit = jnp.where(odd == 1, range_ref[0, 1], range_ref[0, 0])
    shared[limit : limit + 8, :] = jnp.full((8, side), outer_limit, jnp.int32).astype(jnp.float32)
    shared[brought:total, :] = came[0 : total - brought, :]


def home_patches(old_range, old_cells, came, margin, per_device):
    side = old_cells.shape[3]
    total = layout(margin, per_device)[-1]
    return pl.pallas_call(
        functools.partial(home_kernel, margin),
        in_specs=[SMEM, HBM, VMEM],
        out_specs=[VMEM] * 3,
        out_shape=[
            jax.ShapeDtypeStruct((total, side), jnp.float32),
            jax.ShapeDtypeStruct((margin, 3, side, side), jnp.float32),
            jax.ShapeDtypeStruct((per_device, 3, side, side), jnp.float32),
        ],
        scratch_shapes=[
            pltpu.VMEM((margin + per_device, 4, side, side), jnp.float32),
            pltpu.VMEM((side, side), jnp.float32),
            pltpu.VMEM((2 * side, 6 * side), jnp.bfloat16),
            pltpu.SemaphoreType.DMA((margin + per_device,)),
        ],
        cost_estimate=cost(margin + per_device, side),
        compiler_params=room(48),
        name="home",
    )(old_range, old_cells, came)


def entries_of(table, sides, lanes):
    count = table.shape[0]
    return jnp.concatenate([jnp.broadcast_to(table[:, s : s + 1], (count, lanes)) for s in range(sides)], axis=0)


def grid_iota(rows, lanes, axis):
    return lax.broadcasted_iota(jnp.int32, (rows, lanes), axis)


def flag(where):
    return jnp.where(where, 1.0, 0.0)


def ranks(masks):
    rows, lanes = masks[0].shape
    earlier = flag(grid_iota(rows, lanes, 1) < grid_iota(rows, lanes, 0)).astype(jnp.bfloat16)
    stacked = jnp.concatenate(masks, axis=1).astype(jnp.bfloat16)
    if rows < lanes:
        stacked = jnp.concatenate([stacked, jnp.zeros((lanes - rows, stacked.shape[1]), jnp.bfloat16)], axis=0)
    counted = product(earlier, stacked)
    return [counted[:, n * lanes : (n + 1) * lanes] for n in range(len(masks))]


def edge_places(row, count, patch):
    s = row // count
    return 4 * count * (s % 2) + s // 2, 2.0 * patch


def edges_of_field(edges, f):
    tiles = edges.shape[0] // 8
    return [edges[pl.ds(2 * f + parity, tiles, stride=8), :] for parity in range(2)]


def answer_kernel(margin, count, range_ref, mine, theirs, came, edges, message):
    side = edges.shape[1]
    home, limit, brought, _ = layout(margin, count)
    inner = 0
    me, odd = position()
    start, stop = range_ref[0, 0], range_ref[0, 1]
    even = odd == 0
    at_me = pl.multiple_of(16 * count * odd, 16)
    at_them = pl.multiple_of(16 * count * (1 - odd), 16)
    edges[pl.ds(at_me, 16 * count), :] = mine[home : home + 16 * count, :]
    edges[pl.ds(at_them, 16 * count), :] = theirs[home : home + 16 * count, :]
    their_limit = theirs[limit : limit + 8, :]
    low, high = 0, count - margin
    for m in range(margin):
        l = jnp.where(even, high, low) + m
        g = me * count + l
        taken = jnp.where(even, g >= stop, g < start)
        to = pl.multiple_of(at_me + 16 * l, 16)
        from_pair = theirs[inner + 16 * m : inner + 16 * (m + 1), :]
        edges[pl.ds(to, 16), :] = jnp.where(taken, from_pair, edges[pl.ds(to, 16), :])
        l = jnp.where(even, low, high) + m
        g = (me + 1 - 2 * odd) * count + l
        taken = jnp.where(even, g < stop, g >= start)
        to = pl.multiple_of(at_them + 16 * l, 16)
        from_pair = mine[inner + 16 * m : inner + 16 * (m + 1), :]
        edges[pl.ds(to, 16), :] = jnp.where(taken, from_pair, edges[pl.ds(to, 16), :])
        l = jnp.where(even, low, high) + m
        g = me * count + l
        taken = jnp.where(even, g < start, g >= stop)
        to = pl.multiple_of(at_me + 16 * l, 16)
        crossed = mine[brought + 16 * m : brought + 16 * (m + 1), :]
        edges[pl.ds(to, 16), :] = jnp.where(taken, crossed, edges[pl.ds(to, 16), :])
        l = jnp.where(even, high, low) + m
        g = ((me + 1 - 2 * odd) * count + l).astype(jnp.float32)
        to = pl.multiple_of(at_them + 16 * l, 16)
        taken = jnp.where(even, g - their_limit, their_limit - g - 1.0) >= 0.0
        for half in range(2):
            crossed = theirs[brought + 16 * m + 8 * half : brought + 16 * m + 8 * half + 8, :]
            at = pl.multiple_of(to + 8 * half, 8)
            edges[pl.ds(at, 8), :] = jnp.where(taken, crossed, edges[pl.ds(at, 8), :])
    sides, total = 4, 8 * count
    row = grid_iota(total, side, 0)
    lane = grid_iota(total, side, 1)
    which, within = row // (sides * count), row % (sides * count)
    at = 16 * margin
    turned = jnp.transpose(jnp.concatenate([came[at : at + 16, :], jnp.zeros((side - 16, side), jnp.float32)], axis=0))
    tables = [turned[0:count, 8 * n : 8 * n + sides] for n in range(2)]
    listed = jnp.concatenate([entries_of(table, sides, side) for table in tables], axis=0)
    patch = listed - (2 * count * (me // 2)).astype(jnp.float32)
    held = [(patch >= n * count) & (patch < (n + 1) * count) for n in range(2)]
    masks = [
        flag((which == 0) & held[0]),
        jnp.where(even, flag((which == 1) & held[0]), flag((which == 0) & held[1])),
        flag((which == 1) & held[1]),
    ]
    chosen = jnp.zeros((total, side), jnp.float32)
    for k, (mask, rank) in enumerate(zip(masks, ranks(masks))):
        slot = (lane - k * CAP).astype(jnp.float32)
        chosen = chosen + jnp.where((lane // CAP == k) & (rank == slot), mask, 0.0)
    place, twice = edge_places(within, count, patch)
    hot = flag(lane.astype(jnp.float32) == place.astype(jnp.float32) + twice).astype(jnp.bfloat16)
    slots = jnp.transpose(chosen)[0:32, :].astype(jnp.bfloat16)
    picked = product(slots, hot).astype(jnp.bfloat16)
    picked = jnp.concatenate([picked] * 3, axis=1)
    for f in range(4):
        values = jnp.concatenate(edges_of_field(edges, f), axis=0)
        high = values.astype(jnp.bfloat16)
        left = values - high.astype(jnp.float32)
        mid = left.astype(jnp.bfloat16)
        low = (left - mid.astype(jnp.float32)).astype(jnp.bfloat16)
        taken = product(picked, jnp.concatenate([high, mid, low], axis=0))
        message[3 * CAP * f : 3 * CAP * (f + 1), :] = taken[0 : 3 * CAP, :]


def answers(old_range, mine, theirs, came, margin, per_device):
    side = mine.shape[1]
    return pl.pallas_call(
        functools.partial(answer_kernel, margin, per_device),
        in_specs=[SMEM, VMEM, VMEM, VMEM],
        out_specs=[VMEM, VMEM],
        out_shape=[
            jax.ShapeDtypeStruct((32 * per_device, side), jnp.float32),
            jax.ShapeDtypeStruct((12 * CAP, side), jnp.float32),
        ],
        compiler_params=room(4),
        name="answers",
    )(old_range, mine, theirs, came)


def prepare_kernel(table, edges, places, hot, near, walls, turn):
    me, odd = position()
    fill_places(places)
    sides, count = table.shape
    side = edges.shape[1]
    total = sides * count
    even = odd == 0
    row, lane = grid_iota(total, side, 0), grid_iota(total, side, 1)
    s, p = row // count, row % count
    turn[...] = jnp.zeros_like(turn)
    turn[0:sides, 0:count] = table[...].astype(jnp.float32)
    listed = entries_of(jnp.transpose(turn[...])[0:count, :], sides, side)
    wall = listed < 0.0
    patch = listed - (2 * count * (me // 2)).astype(jnp.float32)
    distance = listed - (count * me).astype(jnp.float32)
    first = 4 * count * 2
    step = 3 * CAP
    lists = (
        (-2, -2, first, first + step + 2 * CAP),
        (-1, 1, first + CAP, first + CAP),
        (2, 2, first + step, first + 2 * CAP),
    )
    masks, starts = [], []
    for far_even, far_odd, at_even, at_odd in lists:
        low = (count * jnp.where(even, far_even, far_odd)).astype(jnp.float32)
        masks.append(flag(~wall & (distance >= low) & (distance < low + count)))
        starts.append(jnp.where(even, at_even, at_odd).astype(jnp.float32))
    across = jnp.zeros((total, side), jnp.float32)
    for mask, rank, start in zip(masks, ranks(masks), starts):
        across = across + mask * (rank + start)
    place, twice = edge_places(row, count, patch)
    own = 4 * count * (1 - s % 2) + 2 * (count * odd + p) + s // 2
    inside = (patch >= 0.0) & (patch < 2.0 * count)
    index = jnp.where(inside, place.astype(jnp.float32) + twice, across)
    index = jnp.where(wall, own.astype(jnp.float32), index)
    lane = lane.astype(jnp.float32)
    walls[...] = flag(wall)
    far = flag(lane + first == index)
    hot[...] = jnp.concatenate([far, far], axis=1).astype(jnp.bfloat16)
    at_home = flag(lane == index)
    at_home = jnp.concatenate([at_home, at_home], axis=1).astype(jnp.bfloat16)
    for f in range(4):
        near[total * f : total * (f + 1), :] = product(at_home, halves(jnp.concatenate(edges_of_field(edges, f), axis=0)))


def halves(values):
    high = values.astype(jnp.bfloat16)
    low = (values - high.astype(jnp.float32)).astype(jnp.bfloat16)
    return jnp.concatenate([high, low], axis=0)


def prepared(table, edges):
    side = edges.shape[1]
    total = table.shape[0] * table.shape[1]
    return pl.pallas_call(
        prepare_kernel,
        in_specs=[VMEM] * 2,
        out_specs=[VMEM] * 4,
        out_shape=[
            jax.ShapeDtypeStruct((2 * side, 6 * side), jnp.bfloat16),
            jax.ShapeDtypeStruct((total, 2 * side), jnp.bfloat16),
            jax.ShapeDtypeStruct((4 * total, side), jnp.float32),
            jax.ShapeDtypeStruct((total, side), jnp.float32),
        ],
        scratch_shapes=[pltpu.VMEM((side, side), jnp.float32)],
        compiler_params=room(4),
        name="prepare",
    )(table, edges)


def rim_terms(hot, near, walls, edges, crossed, passed, columns, lines, turn, count, odd):
    side = edges.shape[1]
    total, step = walls.shape[0], 3 * CAP
    outside = []
    for f in range(4):
        parts = [ref[step * f : step * (f + 1), :] for ref in (crossed, passed)]
        parts.append(jnp.zeros((side - 2 * step, side), jnp.float32))
        far = product(hot[...], halves(jnp.concatenate(parts, axis=0)))
        outside.append(near[total * f : total * (f + 1), :] + far)
    wall = walls[...] > 0.0
    turn[...] = jnp.zeros_like(turn)
    lines[...] = jnp.zeros_like(lines)
    for s in range(4):
        parity = 1 - s % 2
        sign = 1.0 - 2.0 * parity
        axis = s // 2
        normal, across = (1, 2) if axis == 0 else (2, 1)

        at = slice(count * s, count * (s + 1))

        def both(f):
            row = 8 * axis + 2 * f + parity
            return edges[pl.ds(16 * count * odd + row, count, stride=16), :], outside[f][at]

        hc, hg = both(0)
        nc, ng = both(normal)
        ng = jnp.where(wall[at], -ng, ng)
        ac, ag = both(across)
        bc, bg = both(3)
        rc, rg = lax.rsqrt(hc), lax.rsqrt(hg)
        uc, ug = nc * rc * rc, ng * rg * rg
        top = jnp.maximum(jnp.abs(uc) + hc * rc, jnp.abs(ug) + hg * rg)
        fc, fg = nc * uc + 0.5 * hc * hc, ng * ug + 0.5 * hg * hg
        c_h = -HALF * (sign * (nc + ng) - top * ((hg + bg) - (hc + bc)))
        c_n = -HALF * (sign * (fc + fg + hc * bg) - top * (ng - nc))
        c_t = -HALF * (sign * (ac * uc + ag * ug) - top * (ag - ac))
        for f, value in ((0, c_h), (normal, c_n), (across, c_t)):
            target = turn if axis == 0 else lines
            target[pl.ds(2 * f + parity, count, stride=8), :] = value
    turn[...] = jnp.transpose(turn[...])
    side = turn.shape[0]
    columns[...] = pieces(jnp.concatenate([turn[spread(j, side), :] for j in range(side // ROWS)], axis=0))


def fill_places(places):
    side = places.shape[0] // 2
    row = lax.broadcasted_iota(jnp.int32, (side, side), 0) % 16
    lane = lax.broadcasted_iota(jnp.int32, (side, side), 1)
    source = row - jnp.where(lane == 0, 1, jnp.where(lane == side - 1, 0, 1024))
    for u in range(2):
        for f in range(3):
            block = jnp.where(source == 8 * u + 2 * f, 1.0, 0.0).astype(jnp.bfloat16)
            for half in range(2):
                at = (3 * u + f) * side
                places[half * side : (half + 1) * side, at : at + side] = block


def final_kernel(
    margin, range_ref, places, hot, near, walls, edges, crossed, passed, own, theirs, came, arrived, out,
    result, turn, columns, lines, sems,
):
    count, side = own.shape[0], lines.shape[1]
    me, odd = position()
    even = odd == 0
    rim_terms(hot, near, walls, edges, crossed, passed, columns, lines, turn, count, odd)
    start, stop = range_ref[0, 0], range_ref[0, 1]
    line = iota(0, side)
    lane = lax.broadcasted_iota(jnp.int32, (side, 2 * side), 1) % side
    steps = side // ROWS
    results = bundle_layout(margin)[1]

    def copy(p):
        return pltpu.make_async_copy(result.at[p], out.at[p], sems.at[p])

    for group in range(0, count, margin):
        patches = range(group, group + margin)
        held = columns[...]
        masked = [held * jnp.where(lane // 16 == p // 2, 1.0, 0.0).astype(jnp.bfloat16) for p in patches[::2]]
        terms = product(jnp.concatenate(masked, axis=0), places[...])
        for m, p in enumerate(patches):
            if group == 0:
                taken = me * count + p < start
            elif group == count - margin:
                taken = me * count + p >= stop
            else:
                taken = None
            beside = even if group else odd == 1
            for f in range(3):
                for j in range(steps):
                    rows = slice(ROWS * j, ROWS * (j + 1))
                    value = own[p, f, rows, :]
                    if taken is not None:
                        if m < FIRST:
                            at = results + (3 * m + f) * side + ROWS * j
                            crossing = came[at : at + ROWS, :]
                        else:
                            crossing = arrived[m - FIRST, f, rows, :]
                        moved = jnp.where(beside, theirs[m, f, rows, :], crossing)
                        value = jnp.where(taken, moved, value)
                    at = side * (m // 2) + ROWS * j
                    block = 3 * (m % 2) + f
                    value = value + terms[at : at + ROWS, block * side : (block + 1) * side]
                    if j == 0:
                        south = lines[8 * p + 2 * f + 1 : 8 * p + 2 * f + 2, :]
                        value = value + jnp.where(line == 0, south, 0.0)
                    if j == steps - 1:
                        north = lines[8 * p + 2 * f : 8 * p + 2 * f + 1, :]
                        value = value + jnp.where(line == ROWS - 1, north, 0.0)
                    result[p, f, spread(j, side), :] = value
            copy(p).start()
    for p in range(count):
        copy(p).wait()


def finished(old_range, ready, edges, crossed, passed, own, theirs, came, arrived, margin):
    count, _, side, _ = own.shape
    return pl.pallas_call(
        functools.partial(final_kernel, margin),
        in_specs=[SMEM] + [VMEM] * 11,
        out_specs=HBM,
        out_shape=jax.ShapeDtypeStruct(own.shape, jnp.float32),
        scratch_shapes=[
            pltpu.VMEM(own.shape, jnp.float32),
            pltpu.VMEM((side, side), jnp.float32),
            pltpu.VMEM((side, 2 * side), jnp.bfloat16),
            pltpu.VMEM((side, side), jnp.float32),
            pltpu.SemaphoreType.DMA((count,)),
        ],
        compiler_params=room(12),
        name="final",
    )(old_range, *ready, edges, crossed, passed, own, theirs, came, arrived)


def swapped(value, first):
    pairs = [(i, i + 1) for i in range(first, lax.axis_size(AXES) - 1, 2)]
    return lax.ppermute(value, AXES, pairs + [(j, i) for i, j in pairs])


def local(old_cells, old_range, neighbours):
    per_device = neighbours.shape[0]
    margin = (old_cells.shape[0] - per_device) // 2
    table = neighbours.T
    their_table = swapped(table, 0)
    rest, bundle = outer_patches(old_cells, margin)
    bundle = with_tables(bundle, table, their_table, margin)
    came = swapped(bundle, 1)
    arrived = swapped(after(rest, bundle), 1)
    shared, inner, own = home_patches(old_range, old_cells, came, margin, per_device)
    their_edges = swapped(shared, 0)
    theirs = swapped(inner, 0)
    edges, message = answers(old_range, shared, their_edges, came, margin, per_device)
    crossed = swapped(message, 1)
    passed = swapped(crossed, 0)
    return finished(old_range, prepared(table, edges), edges, crossed, passed, own, theirs, came, arrived, margin)


def solution(mesh):
    placed = (
        P(("member", "curve", "sub"), None, None, None),
        P(("member", "curve", "sub"), None),
        P(("member", "curve", "sub"), None),
    )
    return jax.shard_map(
        local,
        mesh=mesh,
        in_specs=placed,
        out_specs=P(("member", "curve", "sub"), None, None, None),
        check_vma=False,
    )
```

```python
import functools

import jax
import jax.numpy as jnp
from jax import lax
from jax.experimental import pallas as pl
from jax.experimental.pallas import tpu as pltpu
from jax.sharding import PartitionSpec as P

RATE_STEP = 0.1
HALF = 0.5 * RATE_STEP
AXES = ("curve", "sub")
CAP = 8
ROWS = 8
PAIR = 2
FIRST = 0
VMEM = pl.BlockSpec(memory_space=pltpu.VMEM)
SMEM = pl.BlockSpec(memory_space=pltpu.SMEM)
HBM = pl.BlockSpec(memory_space=pltpu.HBM)


def position():
    me = lax.axis_index(AXES)
    return me, lax.rem(me, 2)


def iota(axis, side):
    return lax.broadcasted_iota(jnp.int32, (ROWS, side), axis)


def spread(j, side):
    return pl.ds(j, ROWS, stride=side // ROWS)


def pieces(x):
    high = x.astype(jnp.bfloat16)
    low = (x - high.astype(jnp.float32)).astype(jnp.bfloat16)
    return jnp.concatenate([high, low], axis=1)


def product(parts, weights):
    return jnp.dot(parts, weights, preferred_element_type=jnp.float32)


AHEAD, EAST, SUMS, SLOPE = slice(0, 2), slice(2, 4), slice(4, 5), slice(5, 6)


def fill_weights(weights):
    side = weights.shape[0] // 2
    row = lax.broadcasted_iota(jnp.int32, (side, side), 0)
    lane = lax.broadcasted_iota(jnp.int32, (side, side), 1)
    one = lambda where: jnp.where(where, 1.0, 0.0)
    after, here, before = one(row == lane + 1), one(row == lane), one(row == lane - 1)
    inner_e, inner_w = lane != side - 1, lane != 0
    east = jnp.where(inner_e, after + here, 0.0)
    west = jnp.where(inner_w, here + before, 0.0)
    blocks = (
        after,
        before,
        jnp.where(inner_e, after - here, 0.0),
        jnp.where(inner_w, here - before, 0.0),
        east - west,
        after - before,
    )
    for n, block in enumerate(blocks):
        for half in range(2):
            weights[half * side : (half + 1) * side, n * side : (n + 1) * side] = block.astype(jnp.bfloat16)


def inner_update(loads, store, side, weights):
    line, lane = iota(0, side), iota(1, side)
    first, last = line == 0, line == ROWS - 1
    rim = jnp.where(lane == 0, 2.0, jnp.where(lane == side - 1, -2.0, 0.0))
    steps = side // ROWS
    many = len(loads)

    def cell(h, mx, my, bed):
        root = lax.rsqrt(h)
        celerity = h * root
        inverse = root * root
        u = mx * inverse
        v = my * inverse
        half_sq = 0.5 * h * h
        cross = my * u
        rate_y = jnp.abs(v) + celerity
        rate_x = jnp.abs(u) + celerity
        return (rate_y, h + bed, mx, my, cross, my * v + half_sq, bed), rate_x, mx * u + half_sq, h

    def face_y(low, high):
        top = jnp.maximum(low[0], high[0])
        return [
            (high[3] + low[3]) - top * (high[1] - low[1]),
            (high[4] + low[4]) - top * (high[2] - low[2]),
            (high[5] + low[5]) - top * (high[3] - low[3]),
        ]

    def taken(block):
        return weights[:, block.start * side : block.stop * side]

    cells = [cell(*[load(f, j) for f in range(4)]) for load in loads for j in range(steps)]
    stack = lambda pick: pieces(jnp.concatenate([pick(c) for c in cells], axis=0))
    eta, mx, my, cross, bed = (stack(lambda c, n=n: c[0][n]) for n in (1, 2, 3, 4, 6))
    fx = stack(lambda c: c[2])
    rates = product(stack(lambda c: c[1]), taken(AHEAD))
    jumps = product(jnp.concatenate([eta, mx, my], axis=0), taken(EAST))
    sums = product(jnp.concatenate([fx, cross], axis=0), taken(SUMS))
    slopes = product(bed, taken(SLOPE))
    for n in range(many):
        mine = cells[n * steps : (n + 1) * steps]
        low = [pltpu.roll(each, 1, 0) for each in mine[steps - 1][0]]
        faces = []
        for j in range(steps):
            faces.append(face_y(low, mine[j][0]))
            low = mine[j][0]
        faces[0] = [jnp.where(first, 0.0, each) for each in faces[0]]
        beds = [c[0][6] for c in mine]
        under = jnp.where(first, 0.0, pltpu.roll(beds[-1], 1, 0))
        over = jnp.where(last, 0.0, pltpu.roll(beds[0], ROWS - 1, 0))
        faces.append([jnp.where(last, 0.0, pltpu.roll(each, ROWS - 1, 0)) for each in faces[0]])
        for j in range(steps):
            (_, _, mx, my, _, _, _), rate, _, h = mine[j]
            at = [(q * many + n) * side + ROWS * j for q in range(3)]
            rows = [slice(r, r + ROWS) for r in at]
            top_e = jnp.maximum(rate, rates[rows[0], :side])
            top_w = jnp.maximum(rate, rates[rows[0], side:])
            total = [jumps[rows[1], :side] + jumps[rows[1], side:] + rim * mx, sums[rows[0]], sums[rows[1]]]
            x = [t - (top_e * jumps[r, :side] - top_w * jumps[r, side:]) for t, r in zip(total, rows)]
            south, north = faces[j], faces[j + 1]
            slope_y = (beds[j + 1] if j + 1 < steps else over) - (beds[j - 1] if j else under)
            store(n, 0, j, h - HALF * (x[0] + (north[0] - south[0])))
            store(n, 1, j, mx - HALF * (x[1] + h * slopes[rows[0]] + (north[1] - south[1])))
            store(n, 2, j, my - HALF * (x[2] + h * slope_y + (north[2] - south[2])))


def gather_columns(loads, columns, first_at, side):
    pair = iota(1, side) // 2
    for j in range(side // ROWS):
        held = columns[spread(j, side), :]
        for n, load in enumerate(loads):
            at = first_at + 8 * n
            for f in range(4):
                held = jnp.where(pair == at // 2 + f, pltpu.roll(load(f, j), at + 2 * f + 1, 1), held)
        columns[spread(j, side), :] = held


def take_edges(count, cells, slot_of, columns, edges, base):
    side = columns.shape[0]
    turned = jnp.transpose(columns[...])
    for p in range(count):
        edges[base + 16 * p : base + 16 * p + 8, :] = turned[8 * p : 8 * p + 8, :]
        for f in range(4):
            row = base + 16 * p + 8 + 2 * f
            edges[row : row + 1, :] = cells[slot_of(p), f, side - 1 : side, :]
            edges[row + 1 : row + 2, :] = cells[slot_of(p), f, 0:1, :]


def loader(cells, i):
    side = cells.shape[3]
    return lambda f, j: cells[i, f, spread(j, side), :]


def update(cells, first, many, weights, put):
    loads = [loader(cells, first + n) for n in range(many)]
    inner_update(loads, lambda n, f, j, value: put(n, f, ROWS * j, value), cells.shape[3], weights)


def fetch(cells_hbm, first, cells, sems, parts):
    def copy(i):
        return pltpu.make_async_copy(cells_hbm.at[first + i], cells.at[i], sems.at[i])

    for start, count in parts:
        for i in range(count):
            copy(start + i).start()
    return copy


def outer_slot(cells_hbm, margin):
    _, odd = position()
    return odd * (cells_hbm.shape[0] - margin)


def bundle_layout(margin):
    tables = 16 * margin
    return tables, tables + 16


def outer_kernel(margin, cells_hbm, rest, bundle, cells, columns, weights, sems):
    side = columns.shape[0]
    copy = fetch(cells_hbm, outer_slot(cells_hbm, margin), cells, sems, [(0, margin)])
    fill_weights(weights)
    results = bundle_layout(margin)[1]
    for i in range(0, margin, margin):
        for n in range(margin):
            copy(i + n).wait()

        def put(n, f, row, value, i=i):
            if i + n < FIRST:
                at = results + (3 * (i + n) + f) * side + row
                bundle[at : at + ROWS, :] = value
            else:
                rest[i + n - FIRST, f, row : row + ROWS, :] = value

        gather_columns([loader(cells, i + n) for n in range(margin)], columns, 8 * i, side)
        update(cells, i, margin, weights, put)

    take_edges(margin, cells, lambda p: p, columns, bundle, 0)


def cost(patches, side):
    return pl.CostEstimate(
        flops=patches * side * side * 800,
        bytes_accessed=patches * side * side * 28,
        transcendentals=patches * side * side,
    )


def room(mebibytes):
    return pltpu.CompilerParams(vmem_limit_bytes=mebibytes << 20)


def outer_patches(old_cells, margin):
    side = old_cells.shape[3]
    return pl.pallas_call(
        functools.partial(outer_kernel, margin),
        in_specs=[HBM],
        out_specs=[VMEM, VMEM],
        out_shape=[
            jax.ShapeDtypeStruct((margin - FIRST, 3, side, side), jnp.float32),
            jax.ShapeDtypeStruct((bundle_layout(margin)[1] + 3 * FIRST * side, side), jnp.float32),
        ],
        scratch_shapes=[
            pltpu.VMEM((margin, 4, side, side), jnp.float32),
            pltpu.VMEM((side, side), jnp.float32),
            pltpu.VMEM((2 * side, 6 * side), jnp.bfloat16),
            pltpu.SemaphoreType.DMA((margin,)),
        ],
        cost_estimate=cost(margin, side),
        compiler_params=room(48),
        name="outer",
    )(old_cells)


def with_tables(bundle, table, their_table, margin):
    any_place = pl.BlockSpec(memory_space=pl.ANY)
    start, end = bundle_layout(margin)
    sides, count = table.shape

    def kernel(bundle_ref, table_ref, their_ref, out_ref, held, sem):
        _, odd = position()
        held[...] = jnp.zeros_like(held)
        for which, ref in ((odd, table_ref), (1 - odd, their_ref)):
            held[pl.ds(pl.multiple_of(8 * which, 8), sides), 0:count] = ref[...].astype(jnp.float32)
        copy = pltpu.make_async_copy(held, out_ref.at[start:end, :], sem)
        copy.start()
        copy.wait()

    return pl.pallas_call(
        kernel,
        in_specs=[any_place, VMEM, VMEM],
        out_specs=any_place,
        out_shape=jax.ShapeDtypeStruct(bundle.shape, bundle.dtype),
        scratch_shapes=[pltpu.VMEM((end - start, bundle.shape[1]), jnp.float32), pltpu.SemaphoreType.DMA],
        input_output_aliases={0: 0},
        compiler_params=room(4),
        name="tables",
    )(bundle, table, their_table)


def after(value, other):
    any_place = pl.BlockSpec(memory_space=pl.ANY)
    return pl.pallas_call(
        lambda value_ref, other_ref, out_ref: None,
        in_specs=[any_place, any_place],
        out_specs=any_place,
        out_shape=jax.ShapeDtypeStruct(value.shape, value.dtype),
        input_output_aliases={0: 0},
        compiler_params=room(4),
        name="after",
    )(value, other)


def layout(margin, per_device):
    home = 16 * margin
    limit = home + 16 * per_device
    brought = limit + 8
    return home, limit, brought, brought + 16 * margin


def home_kernel(margin, range_ref, cells_hbm, came, shared, inner, own, cells, columns, weights, sems):
    side = columns.shape[0]
    count = own.shape[0]
    home, limit, brought, total = layout(margin, count)
    _, odd = position()
    inner_at = (1 - odd) * count
    home_at = odd * margin
    parts = [(inner_at, margin), (home_at, count)]
    copy = fetch(cells_hbm, (1 - odd) * margin, cells, sems, parts)
    fill_weights(weights)

    for at, many, out, row in ((inner_at, margin, inner, 0), (home_at, count, own, home)):

        @pl.loop(0, many // PAIR)
        def _(step, at=at, out=out):
            i = step * PAIR
            for n in range(PAIR):
                copy(at + i + n).wait()

            def put(n, f, row, value):
                out[i + n, f, row : row + ROWS, :] = value

            gather_columns([loader(cells, at + i + n) for n in range(PAIR)], columns, 8 * i, side)
            update(cells, at + i, PAIR, weights, put)

        take_edges(many, cells, lambda p, at=at: at + p, columns, shared, row)

    outer_limit = jnp.where(odd == 1, range_ref[0, 1], range_ref[0, 0])
    shared[limit : limit + 8, :] = jnp.full((8, side), outer_limit, jnp.int32).astype(jnp.float32)
    shared[brought:total, :] = came[0 : total - brought, :]


def home_patches(old_range, old_cells, came, margin, per_device):
    side = old_cells.shape[3]
    total = layout(margin, per_device)[-1]
    return pl.pallas_call(
        functools.partial(home_kernel, margin),
        in_specs=[SMEM, HBM, VMEM],
        out_specs=[VMEM] * 3,
        out_shape=[
            jax.ShapeDtypeStruct((total, side), jnp.float32),
            jax.ShapeDtypeStruct((margin, 3, side, side), jnp.float32),
            jax.ShapeDtypeStruct((per_device, 3, side, side), jnp.float32),
        ],
        scratch_shapes=[
            pltpu.VMEM((margin + per_device, 4, side, side), jnp.float32),
            pltpu.VMEM((side, side), jnp.float32),
            pltpu.VMEM((2 * side, 6 * side), jnp.bfloat16),
            pltpu.SemaphoreType.DMA((margin + per_device,)),
        ],
        cost_estimate=cost(margin + per_device, side),
        compiler_params=room(48),
        name="home",
    )(old_range, old_cells, came)


def entries_of(table, sides, lanes):
    count = table.shape[0]
    return jnp.concatenate([jnp.broadcast_to(table[:, s : s + 1], (count, lanes)) for s in range(sides)], axis=0)


def grid_iota(rows, lanes, axis):
    return lax.broadcasted_iota(jnp.int32, (rows, lanes), axis)


def flag(where):
    return jnp.where(where, 1.0, 0.0)


def ranks(masks):
    rows, lanes = masks[0].shape
    earlier = flag(grid_iota(rows, lanes, 1) < grid_iota(rows, lanes, 0)).astype(jnp.bfloat16)
    stacked = jnp.concatenate(masks, axis=1).astype(jnp.bfloat16)
    if rows < lanes:
        stacked = jnp.concatenate([stacked, jnp.zeros((lanes - rows, stacked.shape[1]), jnp.bfloat16)], axis=0)
    counted = product(earlier, stacked)
    return [counted[:, n * lanes : (n + 1) * lanes] for n in range(len(masks))]


def edge_places(row, count, patch):
    s = row // count
    return 4 * count * (s % 2) + s // 2, 2.0 * patch


def edges_of_field(edges, f):
    tiles = edges.shape[0] // 8
    return [edges[pl.ds(2 * f + parity, tiles, stride=8), :] for parity in range(2)]


def answer_kernel(margin, count, range_ref, mine, theirs, came, edges, message):
    side = edges.shape[1]
    home, limit, brought, _ = layout(margin, count)
    inner = 0
    me, odd = position()
    start, stop = range_ref[0, 0], range_ref[0, 1]
    even = odd == 0
    at_me = pl.multiple_of(16 * count * odd, 16)
    at_them = pl.multiple_of(16 * count * (1 - odd), 16)
    edges[pl.ds(at_me, 16 * count), :] = mine[home : home + 16 * count, :]
    edges[pl.ds(at_them, 16 * count), :] = theirs[home : home + 16 * count, :]
    their_limit = theirs[limit : limit + 8, :]
    low, high = 0, count - margin
    for m in range(margin):
        l = jnp.where(even, high, low) + m
        g = me * count + l
        taken = jnp.where(even, g >= stop, g < start)
        to = pl.multiple_of(at_me + 16 * l, 16)
        from_pair = theirs[inner + 16 * m : inner + 16 * (m + 1), :]
        edges[pl.ds(to, 16), :] = jnp.where(taken, from_pair, edges[pl.ds(to, 16), :])
        l = jnp.where(even, low, high) + m
        g = (me + 1 - 2 * odd) * count + l
        taken = jnp.where(even, g < stop, g >= start)
        to = pl.multiple_of(at_them + 16 * l, 16)
        from_pair = mine[inner + 16 * m : inner + 16 * (m + 1), :]
        edges[pl.ds(to, 16), :] = jnp.where(taken, from_pair, edges[pl.ds(to, 16), :])
        l = jnp.where(even, low, high) + m
        g = me * count + l
        taken = jnp.where(even, g < start, g >= stop)
        to = pl.multiple_of(at_me + 16 * l, 16)
        crossed = mine[brought + 16 * m : brought + 16 * (m + 1), :]
        edges[pl.ds(to, 16), :] = jnp.where(taken, crossed, edges[pl.ds(to, 16), :])
        l = jnp.where(even, high, low) + m
        g = ((me + 1 - 2 * odd) * count + l).astype(jnp.float32)
        to = pl.multiple_of(at_them + 16 * l, 16)
        taken = jnp.where(even, g - their_limit, their_limit - g - 1.0) >= 0.0
        for half in range(2):
            crossed = theirs[brought + 16 * m + 8 * half : brought + 16 * m + 8 * half + 8, :]
            at = pl.multiple_of(to + 8 * half, 8)
            edges[pl.ds(at, 8), :] = jnp.where(taken, crossed, edges[pl.ds(at, 8), :])
    sides, total = 4, 8 * count
    row = grid_iota(total, side, 0)
    lane = grid_iota(total, side, 1)
    which, within = row // (sides * count), row % (sides * count)
    at = 16 * margin
    turned = jnp.transpose(jnp.concatenate([came[at : at + 16, :], jnp.zeros((side - 16, side), jnp.float32)], axis=0))
    tables = [turned[0:count, 8 * n : 8 * n + sides] for n in range(2)]
    listed = jnp.concatenate([entries_of(table, sides, side) for table in tables], axis=0)
    patch = listed - (2 * count * (me // 2)).astype(jnp.float32)
    held = [(patch >= n * count) & (patch < (n + 1) * count) for n in range(2)]
    masks = [
        flag((which == 0) & held[0]),
        jnp.where(even, flag((which == 1) & held[0]), flag((which == 0) & held[1])),
        flag((which == 1) & held[1]),
    ]
    chosen = jnp.zeros((total, side), jnp.float32)
    for k, (mask, rank) in enumerate(zip(masks, ranks(masks))):
        slot = (lane - k * CAP).astype(jnp.float32)
        chosen = chosen + jnp.where((lane // CAP == k) & (rank == slot), mask, 0.0)
    place, twice = edge_places(within, count, patch)
    hot = flag(lane.astype(jnp.float32) == place.astype(jnp.float32) + twice).astype(jnp.bfloat16)
    slots = jnp.transpose(chosen)[0:32, :].astype(jnp.bfloat16)
    picked = product(slots, hot).astype(jnp.bfloat16)
    picked = jnp.concatenate([picked] * 3, axis=1)
    for f in range(4):
        values = jnp.concatenate(edges_of_field(edges, f), axis=0)
        high = values.astype(jnp.bfloat16)
        left = values - high.astype(jnp.float32)
        mid = left.astype(jnp.bfloat16)
        low = (left - mid.astype(jnp.float32)).astype(jnp.bfloat16)
        taken = product(picked, jnp.concatenate([high, mid, low], axis=0))
        message[3 * CAP * f : 3 * CAP * (f + 1), :] = taken[0 : 3 * CAP, :]


def answers(old_range, mine, theirs, came, margin, per_device):
    side = mine.shape[1]
    return pl.pallas_call(
        functools.partial(answer_kernel, margin, per_device),
        in_specs=[SMEM, VMEM, VMEM, VMEM],
        out_specs=[VMEM, VMEM],
        out_shape=[
            jax.ShapeDtypeStruct((32 * per_device, side), jnp.float32),
            jax.ShapeDtypeStruct((12 * CAP, side), jnp.float32),
        ],
        compiler_params=room(4),
        name="answers",
    )(old_range, mine, theirs, came)


def prepare_kernel(table, edges, places, hot, near, walls, turn):
    me, odd = position()
    fill_places(places)
    sides, count = table.shape
    side = edges.shape[1]
    total = sides * count
    even = odd == 0
    row, lane = grid_iota(total, side, 0), grid_iota(total, side, 1)
    s, p = row // count, row % count
    turn[...] = jnp.zeros_like(turn)
    turn[0:sides, 0:count] = table[...].astype(jnp.float32)
    listed = entries_of(jnp.transpose(turn[...])[0:count, :], sides, side)
    wall = listed < 0.0
    patch = listed - (2 * count * (me // 2)).astype(jnp.float32)
    distance = listed - (count * me).astype(jnp.float32)
    first = 4 * count * 2
    step = 3 * CAP
    lists = (
        (-2, -2, first, first + step + 2 * CAP),
        (-1, 1, first + CAP, first + CAP),
        (2, 2, first + step, first + 2 * CAP),
    )
    masks, starts = [], []
    for far_even, far_odd, at_even, at_odd in lists:
        low = (count * jnp.where(even, far_even, far_odd)).astype(jnp.float32)
        masks.append(flag(~wall & (distance >= low) & (distance < low + count)))
        starts.append(jnp.where(even, at_even, at_odd).astype(jnp.float32))
    across = jnp.zeros((total, side), jnp.float32)
    for mask, rank, start in zip(masks, ranks(masks), starts):
        across = across + mask * (rank + start)
    place, twice = edge_places(row, count, patch)
    own = 4 * count * (1 - s % 2) + 2 * (count * odd + p) + s // 2
    inside = (patch >= 0.0) & (patch < 2.0 * count)
    index = jnp.where(inside, place.astype(jnp.float32) + twice, across)
    index = jnp.where(wall, own.astype(jnp.float32), index)
    lane = lane.astype(jnp.float32)
    walls[...] = flag(wall)
    far = flag(lane + first == index)
    hot[...] = jnp.concatenate([far, far], axis=1).astype(jnp.bfloat16)
    at_home = flag(lane == index)
    at_home = jnp.concatenate([at_home, at_home], axis=1).astype(jnp.bfloat16)
    for f in range(4):
        near[total * f : total * (f + 1), :] = product(at_home, halves(jnp.concatenate(edges_of_field(edges, f), axis=0)))


def halves(values):
    high = values.astype(jnp.bfloat16)
    low = (values - high.astype(jnp.float32)).astype(jnp.bfloat16)
    return jnp.concatenate([high, low], axis=0)


def prepared(table, edges):
    side = edges.shape[1]
    total = table.shape[0] * table.shape[1]
    return pl.pallas_call(
        prepare_kernel,
        in_specs=[VMEM] * 2,
        out_specs=[VMEM] * 4,
        out_shape=[
            jax.ShapeDtypeStruct((2 * side, 6 * side), jnp.bfloat16),
            jax.ShapeDtypeStruct((total, 2 * side), jnp.bfloat16),
            jax.ShapeDtypeStruct((4 * total, side), jnp.float32),
            jax.ShapeDtypeStruct((total, side), jnp.float32),
        ],
        scratch_shapes=[pltpu.VMEM((side, side), jnp.float32)],
        compiler_params=room(4),
        name="prepare",
    )(table, edges)


def rim_terms(hot, near, walls, edges, crossed, passed, columns, lines, turn, count, odd):
    side = edges.shape[1]
    total, step = walls.shape[0], 3 * CAP
    outside = []
    for f in range(4):
        parts = [ref[step * f : step * (f + 1), :] for ref in (crossed, passed)]
        parts.append(jnp.zeros((side - 2 * step, side), jnp.float32))
        far = product(hot[...], halves(jnp.concatenate(parts, axis=0)))
        outside.append(near[total * f : total * (f + 1), :] + far)
    wall = walls[...] > 0.0
    turn[...] = jnp.zeros_like(turn)
    lines[...] = jnp.zeros_like(lines)
    for s in range(4):
        parity = 1 - s % 2
        sign = 1.0 - 2.0 * parity
        axis = s // 2
        normal, across = (1, 2) if axis == 0 else (2, 1)

        at = slice(count * s, count * (s + 1))

        def both(f):
            row = 8 * axis + 2 * f + parity
            return edges[pl.ds(16 * count * odd + row, count, stride=16), :], outside[f][at]

        hc, hg = both(0)
        nc, ng = both(normal)
        ng = jnp.where(wall[at], -ng, ng)
        ac, ag = both(across)
        bc, bg = both(3)
        rc, rg = lax.rsqrt(hc), lax.rsqrt(hg)
        uc, ug = nc * rc * rc, ng * rg * rg
        top = jnp.maximum(jnp.abs(uc) + hc * rc, jnp.abs(ug) + hg * rg)
        fc, fg = nc * uc + 0.5 * hc * hc, ng * ug + 0.5 * hg * hg
        c_h = -HALF * (sign * (nc + ng) - top * ((hg + bg) - (hc + bc)))
        c_n = -HALF * (sign * (fc + fg + hc * bg) - top * (ng - nc))
        c_t = -HALF * (sign * (ac * uc + ag * ug) - top * (ag - ac))
        for f, value in ((0, c_h), (normal, c_n), (across, c_t)):
            target = turn if axis == 0 else lines
            target[pl.ds(2 * f + parity, count, stride=8), :] = value
    turn[...] = jnp.transpose(turn[...])
    side = turn.shape[0]
    columns[...] = pieces(jnp.concatenate([turn[spread(j, side), :] for j in range(side // ROWS)], axis=0))


def fill_places(places):
    side = places.shape[0] // 2
    row = lax.broadcasted_iota(jnp.int32, (side, side), 0) % 16
    lane = lax.broadcasted_iota(jnp.int32, (side, side), 1)
    source = row - jnp.where(lane == 0, 1, jnp.where(lane == side - 1, 0, 1024))
    for u in range(2):
        for f in range(3):
            block = jnp.where(source == 8 * u + 2 * f, 1.0, 0.0).astype(jnp.bfloat16)
            for half in range(2):
                at = (3 * u + f) * side
                places[half * side : (half + 1) * side, at : at + side] = block


def final_kernel(
    margin, range_ref, places, hot, near, walls, edges, crossed, passed, own, theirs, came, arrived, out,
    result, turn, columns, lines, sems,
):
    count, side = own.shape[0], lines.shape[1]
    me, odd = position()
    even = odd == 0
    rim_terms(hot, near, walls, edges, crossed, passed, columns, lines, turn, count, odd)
    start, stop = range_ref[0, 0], range_ref[0, 1]
    line = iota(0, side)
    lane = lax.broadcasted_iota(jnp.int32, (side, 2 * side), 1) % side
    steps = side // ROWS
    results = bundle_layout(margin)[1]

    def copy(p):
        return pltpu.make_async_copy(result.at[p], out.at[p], sems.at[p])

    for group in range(0, count, margin):
        patches = range(group, group + margin)
        held = columns[...]
        masked = [held * jnp.where(lane // 16 == p // 2, 1.0, 0.0).astype(jnp.bfloat16) for p in patches[::2]]
        terms = product(jnp.concatenate(masked, axis=0), places[...])
        for m, p in enumerate(patches):
            if group == 0:
                taken = me * count + p < start
            elif group == count - margin:
                taken = me * count + p >= stop
            else:
                taken = None
            beside = even if group else odd == 1
            for f in range(3):
                for j in range(steps):
                    rows = slice(ROWS * j, ROWS * (j + 1))
                    value = own[p, f, rows, :]
                    if taken is not None:
                        if m < FIRST:
                            at = results + (3 * m + f) * side + ROWS * j
                            crossing = came[at : at + ROWS, :]
                        else:
                            crossing = arrived[m - FIRST, f, rows, :]
                        moved = jnp.where(beside, theirs[m, f, rows, :], crossing)
                        value = jnp.where(taken, moved, value)
                    at = side * (m // 2) + ROWS * j
                    block = 3 * (m % 2) + f
                    value = value + terms[at : at + ROWS, block * side : (block + 1) * side]
                    if j == 0:
                        south = lines[8 * p + 2 * f + 1 : 8 * p + 2 * f + 2, :]
                        value = value + jnp.where(line == 0, south, 0.0)
                    if j == steps - 1:
                        north = lines[8 * p + 2 * f : 8 * p + 2 * f + 1, :]
                        value = value + jnp.where(line == ROWS - 1, north, 0.0)
                    result[p, f, spread(j, side), :] = value
            copy(p).start()
    for p in range(count):
        copy(p).wait()


def finished(old_range, ready, edges, crossed, passed, own, theirs, came, arrived, margin):
    count, _, side, _ = own.shape
    return pl.pallas_call(
        functools.partial(final_kernel, margin),
        in_specs=[SMEM] + [VMEM] * 11,
        out_specs=HBM,
        out_shape=jax.ShapeDtypeStruct(own.shape, jnp.float32),
        scratch_shapes=[
            pltpu.VMEM(own.shape, jnp.float32),
            pltpu.VMEM((side, side), jnp.float32),
            pltpu.VMEM((side, 2 * side), jnp.bfloat16),
            pltpu.VMEM((side, side), jnp.float32),
            pltpu.SemaphoreType.DMA((count,)),
        ],
        compiler_params=room(12),
        name="final",
    )(old_range, *ready, edges, crossed, passed, own, theirs, came, arrived)


def swapped(value, first):
    pairs = [(i, i + 1) for i in range(first, lax.axis_size(AXES) - 1, 2)]
    return lax.ppermute(value, AXES, pairs + [(j, i) for i, j in pairs])


def local(old_cells, old_range, neighbours):
    per_device = neighbours.shape[0]
    margin = (old_cells.shape[0] - per_device) // 2
    table = neighbours.T
    their_table = swapped(table, 0)
    rest, bundle = outer_patches(old_cells, margin)
    bundle = with_tables(bundle, table, their_table, margin)
    came = swapped(bundle, 1)
    arrived = swapped(after(rest, bundle), 1)
    shared, inner, own = home_patches(old_range, old_cells, came, margin, per_device)
    their_edges = swapped(shared, 0)
    theirs = swapped(inner, 0)
    edges, message = answers(old_range, shared, their_edges, came, margin, per_device)
    crossed = swapped(message, 1)
    passed = swapped(crossed, 0)
    return finished(old_range, prepared(table, edges), edges, crossed, passed, own, theirs, came, arrived, margin)


def solution(mesh):
    placed = (
        P(("member", "curve", "sub"), None, None, None),
        P(("member", "curve", "sub"), None),
        P(("member", "curve", "sub"), None),
    )
    return jax.shard_map(
        local,
        mesh=mesh,
        in_specs=placed,
        out_specs=P(("member", "curve", "sub"), None, None, None),
        check_vma=False,
    )
```
